32 devices in a mesh: dp: 8 (over y, x, core), seq: 4 (over z).
Axes of the slice: x: 2, y: 2, z: 4, core: 2. Of those that a mesh axis runs over, the one named last changes fastest.
Arguments:
- inputs: bfloat16 [8, 1024, 2048], P('dp', 'seq'), may hold values from -6 to 6
- cotangent: bfloat16 [8, 1024, 2048], P('dp', 'seq'), may hold values from -6 to 6
- attn_params: float32 [2048, 8192], P(('dp', 'seq'))
- attn_first: float32 [2048, 8192], P(('dp', 'seq'))
- attn_second: float32 [2048, 8192], P(('dp', 'seq')), as said below
- mlp_params: float32 [2048, 16384], P(('dp', 'seq'))
- mlp_first: float32 [2048, 16384], P(('dp', 'seq'))
- mlp_second: float32 [2048, 16384], P(('dp', 'seq')), as said below
- small: float32 [2048, 13], P(('dp', 'seq'))
- small_first: float32 [2048, 13], P(('dp', 'seq'))
- small_second: float32 [2048, 13], P(('dp', 'seq')), as said below
Outputs:
- outputs: bfloat16 [8, 1024, 2048], P('dp', 'seq')
- input_grad: float32 [8, 1024, 2048], P('dp', 'seq')
- attn_grad: float32 [2048, 8192], P(('dp', 'seq'))
- attn_new: float32 [2048, 8192], P(('dp', 'seq'))
- attn_first_new: float32 [2048, 8192], P(('dp', 'seq'))
- attn_second_new: float32 [2048, 8192], P(('dp', 'seq'))
- mlp_grad: float32 [2048, 16384], P(('dp', 'seq'))
- mlp_new: float32 [2048, 16384], P(('dp', 'seq'))
- mlp_first_new: float32 [2048, 16384], P(('dp', 'seq'))
- mlp_second_new: float32 [2048, 16384], P(('dp', 'seq'))
- small_grad: float32 [2048, 13], P(('dp', 'seq'))
- small_new: float32 [2048, 13], P(('dp', 'seq'))
- small_first_new: float32 [2048, 13], P(('dp', 'seq'))
- small_second_new: float32 [2048, 13], P(('dp', 'seq'))
The draws below stay inside these ranges and needn't reach their ends.
Inputs may be any that keep to these rules, and one draw needn't show every extreme that they name: `attn_second`: positive. `mlp_second`: positive. `small_second`: positive.
All inputs are finite; a program needn't handle non-finite values.
Results may differ from the reference program's by a relative error of at most 0.012.
Values may be sent and summed in bfloat16 or wider, within the bound.
No kernel may reach another device: no remote copies, remote signals or barrier semaphores. Data moves between devices by JAX's collectives and lax.ppermute only.
A program may use at most 896 MiB of HBM per device.

```python
import math
import jax
import jax.numpy as jnp
from jax import lax

D = 2048
FF = 8192
HEADS = 8
HD = 256
ROT = 64
LENGTH = 1024
STEP = 10
NSEQ = 8
TOKENS = 8192


def block_scale(count, split, lower_value, upper_value):
    column = jnp.arange(count)
    return jnp.where(column < split, lower_value, upper_value)


def first_draw(key, shape, scales):
    return 0.11 * scales * jax.random.normal(key, shape, jnp.float32)


def second_draw(key, shape, scales):
    factor = jnp.exp(jax.random.uniform(key, shape, jnp.float32, 0.0, math.log(4.0)))
    return 0.05 / 0.95 * scales * scales * factor


def attn_grad_scale():
    return block_scale(4 * D, 3 * D, TOKENS ** 0.5, (8.0 * TOKENS / LENGTH) ** 0.5)


def draw_attn_params(key, part):
    key = jax.random.fold_in(key, 1)
    scales = block_scale(4 * D, 3 * D, D ** (-0.5), (8.0 * D / LENGTH) ** (-0.5))
    return jax.random.normal(key, (D, 4 * D), jnp.float32) * scales


def draw_attn_first(key, part):
    key = jax.random.fold_in(key, 2)
    return first_draw(key, (D, 4 * D), attn_grad_scale())


def draw_attn_second(key, part):
    key = jax.random.fold_in(key, 3)
    return second_draw(key, (D, 4 * D), attn_grad_scale())


def draw_mlp_params(key, part):
    key = jax.random.fold_in(key, 4)
    scales = block_scale(2 * FF, FF, D ** (-0.5), FF ** (-0.5))
    return jax.random.normal(key, (D, 2 * FF), jnp.float32) * scales


def draw_mlp_first(key, part):
    key = jax.random.fold_in(key, 5)
    return first_draw(key, (D, 2 * FF), 0.6 * TOKENS ** 0.5)


def draw_mlp_second(key, part):
    key = jax.random.fold_in(key, 6)
    return second_draw(key, (D, 2 * FF), 0.6 * TOKENS ** 0.5)


def draw_small(key, part):
    key = jax.random.fold_in(key, 7)
    gain_key, bias_key = jax.random.split(key)
    gains = jax.random.uniform(gain_key, (D, 13), jnp.float32, 0.5, 1.5)
    biases = jax.random.normal(bias_key, (D, 13), jnp.float32)
    column = jnp.arange(13)
    bias_scale = jnp.where(column == 8, 0.02, 0.1)
    is_gain = (column == 0) | (column == 2)
    return jnp.where(is_gain, gains, biases * bias_scale)


def draw_small_first(key, part):
    key = jax.random.fold_in(key, 8)
    return first_draw(key, (D, 13), 1.5 * TOKENS ** 0.5)


def draw_small_second(key, part):
    key = jax.random.fold_in(key, 9)
    return second_draw(key, (D, 13), 1.5 * TOKENS ** 0.5)


def steps_of(key, extent, cuts, smallest, largest):
    level = 1.0
    for dim, shards_of in cuts:
        draws = jax.random.uniform(jax.random.fold_in(jax.random.fold_in(key, 6), dim), (shards_of,), jnp.float32, smallest / len(cuts), largest / len(cuts))
        level = level * jnp.repeat(jnp.exp(draws), extent[dim] // shards_of).reshape((-1,) + (1,) * (len(extent) - 1 - dim))
    return level


def gaussian(key, shape, deviation, limit, cuts=(), kind=jnp.bfloat16):
    values = deviation * jax.random.normal(key, shape, jnp.float32)
    if cuts:
        values = values * steps_of(key, shape, cuts, -0.22, 0.18)
    return jnp.clip(values, -limit, limit).astype(kind)


def setup_inputs(seed: int = 0) -> dict:
    streams_of = jax.random.split(jax.random.key(seed), 12)
    return {
        "inputs": gaussian(streams_of[0], (NSEQ, LENGTH, D), 1.0, 6.0, ((0, 8), (1, 4))),
        "cotangent": gaussian(streams_of[1], (NSEQ, LENGTH, D), 1.0, 6.0, ((0, 8), (1, 4))),
        "attn_params": draw_attn_params(jax.random.fold_in(streams_of[11], 71), 0),
        "attn_first": draw_attn_first(jax.random.fold_in(streams_of[11], 71), 0),
        "attn_second": draw_attn_second(jax.random.fold_in(streams_of[11], 71), 0),
        "mlp_params": draw_mlp_params(jax.random.fold_in(streams_of[11], 71), 0),
        "mlp_first": draw_mlp_first(jax.random.fold_in(streams_of[11], 71), 0),
        "mlp_second": draw_mlp_second(jax.random.fold_in(streams_of[11], 71), 0),
        "small": draw_small(jax.random.fold_in(streams_of[11], 71), 0),
        "small_first": draw_small_first(jax.random.fold_in(streams_of[11], 71), 0),
        "small_second": draw_small_second(jax.random.fold_in(streams_of[11], 71), 0),
    }


@jax.custom_vjp
def low(v):
    return lax.optimization_barrier(v.astype(jnp.bfloat16)).astype(jnp.float32)

@jax.custom_vjp
def low_back(v):
    return v

def low_keep(v):
    return (low(v), None)

def low_pass(kept, grad):
    return (grad,)

def back_keep(v):
    return (v, None)

def back_low(kept, grad):
    return (low(grad),)
low.defvjp(low_keep, low_pass)
low_back.defvjp(back_keep, back_low)
norm_eps = 1e-05
masked_value = -1e+30
beta_first = 0.9
beta_second = 0.95
adam_eps = 1e-08
decay_rate = 0.01
rate_attention = 0.06
rate_mlp = 0.02
rate_vector = 0.2
highest = lax.Precision.HIGHEST

def layer_norm(values, gain, shift):
    row_mean = lax.optimization_barrier(jnp.mean(values, axis=-1, keepdims=True))
    centred = values - row_mean
    spread = lax.optimization_barrier(jnp.mean(centred * centred, axis=-1, keepdims=True))
    return centred * lax.rsqrt(spread + norm_eps) * gain + shift

def rotary_tables(positions, rot_dims):
    frequency = 10000.0 ** (-(jnp.arange(rot_dims // 2, dtype=jnp.float32) * 2.0) / rot_dims)
    angles = positions.astype(jnp.float32)[:, None] * frequency[None, :]
    angles = jnp.concatenate([angles, angles], axis=-1)
    return (jnp.cos(angles)[:, None, :], jnp.sin(angles)[:, None, :])

def rotate(values, cosine, sine, rot_dims):
    rotated_part = values[..., :rot_dims]
    first_half = rotated_part[..., :rot_dims // 2]
    second_half = rotated_part[..., rot_dims // 2:]
    turned = jnp.concatenate([-second_half, first_half], axis=-1)
    return jnp.concatenate([rotated_part * cosine + turned * sine, values[..., rot_dims:]], axis=-1)

def forward(tokens, attn_w, mlp_w, vectors):
    attn_in = low(layer_norm(tokens, vectors[:, 0], vectors[:, 1]))
    mlp_in = low(layer_norm(tokens, vectors[:, 2], vectors[:, 3]))
    qkv_bias = vectors[:, 6:9].T.reshape(-1)
    up_bias = vectors[:, 9:13].T.reshape(-1)
    projected = low_back(jnp.dot(attn_in, attn_w[:, :3 * D], precision=highest) + qkv_bias)
    shaped = projected.reshape(LENGTH, 3, HEADS, HD)
    positions = jnp.arange(LENGTH, dtype=jnp.int32)
    cosine, sine = rotary_tables(positions, ROT)
    queries = low(rotate(shaped[:, 0], cosine, sine, ROT))
    keys = low(rotate(shaped[:, 1], cosine, sine, ROT))
    values = low(shaped[:, 2])
    raw = low_back(jnp.einsum('qhd,khd->hqk', queries, keys, precision=highest) * HD ** (-0.5))
    causal = positions[None, :] <= positions[:, None]
    scores = jnp.where(causal[None], raw, masked_value)
    row_max = lax.optimization_barrier(jnp.max(scores, axis=-1, keepdims=True))
    exp_terms = jnp.exp(scores - row_max)
    weights = low(exp_terms / lax.optimization_barrier(jnp.sum(exp_terms, axis=-1, keepdims=True)))
    mixed = jnp.einsum('hqk,khd->qhd', weights, values, precision=highest).reshape(LENGTH, D)
    mixed = low(low_back(mixed))
    attn_out = jnp.dot(mixed, attn_w[:, 3 * D:], precision=highest) + vectors[:, 4]
    gate_pre = low_back(jnp.dot(mlp_in, mlp_w[:, :FF], precision=highest) + up_bias)
    activated = low(jax.nn.gelu(gate_pre, approximate=False))
    mlp_out = jnp.dot(activated, mlp_w[:, FF:].T, precision=highest) + vectors[:, 5]
    return tokens + attn_out + mlp_out

def adamw(master, gradient, first_old, second_old, step_rate):
    first_new = beta_first * first_old + (1.0 - beta_first) * gradient
    second_new = beta_second * second_old + (1.0 - beta_second) * gradient * gradient
    first_hat = first_new / (1.0 - beta_first ** STEP)
    second_hat = second_new / (1.0 - beta_second ** STEP)
    updated = master - step_rate * (first_hat / (jnp.sqrt(second_hat) + adam_eps) + decay_rate * master)
    return (gradient, updated, first_new, second_new)

def reference(inputs, cotangent, attn_params, attn_first, attn_second, mlp_params, mlp_first, mlp_second, small, small_first, small_second):
    attn_w = low(attn_params)
    mlp_w = low(mlp_params)
    vectors = low(small)

    def one_sequence(carry, pair):
        tokens, upstream = pair
        result, pull = jax.vjp(forward, tokens, attn_w, mlp_w, vectors)
        token_grad, attn_g, mlp_g, small_g = pull(upstream)
        return ((carry[0] + attn_g, carry[1] + mlp_g, carry[2] + small_g), (result.astype(jnp.bfloat16), token_grad))
    start = (jnp.zeros_like(attn_params), jnp.zeros_like(mlp_params), jnp.zeros_like(small))
    sums, results = lax.scan(one_sequence, start, (inputs.astype(jnp.float32), cotangent.astype(jnp.float32)))
    outputs, input_grad = results
    attn_out = adamw(attn_params, sums[0], attn_first, attn_second, rate_attention)
    mlp_out = adamw(mlp_params, sums[1], mlp_first, mlp_second, rate_mlp)
    small_out = adamw(small, sums[2], small_first, small_second, rate_vector)
    return (outputs, input_grad, attn_out[0], attn_out[1], attn_out[2], attn_out[3], mlp_out[0], mlp_out[1], mlp_out[2], mlp_out[3], small_out[0], small_out[1], small_out[2], small_out[3])
```

```python
from functools import partial

import jax
import jax.numpy as jnp
from jax import lax
from jax.experimental import pallas as pl
from jax.experimental.pallas import tpu as pltpu
from jax.sharding import PartitionSpec as P

HEADS = 8
STEP = 10
AXES = ("dp", "seq")
LANES = 128
VMEM_LIMIT = 56 * 2**20

norm_eps = 1e-05
masked_value = -1e30
beta_first = 0.9
beta_second = 0.95
adam_eps = 1e-08
decay_rate = 0.01
rate_attention = 0.06
rate_mlp = 0.02
rate_vector = 0.2

f32 = jnp.float32
bf16 = jnp.bfloat16


def normalize(values):
    row_mean = jnp.mean(values, axis=-1, keepdims=True)
    centred = values - row_mean
    spread = jnp.mean(centred * centred, axis=-1, keepdims=True)
    scaling = lax.rsqrt(spread + norm_eps)
    return (centred * scaling, scaling)


def dot(left_op, right_op, left_dim=1, right_dim=0):
    return lax.dot_general(
        left_op,
        right_op,
        (((left_dim,), (right_dim,)), ((), ())),
        preferred_element_type=f32,
    )


def adamw(master, gradient, first_old, second_old, step_rate):
    first_new = beta_first * first_old + (1.0 - beta_first) * gradient
    second_new = beta_second * second_old + (1.0 - beta_second) * gradient * gradient
    first_hat = first_new / (1.0 - beta_first**STEP)
    second_hat = second_new / (1.0 - beta_second**STEP)
    updated = master - step_rate * (
        first_hat / (jnp.sqrt(second_hat) + adam_eps) + decay_rate * master
    )
    return (gradient, updated, first_new, second_new)


def params(cost=None, **kw):
    return dict(
        compiler_params=pltpu.CompilerParams(vmem_limit_bytes=VMEM_LIMIT, **kw),
        cost_estimate=cost and pl.CostEstimate(flops=cost[0], bytes_accessed=cost[1], transcendentals=0),
    )


class Layout:
    def __init__(self, nd, nz):
        self.nd, self.nz = nd, nz
        self.pair = HEADS // nz
        self.groups = nd // self.pair
        self.dp = lax.axis_index("dp")
        self.z = lax.axis_index("seq")
        self.g = self.dp // self.pair
        self.c = self.dp % self.pair
        self.t = self.z * self.pair + self.c

    def perm(self, target):
        pairs = []
        for dp in range(self.nd):
            for z in range(self.nz):
                goal = target(dp // self.pair, dp % self.pair, z)
                if goal is not None:
                    g, c, s = goal
                    pairs.append((dp * self.nz + z, (g * self.pair + c) * self.nz + s))
        return pairs

    def hop(self, value, target):
        return lax.ppermute(value, AXES, self.perm(target))

    def group_hop(self, value, bit):
        return self.hop(value, lambda g, c, z: (g ^ bit, c, z))

    def core_hop(self, value, r):
        return self.hop(value, lambda g, c, z: (g, c ^ r, z))

    def ring(self, value):
        return self.hop(value, lambda g, c, z: (g, c, (z + 1) % self.nz))

    def flat_hop(self, value, bit):
        return lax.ppermute(value, AXES, [(i, i ^ bit) for i in range(self.nd * self.nz)])

    def head_owner_perm(self):
        pairs = []
        for r in range(self.nd * self.nz):
            head, quarter = r // self.groups, r % self.groups
            s, c = head // self.pair, head % self.pair
            pairs.append((r, (quarter * self.pair + c) * self.nz + s))
        return pairs


def bits_of(count, descending):
    bits = []
    bit = 1
    while bit < count:
        bits.append(bit)
        bit *= 2
    return bits[::-1] if descending else bits


def group_gather(lay, block, descending):
    held = {0: block}
    for bit in bits_of(lay.groups, descending):
        for m in list(held):
            held[m ^ bit] = lay.group_hop(held[m], bit)
    return held


def group_scatter(lay, blocks, descending):
    held = dict(blocks)
    for bit in bits_of(lay.groups, descending):
        kept = {}
        for m in held:
            if not m & bit:
                got = lay.group_hop(held[m ^ bit].astype(bf16), bit)
                kept[m] = held[m].astype(f32) + got.astype(f32)
        held = kept
    return held[0]


def total_sum(lay, vector):
    bit = 1
    while bit < lay.nd * lay.nz:
        vector = vector + lay.flat_hop(vector, bit)
        bit *= 2
    return vector


def norm_kernel(pair, first, pos_ref, *refs):
    x_refs = refs[:pair]
    vec_ref = refs[pair]
    out_refs = refs[-3:]
    for r in range(pair):
        normed, _ = normalize(x_refs[r][0].astype(f32))
        out_refs[0][r, 0, 0] = (normed * vec_ref[0:1] + vec_ref[1:2]).astype(bf16)
        out_refs[1][r, 0, 0] = (normed * vec_ref[2:3] + vec_ref[3:4]).astype(bf16)
        out_refs[2][r, 0, 0] = normed.astype(bf16)


def norm_place(lay, pieces, vec, where, held):
    count, span, width = pieces[0].shape
    pair = lay.pair
    tile = min(span, 128)
    out = jax.ShapeDtypeStruct((pair, count, lay.nz, span, width), bf16)
    x_spec = pl.BlockSpec((1, tile, width), lambda i, j, pos: (i, j, 0))
    v_spec = pl.BlockSpec(vec.shape, lambda i, j, pos: (0, 0))
    o_spec = pl.BlockSpec((pair, 1, 1, tile, width), lambda i, j, pos: (0, i, pos[0], j, 0))
    in_specs = [x_spec] * pair + [v_spec]
    aliases = {}
    if held:
        in_specs += [pl.BlockSpec(memory_space=pl.ANY)] * 3
        aliases = {pair + 2 + k: k for k in range(3)}
    return pl.pallas_call(
        partial(norm_kernel, pair, not held),
        grid_spec=pltpu.PrefetchScalarGridSpec(
            num_scalar_prefetch=1,
            grid=(count, span // tile),
            in_specs=in_specs,
            out_specs=[o_spec] * 3,
        ),
        out_shape=[out] * 3,
        input_output_aliases=aliases,
        name="norm_place",
        **params((20 * pair * count * span * width, 8 * pair * count * span * width)),
    )(jnp.reshape(where, (1,)).astype(jnp.int32), *pieces, vec, *held)


def turn(values, cosine, low_sine, high_sine, quarter):
    head = values[:, :LANES]
    turned = (
        head * cosine
        + pltpu.roll(head, LANES - quarter, 1) * low_sine
        + pltpu.roll(head, quarter, 1) * high_sine
    )
    return jnp.concatenate([turned, values[:, LANES:]], axis=1)


def attn_fwd_kernel(quarter, scale, tile, a_ref, wq_ref, wk_ref, wv_ref, b_ref, tab_ref, qkv_ref, o_ref, lse_ref):
    length, hd = o_ref.shape[1:]
    cosine, low_sine, high_sine = tab_ref[0], tab_ref[1], tab_ref[2]
    a = a_ref[0]
    q = dot(a, wq_ref[...]) + b_ref[0:1, :hd]
    qkv_ref[0, :, :hd] = turn(q, cosine, low_sine, high_sine, quarter).astype(bf16)
    k = dot(a, wk_ref[...]) + b_ref[0:1, hd : 2 * hd]
    qkv_ref[0, :, hd : 2 * hd] = turn(k, cosine, low_sine, high_sine, quarter).astype(bf16)
    v = dot(a, wv_ref[...]) + b_ref[0:1, 2 * hd :]
    qkv_ref[0, :, 2 * hd :] = v.astype(bf16)
    for i in range(length // tile):
        end = (i + 1) * tile
        q_i = qkv_ref[0, i * tile : end, :hd]
        scores = dot(q_i, qkv_ref[0, :end, hd : 2 * hd], 1, 1) * scale
        row = lax.broadcasted_iota(jnp.int32, scores.shape, 0) + i * tile
        col = lax.broadcasted_iota(jnp.int32, scores.shape, 1)
        scores = jnp.where(col <= row, scores, masked_value)
        row_max = jnp.max(scores, axis=1, keepdims=True)
        terms = jnp.exp(scores - row_max)
        row_sum = jnp.sum(terms, axis=1, keepdims=True)
        probs = (terms / row_sum).astype(bf16)
        o_ref[0, i * tile : end] = dot(probs, qkv_ref[0, :end, 2 * hd :]).astype(bf16)
        lse_ref[0, i * tile : end] = jnp.broadcast_to(row_max + jnp.log(row_sum), (tile, LANES))


def attn_forward(a, w_qu, bias, tables, unit, hd, scale):
    seqs, length, width = a.shape
    first = unit // hd
    w_spec = [pl.BlockSpec((width, hd), lambda s, j=j: (0, first + j)) for j in range(3)]
    flops = 2 * seqs * length * (3 * hd * width + 2 * length * hd)
    return pl.pallas_call(
        partial(attn_fwd_kernel, hd // 8, scale, min(256, length)),
        grid=(seqs,),
        in_specs=[pl.BlockSpec((1, length, width), lambda s: (s, 0, 0))]
        + w_spec
        + [
            pl.BlockSpec(bias.shape, lambda s: (0, 0)),
            pl.BlockSpec(tables.shape, lambda s: (0, 0, 0)),
        ],
        out_specs=[
            pl.BlockSpec((1, length, 3 * hd), lambda s: (s, 0, 0)),
            pl.BlockSpec((1, length, hd), lambda s: (s, 0, 0)),
            pl.BlockSpec((1, length, LANES), lambda s: (s, 0, 0)),
        ],
        out_shape=[
            jax.ShapeDtypeStruct((seqs, length, 3 * hd), bf16),
            jax.ShapeDtypeStruct((seqs, length, hd), bf16),
            jax.ShapeDtypeStruct((seqs, length, LANES), f32),
        ],
        name="attn_forward",
        **params((flops, 12 * seqs * length * width)),
    )(a, w_qu, w_qu, w_qu, bias, tables)


def attn_bwd_kernel(quarter, scale, tile, dy_ref, wo_ref, qkv_ref, lse_ref, tab_ref, dp_ref, sum_ref, do_s, dk_s, dv_s):
    length = dy_ref.shape[1]
    hd = wo_ref.shape[0]
    cosine, low_sine, high_sine = tab_ref[0], -tab_ref[1], -tab_ref[2]
    do_s[...] = dot(dy_ref[0], wo_ref[...], 1, 1).astype(bf16)
    steps = length // tile
    for i in reversed(range(steps)):
        end = (i + 1) * tile
        q_i = qkv_ref[0, i * tile : end, :hd]
        k = qkv_ref[0, :end, hd : 2 * hd]
        do_i = do_s[i * tile : end]
        scores = dot(q_i, k, 1, 1) * scale
        row = lax.broadcasted_iota(jnp.int32, scores.shape, 0) + i * tile
        col = lax.broadcasted_iota(jnp.int32, scores.shape, 1)
        probs = jnp.where(col <= row, jnp.exp(scores - lse_ref[0, i * tile : end, 0:1]), 0.0)
        probs_grad = dot(do_i, qkv_ref[0, :end, 2 * hd :], 1, 1)
        row_dot = jnp.sum(probs * probs_grad, axis=1, keepdims=True)
        score_grad = (probs * (probs_grad - row_dot)).astype(bf16)
        dq = dot(score_grad, k) * scale
        dp_ref[0, i * tile : end, :hd] = turn(
            dq,
            cosine[i * tile : end],
            low_sine[i * tile : end],
            high_sine[i * tile : end],
            quarter,
        ).astype(bf16)
        dk = dot(score_grad, q_i, 0, 0)
        dv = dot(probs.astype(bf16), do_i, 0, 0)
        if i == steps - 1:
            dk_s[...] = dk
            dv_s[...] = dv
        else:
            dk_s[:end] += dk
            dv_s[:end] += dv
    dp_ref[0, :, hd : 2 * hd] = turn(
        dk_s[...] * scale, cosine, low_sine, high_sine, quarter
    ).astype(bf16)
    dp_ref[0, :, 2 * hd :] = dv_s[...].astype(bf16)
    total = jnp.sum(dp_ref[0].astype(f32), axis=0, keepdims=True)
    sum_ref[0] = jnp.broadcast_to(total, sum_ref.shape[1:])


def attn_backward(dy, w_out, qkv, lse, tables, scale):
    seqs, length, width = dy.shape
    hd = w_out.shape[0]
    flops = 2 * seqs * length * (hd * width + 5 * length * hd)
    return pl.pallas_call(
        partial(attn_bwd_kernel, hd // 8, scale, min(256, length)),
        grid=(seqs,),
        in_specs=[
            pl.BlockSpec((1, length, width), lambda s: (s, 0, 0)),
            pl.BlockSpec(w_out.shape, lambda s: (0, 0)),
            pl.BlockSpec((1, length, 3 * hd), lambda s: (s, 0, 0)),
            pl.BlockSpec((1, length, LANES), lambda s: (s, 0, 0)),
            pl.BlockSpec(tables.shape, lambda s: (0, 0, 0)),
        ],
        out_specs=[
            pl.BlockSpec((1, length, 3 * hd), lambda s: (s, 0, 0)),
            pl.BlockSpec((1, 8, 3 * hd), lambda s: (s, 0, 0)),
        ],
        out_shape=[
            jax.ShapeDtypeStruct((seqs, length, 3 * hd), bf16),
            jax.ShapeDtypeStruct((seqs, 8, 3 * hd), f32),
        ],
        scratch_shapes=[
            pltpu.VMEM((length, hd), bf16),
            pltpu.VMEM((length, hd), f32),
            pltpu.VMEM((length, hd), f32),
        ],
        name="attn_backward",
        **params((flops, 8 * seqs * length * width)),
    )(dy, w_out, qkv, lse, tables)


def mlp_fwd_kernel(m_ref, wu_ref, b_ref, wd_ref, o_ref, wo_ref, g_ref, slope_ref, out_ref):
    u = dot(m_ref[...], wu_ref[...]) + b_ref[0:1]
    half = 0.5 * (1.0 + lax.erf(u * (0.5**0.5)))
    g_ref[...] = (u * half).astype(bf16)
    slope = half + u * (jnp.exp(-0.5 * u * u) * 0.3989422804014327)
    slope_ref[...] = slope.astype(bf16)
    total = dot(g_ref[...], wd_ref[...], 1, 1) + dot(o_ref[...], wo_ref[...])
    out_ref[...] = total.astype(bf16)


def mlp_forward(m, w_qu, bias, w_down, o, w_out, tile):
    tokens, width = m.shape
    unit, hd = w_down.shape[1], o.shape[1]
    flops = 2 * tokens * width * (2 * unit + hd)
    return pl.pallas_call(
        mlp_fwd_kernel,
        grid=(tokens // tile,),
        in_specs=[
            pl.BlockSpec((tile, width), lambda i: (i, 0)),
            pl.BlockSpec((width, unit), lambda i: (0, 0)),
            pl.BlockSpec(bias.shape, lambda i: (0, 0)),
            pl.BlockSpec(w_down.shape, lambda i: (0, 0)),
            pl.BlockSpec((tile, hd), lambda i: (i, 0)),
            pl.BlockSpec(w_out.shape, lambda i: (0, 0)),
        ],
        out_specs=[
            pl.BlockSpec((tile, unit), lambda i: (i, 0)),
            pl.BlockSpec((tile, unit), lambda i: (i, 0)),
            pl.BlockSpec((tile, width), lambda i: (i, 0)),
        ],
        out_shape=[
            jax.ShapeDtypeStruct((tokens, unit), bf16),
            jax.ShapeDtypeStruct((tokens, unit), bf16),
            jax.ShapeDtypeStruct((tokens, width), bf16),
        ],
        name="mlp_forward",
        **params((flops, 12 * tokens * width)),
    )(m, w_qu, bias, w_down, o, w_out)


def mlp_bwd_kernel(hd, dy_ref, wd_ref, slope_ref, dp_ref, wu_ref, wq_ref, wk_ref, wv_ref, vec_ref, du_ref, sum_ref, z_ref):
    dg = dot(dy_ref[...], wd_ref[...])
    du_ref[...] = (dg * slope_ref[...].astype(f32)).astype(bf16)
    total = jnp.sum(du_ref[...].astype(f32), axis=0, keepdims=True)
    total = jnp.broadcast_to(total, sum_ref.shape)

    @pl.when(pl.program_id(0) == 0)
    def _():
        sum_ref[...] = total

    @pl.when(pl.program_id(0) > 0)
    def _():
        sum_ref[...] += total

    da = (
        dot(dp_ref[:, :hd], wq_ref[...], 1, 1)
        + dot(dp_ref[:, hd : 2 * hd], wk_ref[...], 1, 1)
        + dot(dp_ref[:, 2 * hd :], wv_ref[...], 1, 1)
    )
    dm = dot(du_ref[...], wu_ref[...], 1, 1)
    z_ref[...] = (da * vec_ref[0:1] + dm * vec_ref[2:3]).astype(bf16)


def mlp_backward(dy, w_down, slope, dp, w_qu, vec, tile):
    tokens, width = dy.shape
    unit, hd = w_down.shape[1], dp.shape[1] // 3
    first = unit // hd
    flops = 2 * tokens * width * (2 * unit + 3 * hd)
    return pl.pallas_call(
        partial(mlp_bwd_kernel, hd),
        grid=(tokens // tile,),
        in_specs=[
            pl.BlockSpec((tile, width), lambda i: (i, 0)),
            pl.BlockSpec(w_down.shape, lambda i: (0, 0)),
            pl.BlockSpec((tile, unit), lambda i: (i, 0)),
            pl.BlockSpec((tile, 3 * hd), lambda i: (i, 0)),
            pl.BlockSpec((width, unit), lambda i: (0, 0)),
        ]
        + [pl.BlockSpec((width, hd), lambda i, j=j: (0, first + j)) for j in range(3)]
        + [pl.BlockSpec(vec.shape, lambda i: (0, 0))],
        out_specs=[
            pl.BlockSpec((tile, unit), lambda i: (i, 0)),
            pl.BlockSpec((8, unit), lambda i: (0, 0)),
            pl.BlockSpec((tile, width), lambda i: (i, 0)),
        ],
        out_shape=[
            jax.ShapeDtypeStruct((tokens, unit), bf16),
            jax.ShapeDtypeStruct((8, unit), f32),
            jax.ShapeDtypeStruct((tokens, width), bf16),
        ],
        name="mlp_backward",
        **params((flops, 12 * tokens * width)),
    )(dy, w_down, slope, dp, w_qu, w_qu, w_qu, w_qu, vec)


def adam_kernel(pair, rate, folded, c_ref, *refs):
    g_refs = refs[:pair]
    w_ref, m_ref, v_ref = refs[pair : pair + 3]
    outs = refs[-5:] if folded else refs[-4:]
    parts = [r[0].astype(f32) for r in g_refs]
    if pair == 2:
        swapped = c_ref[0] == 1
        parts = [jnp.where(swapped, parts[1], parts[0]), jnp.where(swapped, parts[0], parts[1])]
    raw = parts[0] if pair == 1 else jnp.concatenate(parts, axis=1)
    w = w_ref[...]
    if folded:
        vec_ref, colsum_ref = refs[pair + 3 : pair + 5]
        low = w.astype(bf16).astype(f32)
        colsum = colsum_ref[0:1]
        grad = raw * vec_ref[:, 0:1] + colsum * vec_ref[:, 1:2]
        moment = jnp.sum(low * raw, axis=1, keepdims=True)
        plain = jnp.sum(low * colsum, axis=1, keepdims=True)
        lane = lax.broadcasted_iota(jnp.int32, outs[4].shape, 1)
        sums = jnp.where(lane == 0, moment, jnp.where(lane == 1, plain, 0.0))
        start = pl.program_id(0) == 0
        if len(c_ref.shape) and True:
            for d in range(1, 2):
                start = jnp.logical_and(start, pl.program_id(d) == 0)

        @pl.when(start)
        def _():
            outs[4][...] = sums

        @pl.when(jnp.logical_not(start))
        def _():
            outs[4][...] += sums
    else:
        grad = raw
    result = adamw(w, grad, m_ref[...], v_ref[...], rate)
    for ref, value in zip(outs, result, strict=False):
        ref[...] = value


def adam_columns(lay, rate, parts, state, start, kinds, piece, held, fold=None):
    pair, nz = lay.pair, lay.nz
    rows, total = state[0].shape
    wide = pair * piece
    first = start // wide

    def col(j, z, c):
        return (0, first + j * nz + z)

    w_spec = pl.BlockSpec((rows, wide), col)
    in_specs = [pl.BlockSpec((1, rows, piece), lambda j, z, c: (z, 0, j))] * pair + [w_spec] * 3
    operands = list(parts) + list(state)
    out_specs = [w_spec] * 4
    out_shape = [jax.ShapeDtypeStruct((rows, total), f32)] * 4
    if fold is not None:
        vec, colsum = fold
        in_specs += [
            pl.BlockSpec(vec.shape, lambda j, z, c: (0, 0)),
            pl.BlockSpec((8, wide), lambda j, z, c: (0, j * nz + z)),
        ]
        operands += [vec, colsum]
        out_specs += [pl.BlockSpec((rows, LANES), lambda j, z, c: (0, 0))]
        out_shape += [jax.ShapeDtypeStruct((rows, LANES), f32)]
    aliases = {}
    if held:
        aliases = {1 + len(operands) + k: k for k in range(4)}
        in_specs += [pl.BlockSpec(memory_space=pl.ANY)] * 4
        operands += list(held)
    return pl.pallas_call(
        partial(adam_kernel, pair, rate, fold is not None),
        grid_spec=pltpu.PrefetchScalarGridSpec(
            num_scalar_prefetch=1, grid=(kinds, nz), in_specs=in_specs, out_specs=out_specs
        ),
        out_shape=out_shape,
        input_output_aliases=aliases,
        name="adam_columns",
        **params((30 * rows * kinds * piece * HEADS, 30 * rows * kinds * piece * HEADS)),
    )(jnp.reshape(lay.c, (1,)).astype(jnp.int32), *operands)


def gather_pieces(lay, own):
    piece = own
    for k in range(lay.nz):
        if k:
            piece = lay.ring(piece)
        pieces = [piece] + [lay.core_hop(piece, r) for r in range(1, lay.pair)]
        yield (lay.z - k) % lay.nz, pieces


def gather_tokens(lay, own):
    count, span, width = own.shape
    out = jnp.zeros((lay.pair * count * lay.nz, span, width), own.dtype)
    for where, pieces in gather_pieces(lay, own):
        for r, piece in enumerate(pieces):
            for s in range(count):
                out = lax.dynamic_update_index_in_dim(
                    out, piece[s], (r * count + s) * lay.nz + where, 0
                )
    return out.reshape(lay.pair * count, lay.nz * span, width)


def scatter_tokens(lay, partial_sum, count):
    total, length, width = partial_sum.shape
    span = length // lay.nz
    parts = [partial_sum[:count].reshape(count, lay.nz, span, width)]
    for r in range(1, lay.pair):
        other = lay.core_hop(partial_sum[r * count : (r + 1) * count], r)
        parts.append(other.reshape(count, lay.nz, span, width))

    def chunk(place):
        place = place % lay.nz
        return sum(
            lax.dynamic_index_in_dim(p, place, 1, keepdims=False).astype(f32) for p in parts
        )

    acc = chunk(lay.z - 1)
    for k in range(1, lay.nz):
        got = lay.ring(acc.astype(bf16))
        acc = got.astype(f32) + chunk(lay.z - 1 - k)
    return acc


def body(
    inputs,
    cotangent,
    attn_params,
    attn_first,
    attn_second,
    mlp_params,
    mlp_first,
    mlp_second,
    small,
    small_first,
    small_second,
):
    lay = Layout(lax.axis_size("dp"), lax.axis_size("seq"))
    groups, nz, pair = lay.groups, lay.nz, lay.pair
    count, span, width = inputs.shape
    rows = attn_params.shape[0]
    ff = mlp_params.shape[1] // 2
    hd = width // HEADS
    unit = ff // HEADS
    rot_dims = hd // 4
    score_scale = hd ** (-0.5)
    first_row = (lay.dp * nz + lay.z) * rows
    seqs, length = count * pair, span * nz
    tokens_here = seqs * length

    vec = small.astype(bf16)
    placed = jnp.concatenate([vec.T, jnp.zeros((3, rows), bf16)], axis=0)
    placed = lax.dynamic_update_slice(jnp.zeros((16, width), bf16), placed, (0, first_row))
    vectors = total_sum(lay, placed).astype(f32)
    norm_vec = vectors[:8]
    qkv_bias = vectors[6:9].reshape(3, HEADS, hd)
    qkv_bias = lax.dynamic_index_in_dim(qkv_bias, lay.t, 1, keepdims=False).reshape(1, 3 * hd)
    up_bias = lax.dynamic_slice(vectors[9:13].reshape(-1), (lay.t * unit,), (unit,))[None]
    out_bias = vectors[4] + vectors[5]

    attn_low = attn_params.astype(bf16)
    mlp_low = mlp_params.astype(bf16)

    def by_target(columns, kinds):
        piece = columns.shape[1] // kinds // HEADS
        blocks = columns.reshape(rows, kinds, nz, pair, piece).transpose(3, 2, 0, 1, 4)
        return blocks.reshape(pair, nz, rows, kinds * piece)

    def to_columns(blocks):
        halves = []
        for r in range(pair):
            half = lax.dynamic_index_in_dim(blocks, lay.c ^ r, 0, keepdims=False)
            if r:
                half = lay.core_hop(half, r)
            half = lax.all_to_all(half, "seq", 0, 0, tiled=True)
            halves.append(half.reshape(nz * rows, -1))
        return halves

    def whole(halves):
        n = halves[0].shape[1]
        out = jnp.zeros((groups * pair, nz * rows, n), bf16)
        for r, half in enumerate(halves):
            for m, v in group_gather(lay, half, bool(r)).items():
                out = lax.dynamic_update_index_in_dim(
                    out, v, (lay.g ^ m) * pair + (lay.c ^ r), 0
                )
        return out.reshape(width, n)

    qu_blocks = jnp.concatenate(
        [by_target(mlp_low[:, :ff], 1), by_target(attn_low[:, : 3 * width], 3)], axis=-1
    )
    w_qu = whole(to_columns(qu_blocks))
    w_down = whole(to_columns(by_target(mlp_low[:, ff:], 1)))
    w_out = lax.ppermute(attn_low[:, 3 * width :], AXES, lay.head_owner_perm())
    w_out_buf = jnp.zeros((groups, rows, width), bf16)
    for m, v in group_gather(lay, w_out, True).items():
        w_out_buf = lax.dynamic_update_index_in_dim(w_out_buf, v, lay.g ^ m, 0)
    w_out = w_out_buf.reshape(hd, width)

    held = ()
    for where, pieces in gather_pieces(lay, inputs):
        held = norm_place(lay, pieces, norm_vec, where, held)
    a_all, m_all, x_all = (v.reshape(seqs, length, width) for v in held)
    dy_all = gather_tokens(lay, cotangent)

    positions = jnp.arange(length, dtype=f32)
    frequency = 10000.0 ** (-(jnp.arange(rot_dims // 2, dtype=f32) * 2.0) / rot_dims)
    angles = positions[:, None] * frequency[None, :]
    cosine, sine = jnp.cos(angles), jnp.sin(angles)
    blank = jnp.zeros_like(sine)
    rest = jnp.zeros((length, LANES - rot_dims), f32)
    tables = jnp.stack(
        [
            jnp.concatenate([cosine, cosine, rest + 1.0], axis=1),
            jnp.concatenate([-sine, blank, rest], axis=1),
            jnp.concatenate([blank, sine, rest], axis=1),
        ]
    )

    tile = min(512, tokens_here)
    qkv, o, lse = attn_forward(a_all, w_qu, qkv_bias, tables, unit, hd, score_scale)
    flat = (tokens_here, width)
    o = o.reshape(tokens_here, hd)
    g, slope, out_part = mlp_forward(m_all.reshape(flat), w_qu, up_bias, w_down, o, w_out, tile)
    out_sum = scatter_tokens(lay, out_part.reshape(seqs, length, width), count)
    outputs = (inputs.astype(f32) + out_sum + out_bias).astype(bf16)

    dy_flat, x_flat = dy_all.reshape(flat), x_all.reshape(flat)
    dp, dp_sums = attn_backward(dy_all, w_out, qkv, lse, tables, score_scale)
    dp = dp.reshape(tokens_here, 3 * hd)
    du, du_sums, z_part = mlp_backward(dy_flat, w_down, slope, dp, w_qu, norm_vec, tile)
    normed_grad = scatter_tokens(lay, z_part.reshape(seqs, length, width), count)
    normed, scaling = normalize(inputs.astype(f32))
    grad_mean = jnp.mean(normed_grad, axis=-1, keepdims=True)
    grad_proj = jnp.mean(normed_grad * normed, axis=-1, keepdims=True)
    upstream = cotangent.astype(f32)
    input_grad = upstream + scaling * (normed_grad - grad_mean - normed * grad_proj)

    def own_rows(partial_sum):
        n = partial_sum.shape[-1]
        stacked = partial_sum.reshape(groups * pair, nz * rows, n)
        parts = []
        for r in range(pair):
            blocks = {
                m: lax.dynamic_index_in_dim(
                    stacked, (lay.g ^ m) * pair + (lay.c ^ r), 0, keepdims=False
                )
                for m in range(groups)
            }
            half = group_scatter(lay, blocks, bool(r)).astype(bf16).reshape(nz, rows, n)
            half = lax.all_to_all(half, "seq", 0, 0, tiled=True)
            parts.append(lay.core_hop(half, r) if r else half)
        return parts

    down_parts = own_rows(dot(dy_flat, g, 0, 0).astype(bf16))
    up_parts = own_rows(dot(x_flat, du, 0, 0).astype(bf16))
    qkv_parts = own_rows(dot(x_flat, dp, 0, 0).astype(bf16))
    out_grad = dot(o, dy_flat, 0, 0).astype(bf16).reshape(groups, rows, width)
    out_grad = {
        m: lax.dynamic_index_in_dim(out_grad, lay.g ^ m, 0, keepdims=False) for m in range(groups)
    }
    out_grad = group_scatter(lay, out_grad, True).astype(bf16)
    out_grad = lax.ppermute(out_grad, AXES, [(b, a) for a, b in lay.head_owner_perm()])

    qkv_sum = jnp.sum(dp_sums[:, 0], axis=0).reshape(3, 1, hd)
    qkv_sum = lax.dynamic_update_slice(jnp.zeros((3, HEADS, hd), f32), qkv_sum, (0, lay.t, 0))
    up_sum = lax.dynamic_update_slice(jnp.zeros((ff,), f32), du_sums[0], (lay.t * unit,))
    upstream_sum = jnp.sum(upstream, axis=(0, 1))
    sums = jnp.concatenate([qkv_sum.reshape(-1), up_sum, upstream_sum]).reshape(8, width)
    sums = total_sum(lay, sums)
    qkv_sum = jnp.broadcast_to(sums[:3].reshape(1, -1), (8, 3 * width))
    up_sum = jnp.broadcast_to(sums[3:7].reshape(1, -1), (8, ff))

    own_vec = vec.astype(f32)
    mlp_state = (mlp_params, mlp_first, mlp_second)
    attn_state = (attn_params, attn_first, attn_second)
    mlp_result = adam_columns(lay, rate_mlp, down_parts, mlp_state, ff, 1, unit, ())
    *mlp_result, up_small = adam_columns(
        lay, rate_mlp, up_parts, mlp_state, 0, 1, unit, mlp_result, (own_vec[:, 2:4], up_sum)
    )
    *attn_result, qkv_small = adam_columns(
        lay, rate_attention, qkv_parts, attn_state, 0, 3, hd, (), (own_vec[:, 0:2], qkv_sum)
    )
    out_state = tuple(v[:, 3 * width :] for v in attn_state)
    out_result = adamw(out_state[0], out_grad.astype(f32), out_state[1], out_state[2], rate_attention)
    attn_result = [
        lax.dynamic_update_slice(v, n, (0, 3 * width)) for v, n in zip(attn_result, out_result)
    ]
    own_sums = lax.dynamic_slice(sums, (0, first_row), (8, rows)).T
    small_grad = jnp.concatenate(
        [
            qkv_small[:, 0:2],
            up_small[:, 0:2],
            own_sums[:, 7:8],
            own_sums[:, 7:8],
            own_sums[:, :7],
        ],
        axis=1,
    )
    small_result = adamw(small, small_grad, small_first, small_second, rate_vector)
    return (outputs, input_grad, *attn_result, *mlp_result, *small_result)


def solution(mesh):
    tokens, weights = P("dp", "seq", None), P(("dp", "seq"), None)
    return jax.shard_map(
        body,
        mesh=mesh,
        in_specs=(tokens,) * 2 + (weights,) * 9,
        out_specs=(tokens,) * 2 + (weights,) * 12,
        check_vma=False,
    )
```

```python
from functools import partial

import jax
import jax.numpy as jnp
from jax import lax
from jax.experimental import pallas as pl
from jax.experimental.pallas import tpu as pltpu
from jax.sharding import PartitionSpec as P

HEADS = 8
STEP = 10
AXES = ("dp", "seq")
LANES = 128
VMEM_LIMIT = 56 * 2**20

norm_eps = 1e-05
masked_value = -1e30
beta_first = 0.9
beta_second = 0.95
adam_eps = 1e-08
decay_rate = 0.01
rate_attention = 0.06
rate_mlp = 0.02
rate_vector = 0.2

f32 = jnp.float32
bf16 = jnp.bfloat16


def normalize(values):
    row_mean = jnp.mean(values, axis=-1, keepdims=True)
    centred = values - row_mean
    spread = jnp.mean(centred * centred, axis=-1, keepdims=True)
    scaling = lax.rsqrt(spread + norm_eps)
    return (centred * scaling, scaling)


def dot(left_op, right_op, left_dim=1, right_dim=0):
    return lax.dot_general(
        left_op,
        right_op,
        (((left_dim,), (right_dim,)), ((), ())),
        preferred_element_type=f32,
    )


def adamw(master, gradient, first_old, second_old, step_rate):
    first_new = beta_first * first_old + (1.0 - beta_first) * gradient
    second_new = beta_second * second_old + (1.0 - beta_second) * gradient * gradient
    first_hat = first_new / (1.0 - beta_first**STEP)
    second_hat = second_new / (1.0 - beta_second**STEP)
    updated = master - step_rate * (
        first_hat / (jnp.sqrt(second_hat) + adam_eps) + decay_rate * master
    )
    return (gradient, updated, first_new, second_new)


def params(cost=None, **kw):
    return dict(
        compiler_params=pltpu.CompilerParams(vmem_limit_bytes=VMEM_LIMIT, **kw),
        cost_estimate=cost and pl.CostEstimate(flops=cost[0] // 1000 + 1, bytes_accessed=cost[1] // 1000 + 1, transcendentals=0),
    )


class Layout:
    def __init__(self, nd, nz):
        self.nd, self.nz = nd, nz
        self.pair = HEADS // nz
        self.groups = nd // self.pair
        self.dp = lax.axis_index("dp")
        self.z = lax.axis_index("seq")
        self.g = self.dp // self.pair
        self.c = self.dp % self.pair
        self.t = self.z * self.pair + self.c

    def perm(self, target):
        pairs = []
        for dp in range(self.nd):
            for z in range(self.nz):
                goal = target(dp // self.pair, dp % self.pair, z)
                if goal is not None:
                    g, c, s = goal
                    pairs.append((dp * self.nz + z, (g * self.pair + c) * self.nz + s))
        return pairs

    def hop(self, value, target):
        return lax.ppermute(value, AXES, self.perm(target))

    def group_hop(self, value, bit):
        return self.hop(value, lambda g, c, z: (g ^ bit, c, z))

    def core_hop(self, value, r):
        return self.hop(value, lambda g, c, z: (g, c ^ r, z))

    def ring(self, value):
        return self.hop(value, lambda g, c, z: (g, c, (z + 1) % self.nz))

    def flat_hop(self, value, bit):
        return lax.ppermute(value, AXES, [(i, i ^ bit) for i in range(self.nd * self.nz)])

    def head_owner_perm(self):
        pairs = []
        for r in range(self.nd * self.nz):
            head, quarter = r // self.groups, r % self.groups
            s, c = head // self.pair, head % self.pair
            pairs.append((r, (quarter * self.pair + c) * self.nz + s))
        return pairs


def after(values, *deps):
    flat, tree = jax.tree.flatten((values, deps))
    return jax.tree.unflatten(tree, lax.optimization_barrier(flat))[0]


def join(*values):
    return after(values)


def bits_of(count, descending):
    bits = []
    bit = 1
    while bit < count:
        bits.append(bit)
        bit *= 2
    return bits[::-1] if descending else bits


class GroupGather:
    def __init__(self, lay, block, descending):
        self.lay = lay
        self.rows = block.shape[0]
        self.held = {0: (block, 0)}
        self.rounds = [[] for _ in bits_of(lay.groups, False)]
        known = [0]
        for bit in bits_of(lay.groups, descending):
            for m in list(known):
                self.rounds[bin(m).count("1")].append((m, bit))
                known.append(m ^ bit)

    def block(self, m):
        array, first = self.held[m]
        return array[first : first + self.rows]

    def send(self, depth):
        if depth < len(self.rounds):
            for m, bit in self.rounds[depth]:
                self.held[m ^ bit] = (self.lay.group_hop(self.block(m), bit), 0)

    @staticmethod
    def send_first(halves):
        lay = halves[0].lay
        stack = jnp.concatenate([h.block(0) for h in halves])
        for bit in bits_of(lay.groups, False):
            got = lay.group_hop(stack, bit)
            first = 0
            for h in halves:
                h.held[bit] = (got, first)
                first += h.rows

    @property
    def state(self):
        return {m: v for m, (v, _) in self.held.items()}

    @state.setter
    def state(self, state):
        for m, v in state.items():
            self.held[m] = (v, self.held[m][1])

    def rest(self, depth):
        while depth < len(self.rounds):
            self.send(depth)
            depth += 1
        return self.held


class GroupScatter:
    def __init__(self, lay, keep, send, descending):
        self.lay = lay
        self.keep, self.send = keep, send
        self.bits = bits_of(lay.groups, descending)
        self.at = 0

    @staticmethod
    def member(lay, index, descending):
        bits = bits_of(lay.groups, descending)
        return sum(bit for j, bit in enumerate(bits) if index >> (len(bits) - 1 - j) & 1)

    @property
    def state(self):
        return (self.keep, self.send)

    @state.setter
    def state(self, state):
        self.keep, self.send = state

    def step(self):
        if self.at < len(self.bits):
            self.send = self.lay.group_hop(self.send, self.bits[self.at])
            self.at += 1

    def fold(self):
        total = self.keep.astype(f32) + self.send.astype(f32)
        half = total.shape[0] // 2
        self.keep, self.send = total[:half], total[half:].astype(bf16)

    def result(self):
        return (self.keep.astype(f32) + self.send.astype(f32))[0]


def cast_kernel(c_ref, *refs):
    out_ref = refs[-1]
    at = 0
    for ref in refs[:-1]:
        out_ref[0, :, at : at + ref.shape[1]] = ref[...].astype(bf16)
        at += ref.shape[1]


def prepare(lay, r, sources):
    rows, pair, nz = sources[0][0].shape[0], lay.pair, lay.nz

    def spec(first, width):
        if first is None:
            return pl.BlockSpec((rows, width), lambda z, c: (0, 0))
        return pl.BlockSpec((rows, width), lambda z, c: (0, first + z * pair + (c[0] ^ r)))

    total = sum(width for _, _, width in sources)
    return pl.pallas_call(
        cast_kernel,
        grid_spec=pltpu.PrefetchScalarGridSpec(
            num_scalar_prefetch=1,
            grid=(nz,),
            in_specs=[spec(first, width) for _, first, width in sources],
            out_specs=pl.BlockSpec((1, rows, total), lambda z, c: (z, 0, 0)),
        ),
        out_shape=jax.ShapeDtypeStruct((nz, rows, total), bf16),
        name="prepare",
        **params((rows * total * nz, rows * total * nz * 6)),
    )(jnp.reshape(lay.c, (1,)).astype(jnp.int32), *[v for v, _, _ in sources])


def place_kernel(count, tile, slot_ref, *refs):
    out_ref, sems = refs[-2], refs[-1]
    here = pl.ds(pl.multiple_of(pl.program_id(0) * tile, tile), tile)

    def copy(i):
        return pltpu.make_async_copy(refs[i], out_ref.at[slot_ref[i], here], sems.at[i])

    for i in range(count):

        @pl.when(slot_ref[i] >= 0)
        def _(i=i):
            copy(i).start()

    for i in range(count):

        @pl.when(slot_ref[i] >= 0)
        def _(i=i):
            copy(i).wait()


def place(blocks, slots, rows, total, held=None):
    count = len(blocks)
    width = blocks[0][0].shape[1]
    tile = max(min(64, rows), rows // 2)
    operands = [v for v, _ in blocks] + ([] if held is None else [held])
    any_spec = pl.BlockSpec(memory_space=pl.ANY)
    return pl.pallas_call(
        partial(place_kernel, count, tile),
        grid_spec=pltpu.PrefetchScalarGridSpec(
            num_scalar_prefetch=1,
            grid=(rows // tile,),
            in_specs=[
                pl.BlockSpec(
                    (tile, width),
                    lambda i, slot, first=first, j=j: (
                        first // tile + jnp.where(slot[j] >= 0, i, 0),
                        0,
                    ),
                )
                for j, (_, first) in enumerate(blocks)
            ]
            + [any_spec] * (len(operands) - count),
            out_specs=any_spec,
            scratch_shapes=[pltpu.SemaphoreType.DMA((count,))],
        ),
        out_shape=jax.ShapeDtypeStruct((total, rows, width), blocks[0][0].dtype),
        input_output_aliases={} if held is None else {count + 1: 0},
        name="place",
        **params((count, 4 * count * rows * width)),
    )(jnp.stack([jnp.asarray(v, jnp.int32) for v in slots]), *operands)


def flip_kernel(in_ref, out_ref):
    out_ref[...] = in_ref[...].astype(f32).T


def last_columns(array):
    rows, total = array.shape
    return pl.pallas_call(
        flip_kernel,
        grid=(1,),
        in_specs=[pl.BlockSpec((rows, LANES), lambda i: (0, total // LANES - 1))],
        out_specs=pl.BlockSpec((LANES, rows), lambda i: (0, 0)),
        out_shape=jax.ShapeDtypeStruct((LANES, rows), f32),
        name="last_columns",
        **params(),
    )(array)


def block_order(lay):
    order = []
    for part in (1, 0):
        for r in range(lay.pair):
            for i in range(lay.groups // 2):
                m = GroupScatter.member(lay, part * (lay.groups // 2) + i, bool(r))
                order.append((lay.g ^ m) * lay.pair + (lay.c ^ r))
    return jnp.stack(order).astype(jnp.int32)


def write_block(half, outs, at, value):
    i = pl.program_id(0)
    for k, out in enumerate(outs):

        @pl.when(jnp.logical_and(i >= k * half, i < (k + 1) * half))
        def _(out=out):
            out[0, :, at : at + value.shape[1]] = value


def gradient_kernel(half, block_ref, left_ref, right_ref, *outs):
    write_block(half, outs, 0, dot(left_ref[...], right_ref[...], 0, 0).astype(bf16))


def folded_kernel(half, first, gain, rides, block_ref, x_ref, right_ref, sums_ref, w_ref, small_ref, *refs):
    others, outs = (refs[:2], refs[2:]) if rides else ((), refs[:-1])
    vec = small_ref[...].astype(f32)
    raw = dot(x_ref[...], right_ref[...], 0, 0)
    sums = sums_ref[0:1]
    grad = raw * vec[:, gain : gain + 1] + sums * vec[:, gain + 1 : gain + 2]
    write_block(half, outs, 0, grad.astype(bf16))
    w = w_ref[:, first : first + raw.shape[1]].astype(f32)
    lane = lax.broadcasted_iota(jnp.int32, vec.shape, 1)
    moment = jnp.sum(w * raw, axis=1, keepdims=True)
    plain = jnp.sum(w * sums, axis=1, keepdims=True)
    lanes = jnp.where(lane == gain, moment, jnp.where(lane == gain + 1, plain, 0.0))
    if rides:
        lanes = lanes + others[0][...] + others[1][...]
        write_block(half, outs, raw.shape[1], lanes.astype(bf16))
    else:
        refs[-1][...] = lanes


def gradient_call(lay, kernel, left, rights, by_rows, n, more=()):
    tokens, width = left.shape
    pair, half = lay.pair, lay.groups // 2
    rows = width // (lay.groups * pair)
    outs = 2 * pair

    def out_map(k):
        return lambda i, block: (jnp.clip(i - k * half, 0, half - 1), 0, 0)

    def row_map(column):
        return lambda i, block: (block[i], column)

    values = pl.pallas_call(
        partial(kernel, half),
        grid_spec=pltpu.PrefetchScalarGridSpec(
            num_scalar_prefetch=1,
            grid=(outs * half,),
            in_specs=[pl.BlockSpec((tokens, rows), lambda i, block: (0, block[i]))]
            + [pl.BlockSpec(v.shape, lambda i, block: (0, 0)) for v in rights]
            + [pl.BlockSpec((rows, size), row_map(column)) for _, size, column in by_rows],
            out_specs=[pl.BlockSpec((1, rows, n), out_map(k)) for k in range(outs)]
            + [pl.BlockSpec((rows, size), row_map(0)) for size in more],
        ),
        out_shape=[jax.ShapeDtypeStruct((half, rows, n), bf16)] * outs
        + [jax.ShapeDtypeStruct((width, size), f32) for size in more],
        name="gradient",
        **params((2 * tokens * width * n, 2 * (tokens * width + tokens * n + width * n))),
    )(block_order(lay), left, *rights, *[v for v, _, _ in by_rows])
    parts = [GroupScatter(lay, values[pair + r], values[r], bool(r)) for r in range(pair)]
    return (parts, *values[outs:])


def gradient(lay, left, right):
    return gradient_call(lay, gradient_kernel, left, [right], [], right.shape[1])[0]


def folded_gradient(lay, x, right, sums, w_qu, first, gain, others=()):
    total = w_qu.shape[1]
    by_rows = [(w_qu, total, 0), (w_qu, LANES, total // LANES - 1)]
    by_rows += [(v, LANES, 0) for v in others]
    rides = len(others) > 0

    def call(half, *refs):
        folded_kernel(half, first, gain, rides, *refs)

    n = right.shape[1] + (LANES if rides else 0)
    return gradient_call(lay, call, x, [right, sums], by_rows, n, () if rides else (LANES,))


def fold_kernel(*refs):
    count = len(refs) // 4
    for p in range(count):
        keep, got, next_keep, next_send = refs[p], refs[count + p], refs[2 * count + p], refs[3 * count + p]
        half = next_keep.shape[0]
        total = keep[...].astype(f32) + got[...].astype(f32)
        next_keep[...] = total[:half]
        next_send[...] = total[half:].astype(bf16)


def fold(parts):
    held, rows, n = parts[0].keep.shape
    half = held // 2
    tile = min(64, rows)
    full = pl.BlockSpec((held, tile, n), lambda i: (0, i, 0))
    part = pl.BlockSpec((half, tile, n), lambda i: (0, i, 0))
    count = len(parts)
    values = pl.pallas_call(
        fold_kernel,
        grid=(rows // tile,),
        in_specs=[full] * (2 * count),
        out_specs=[part] * (2 * count),
        out_shape=[jax.ShapeDtypeStruct((half, rows, n), f32)] * count
        + [jax.ShapeDtypeStruct((half, rows, n), bf16)] * count,
        name="fold",
        **params((held * rows * n, 8 * held * rows * n)),
    )(*[p.keep for p in parts], *[p.send for p in parts])
    for k, p in enumerate(parts):
        p.keep, p.send = values[k], values[count + k]


def blocks_kernel(count, *refs):
    out_ref = refs[-1]
    for p in range(count):
        out_ref[0, p] = (refs[p][0].astype(f32) + refs[count + p][0].astype(f32)).astype(bf16)


def final_blocks(parts, nz):
    _, total, n = parts[0].keep.shape
    rows, count = total // nz, len(parts)
    return pl.pallas_call(
        partial(blocks_kernel, count),
        grid=(nz,),
        in_specs=[pl.BlockSpec((1, rows, n), lambda i: (0, i, 0))] * (2 * count),
        out_specs=pl.BlockSpec((1, count, rows, n), lambda i: (i, 0, 0, 0)),
        out_shape=jax.ShapeDtypeStruct((nz, count, rows, n), bf16),
        name="final_blocks",
        **params((count * total * n, 8 * count * total * n)),
    )(*[p.keep for p in parts], *[p.send for p in parts])


def chunk_kernel(count, ways, slot_ref, *refs):
    for k in range(ways):

        @pl.when(slot_ref[k] >= 0)
        def _(k=k):
            total = sum(refs[k * count + p][...].astype(f32) for p in range(count))
            out = refs[-ways + k]
            out[...] = total.astype(out.dtype)


def chunk_sums(parts, slots, received):
    count, _, span, width = parts[0].shape
    tile = min(span, 128)
    ways = len(slots)

    def whole(k):
        return lambda i, slot: (0, jnp.where(slot[k] >= 0, i, 0), 0)

    def part(k):
        return lambda i, slot: (0, jnp.maximum(slot[k], 0), jnp.where(slot[k] >= 0, i, 0), 0)

    in_specs, operands = [], []
    for k in range(ways):
        for p in parts:
            in_specs.append(pl.BlockSpec((count, None, tile, width), part(k)))
            operands.append(p)
        if received:
            in_specs.append(pl.BlockSpec((count, tile, width), whole(k)))
            operands.append(received[k])
    shape = jax.ShapeDtypeStruct((count, span, width), bf16)
    return pl.pallas_call(
        partial(chunk_kernel, len(operands) // ways, ways),
        grid_spec=pltpu.PrefetchScalarGridSpec(
            num_scalar_prefetch=1,
            grid=(span // tile,),
            in_specs=in_specs,
            out_specs=[pl.BlockSpec((count, tile, width), whole(k)) for k in range(ways)],
        ),
        out_shape=[shape] * ways,
        name="chunk_sums",
        **params((8 * count * span * width, 16 * count * span * width)),
    )(jnp.stack(slots).astype(jnp.int32), *operands)


def turn(values, cosine, low_sine, high_sine, quarter):
    head = values[:, :LANES]
    turned = (
        head * cosine
        + pltpu.roll(head, LANES - quarter, 1) * low_sine
        + pltpu.roll(head, quarter, 1) * high_sine
    )
    return jnp.concatenate([turned, values[:, LANES:]], axis=1)


def piece_kernel(pair, places, quarter, pos_ref, *refs):
    x_refs, refs = refs[: pair * places], refs[pair * places :]
    for p in range(places):

        @pl.when(pl.program_id(1) == p)
        def _(p=p):
            piece_rows(pair, quarter, x_refs[p * pair : (p + 1) * pair], refs)


def piece_rows(pair, quarter, x_refs, refs):
    vec_ref, w_ref, qkv_bias_ref, up_bias_ref, tab_ref = refs[:5]
    x_out, qkv_out, g_out, slope_out = refs[-4:]
    tile = x_refs[0].shape[1]
    unit, wide = g_out.shape[-1], qkv_out.shape[-1]
    hd = wide // 3
    x = jnp.concatenate([ref[0].astype(f32) for ref in x_refs])
    normed, _ = normalize(x)
    a = (normed * vec_ref[0:1] + vec_ref[1:2]).astype(bf16)
    m = (normed * vec_ref[2:3] + vec_ref[3:4]).astype(bf16)
    cosine, low_sine, high_sine = (jnp.concatenate([tab_ref[k]] * pair) for k in range(3))

    def put(out, at, value):
        value = value.astype(bf16)
        for r in range(pair):
            out[r, 0, 0, :, at : at + value.shape[1]] = value[r * tile : (r + 1) * tile]

    put(x_out, 0, normed)
    for j in range(3):
        part = dot(a, w_ref[:, unit + j * hd : unit + (j + 1) * hd])
        part = part + qkv_bias_ref[0:1, j * hd : (j + 1) * hd]
        put(qkv_out, j * hd, turn(part, cosine, low_sine, high_sine, quarter) if j < 2 else part)
    u = dot(m, w_ref[:, :unit]) + up_bias_ref[0:1]
    half = 0.5 * (1.0 + lax.erf(u * (0.5**0.5)))
    put(g_out, 0, u * half)
    put(slope_out, 0, half + u * (jnp.exp(-0.5 * u * u) * 0.3989422804014327))


def piece_forward(lay, pieces, where, vec, w_qu, qkv_bias, up_bias, tables, held):
    count, span, width = pieces[0].shape
    pair, nz, places = lay.pair, lay.nz, len(where)
    unit, wide = up_bias.shape[1], qkv_bias.shape[1]
    tile = min(span, 128)
    steps = span // tile

    def out(n):
        return (
            jax.ShapeDtypeStruct((pair, count, nz, span, n), bf16),
            pl.BlockSpec((pair, 1, 1, tile, n), lambda i, p, j, pos: (0, i, pos[p], j, 0)),
        )

    def whole(v):
        return pl.BlockSpec(v.shape, lambda i, p, j, pos: (0,) * v.ndim)

    def row_map(q):
        return lambda i, p, j, pos: (i, jnp.where(p == q, j, jnp.where(p < q, 0, steps - 1)), 0)

    outs = [out(n) for n in (width, wide, unit, unit)]
    in_specs = [pl.BlockSpec((1, tile, width), row_map(q)) for q in range(places) for _ in range(pair)]
    in_specs += [whole(v) for v in (vec, w_qu, qkv_bias, up_bias)]
    in_specs += [pl.BlockSpec((3, tile, LANES), lambda i, p, j, pos: (0, pos[p] * steps + j, 0))]
    in_specs += [pl.BlockSpec(memory_space=pl.ANY)] * len(held)
    tokens = pair * places * count * span
    return pl.pallas_call(
        partial(piece_kernel, pair, places, wide // 24),
        grid_spec=pltpu.PrefetchScalarGridSpec(
            num_scalar_prefetch=1,
            grid=(count, places, steps),
            in_specs=in_specs,
            out_specs=[o[1] for o in outs],
        ),
        out_shape=[o[0] for o in outs],
        input_output_aliases={pair * places + 6 + k: k for k in range(len(held))},
        name="piece_forward",
        **params((2 * tokens * width * (unit + wide), 12 * tokens * width)),
    )(
        jnp.stack(where).astype(jnp.int32),
        *pieces,
        vec,
        w_qu,
        qkv_bias,
        up_bias,
        tables,
        *held,
    )


def attn_fwd_kernel(scale, tile, qkv_ref, o_ref, lse_ref):
    length, hd = o_ref.shape[1:]
    for i in range(length // tile):
        end = (i + 1) * tile
        q_i = qkv_ref[0, i * tile : end, :hd]
        scores = dot(q_i, qkv_ref[0, :end, hd : 2 * hd], 1, 1) * scale
        row = lax.broadcasted_iota(jnp.int32, scores.shape, 0) + i * tile
        col = lax.broadcasted_iota(jnp.int32, scores.shape, 1)
        scores = jnp.where(col <= row, scores, masked_value)
        row_max = jnp.max(scores, axis=1, keepdims=True)
        terms = jnp.exp(scores - row_max)
        row_sum = jnp.sum(terms, axis=1, keepdims=True)
        probs = (terms / row_sum).astype(bf16)
        o_ref[0, i * tile : end] = dot(probs, qkv_ref[0, :end, 2 * hd :]).astype(bf16)
        lse_ref[0, i * tile : end] = jnp.broadcast_to(row_max + jnp.log(row_sum), (tile, LANES))


def attn_forward(qkv, scale):
    seqs, length, wide = qkv.shape
    hd = wide // 3
    return pl.pallas_call(
        partial(attn_fwd_kernel, scale, min(256, length)),
        grid=(seqs,),
        in_specs=[pl.BlockSpec((1, length, wide), lambda s: (s, 0, 0))],
        out_specs=[
            pl.BlockSpec((1, length, hd), lambda s: (s, 0, 0)),
            pl.BlockSpec((1, length, LANES), lambda s: (s, 0, 0)),
        ],
        out_shape=[
            jax.ShapeDtypeStruct((seqs, length, hd), bf16),
            jax.ShapeDtypeStruct((seqs, length, LANES), f32),
        ],
        name="attn_forward",
        **params((4 * seqs * length * length * hd, 8 * seqs * length * wide)),
    )(qkv)


def attn_bwd_kernel(quarter, scale, tile, dy_ref, wo_ref, qkv_ref, lse_ref, tab_ref, dp_ref, sum_ref, do_s, dk_s, dv_s):
    length = dy_ref.shape[1]
    hd = wo_ref.shape[0]
    cosine, low_sine, high_sine = tab_ref[0], -tab_ref[1], -tab_ref[2]
    do_s[...] = dot(dy_ref[0], wo_ref[...], 1, 1).astype(bf16)
    steps = length // tile
    for i in reversed(range(steps)):
        end = (i + 1) * tile
        q_i = qkv_ref[0, i * tile : end, :hd]
        k = qkv_ref[0, :end, hd : 2 * hd]
        do_i = do_s[i * tile : end]
        scores = dot(q_i, k, 1, 1) * scale
        row = lax.broadcasted_iota(jnp.int32, scores.shape, 0) + i * tile
        col = lax.broadcasted_iota(jnp.int32, scores.shape, 1)
        probs = jnp.where(col <= row, jnp.exp(scores - lse_ref[0, i * tile : end, 0:1]), 0.0)
        probs_grad = dot(do_i, qkv_ref[0, :end, 2 * hd :], 1, 1)
        row_dot = jnp.sum(probs * probs_grad, axis=1, keepdims=True)
        score_grad = (probs * (probs_grad - row_dot)).astype(bf16)
        dq = dot(score_grad, k) * scale
        dp_ref[0, i * tile : end, :hd] = turn(
            dq,
            cosine[i * tile : end],
            low_sine[i * tile : end],
            high_sine[i * tile : end],
            quarter,
        ).astype(bf16)
        dk = dot(score_grad, q_i, 0, 0)
        dv = dot(probs.astype(bf16), do_i, 0, 0)
        if i == steps - 1:
            dk_s[...] = dk
            dv_s[...] = dv
        else:
            dk_s[:end] += dk
            dv_s[:end] += dv
    dp_ref[0, :, hd : 2 * hd] = turn(
        dk_s[...] * scale, cosine, low_sine, high_sine, quarter
    ).astype(bf16)
    dp_ref[0, :, 2 * hd :] = dv_s[...].astype(bf16)
    total = jnp.sum(dp_ref[0].astype(f32), axis=0, keepdims=True)
    sum_ref[0] = jnp.broadcast_to(total, sum_ref.shape[1:])


def attn_backward(dy, w_out, qkv, lse, tables, scale):
    seqs, length, width = dy.shape
    hd = w_out.shape[0]
    flops = 2 * seqs * length * (hd * width + 5 * length * hd)
    return pl.pallas_call(
        partial(attn_bwd_kernel, hd // 8, scale, min(256, length)),
        grid=(seqs,),
        in_specs=[
            pl.BlockSpec((1, length, width), lambda s: (s, 0, 0)),
            pl.BlockSpec(w_out.shape, lambda s: (0, 0)),
            pl.BlockSpec((1, length, 3 * hd), lambda s: (s, 0, 0)),
            pl.BlockSpec((1, length, LANES), lambda s: (s, 0, 0)),
            pl.BlockSpec(tables.shape, lambda s: (0, 0, 0)),
        ],
        out_specs=[
            pl.BlockSpec((1, length, 3 * hd), lambda s: (s, 0, 0)),
            pl.BlockSpec((1, 8, 3 * hd), lambda s: (s, 0, 0)),
        ],
        out_shape=[
            jax.ShapeDtypeStruct((seqs, length, 3 * hd), bf16),
            jax.ShapeDtypeStruct((seqs, 8, 3 * hd), f32),
        ],
        scratch_shapes=[
            pltpu.VMEM((length, hd), bf16),
            pltpu.VMEM((length, hd), f32),
            pltpu.VMEM((length, hd), f32),
        ],
        name="attn_backward",
        **params((flops, 8 * seqs * length * width)),
    )(dy, w_out, qkv, lse, tables)


def output_kernel(g_ref, wd_ref, o_ref, wo_ref, out_ref):
    total = dot(g_ref[...], wd_ref[...], 1, 1) + dot(o_ref[...], wo_ref[...])
    out_ref[...] = total.astype(bf16)


def output_forward(g, w_down, o, w_out, tile, part, parts):
    tokens, unit = g.shape[0] // parts, g.shape[1]
    width, hd = w_down.shape[0], o.shape[1]
    first = part * tokens // tile
    return pl.pallas_call(
        output_kernel,
        grid=(tokens // tile,),
        in_specs=[
            pl.BlockSpec((tile, unit), lambda i: (first + i, 0)),
            pl.BlockSpec(w_down.shape, lambda i: (0, 0)),
            pl.BlockSpec((tile, hd), lambda i: (first + i, 0)),
            pl.BlockSpec(w_out.shape, lambda i: (0, 0)),
        ],
        out_specs=pl.BlockSpec((tile, width), lambda i: (i, 0)),
        out_shape=jax.ShapeDtypeStruct((tokens, width), bf16),
        name="output_forward",
        **params((2 * tokens * width * (unit + hd), 8 * tokens * width)),
    )(g, w_down, o, w_out)


def hidden_kernel(dy_ref, wd_ref, slope_ref, du_ref, sum_ref):
    dg = dot(dy_ref[...], wd_ref[...])
    du_ref[...] = (dg * slope_ref[...].astype(f32)).astype(bf16)
    total = jnp.sum(du_ref[...].astype(f32), axis=0, keepdims=True)
    total = jnp.broadcast_to(total, sum_ref.shape)

    @pl.when(pl.program_id(0) == 0)
    def _():
        sum_ref[...] = total

    @pl.when(pl.program_id(0) > 0)
    def _():
        sum_ref[...] += total


def hidden_backward(dy, w_down, slope, tile):
    tokens, width = dy.shape
    unit = w_down.shape[1]
    return pl.pallas_call(
        hidden_kernel,
        grid=(tokens // tile,),
        in_specs=[
            pl.BlockSpec((tile, width), lambda i: (i, 0)),
            pl.BlockSpec(w_down.shape, lambda i: (0, 0)),
            pl.BlockSpec((tile, unit), lambda i: (i, 0)),
        ],
        out_specs=[
            pl.BlockSpec((tile, unit), lambda i: (i, 0)),
            pl.BlockSpec((8, unit), lambda i: (0, 0)),
        ],
        out_shape=[
            jax.ShapeDtypeStruct((tokens, unit), bf16),
            jax.ShapeDtypeStruct((8, unit), f32),
        ],
        name="hidden_backward",
        **params((2 * tokens * width * unit, 6 * tokens * width)),
    )(dy, w_down, slope)


def input_kernel(hd, du_ref, dp_ref, wu_ref, wq_ref, wk_ref, wv_ref, vec_ref, z_ref):
    da = (
        dot(dp_ref[:, :hd], wq_ref[...], 1, 1)
        + dot(dp_ref[:, hd : 2 * hd], wk_ref[...], 1, 1)
        + dot(dp_ref[:, 2 * hd :], wv_ref[...], 1, 1)
    )
    dm = dot(du_ref[...], wu_ref[...], 1, 1)
    z_ref[...] = (da * vec_ref[0:1] + dm * vec_ref[2:3]).astype(bf16)


def input_backward(du, dp, w_qu, vec, tile, seq, seqs):
    tokens, unit = du.shape
    width, hd = w_qu.shape[0], dp.shape[1] // 3
    first = unit // hd
    steps = tokens // seqs // tile
    flops = 2 * tokens // seqs * width * (unit + 3 * hd)
    return pl.pallas_call(
        partial(input_kernel, hd),
        grid=(steps,),
        in_specs=[
            pl.BlockSpec((tile, unit), lambda i: (seq * steps + i, 0)),
            pl.BlockSpec((tile, 3 * hd), lambda i: (seq * steps + i, 0)),
            pl.BlockSpec((width, unit), lambda i: (0, 0)),
        ]
        + [pl.BlockSpec((width, hd), lambda i, j=j: (0, first + j)) for j in range(3)]
        + [pl.BlockSpec(vec.shape, lambda i: (0, 0))],
        out_specs=pl.BlockSpec((tile, width), lambda i: (i, 0)),
        out_shape=jax.ShapeDtypeStruct((tokens // seqs, width), bf16),
        name="input_backward",
        **params((flops, 12 * tokens // seqs * width)),
    )(du, dp, w_qu, w_qu, w_qu, w_qu, vec)


def adam_kernel(pair, places, rate, c_ref, *refs):
    g_refs, (w_ref, m_ref, v_ref), outs = refs[:pair], refs[pair : pair + 3], refs[-4:]
    pieces = []
    for z in range(places):
        parts = [ref[z].astype(f32) for ref in g_refs]
        if pair == 2:
            swapped = c_ref[0] == 1
            parts = [jnp.where(swapped, parts[1], parts[0]), jnp.where(swapped, parts[0], parts[1])]
        pieces += parts
    grad = pieces[0] if len(pieces) == 1 else jnp.concatenate(pieces, axis=1)
    result = adamw(w_ref[...], grad, m_ref[...], v_ref[...], rate)
    for ref, value in zip(outs, result, strict=True):
        ref[...] = value


def adam_columns(lay, rate, parts, at, piece, state, start, kinds, held):
    nz, rows, _ = parts[0].shape
    pair = len(parts)
    total = state[0].shape[1]
    places = max(1, min(nz, 2048 // (pair * piece)))
    wide = places * pair * piece
    steps = nz // places
    first = start // wide

    w_spec = pl.BlockSpec((rows, wide), lambda j, z, c: (0, first + j * steps + z))
    g_spec = pl.BlockSpec((places, rows, piece), lambda j, z, c: (z, 0, at // piece + j))
    operands = list(parts) + list(state) + list(held)
    return pl.pallas_call(
        partial(adam_kernel, pair, places, rate),
        grid_spec=pltpu.PrefetchScalarGridSpec(
            num_scalar_prefetch=1,
            grid=(kinds, steps),
            in_specs=[g_spec] * pair
            + [w_spec] * 3
            + [pl.BlockSpec(memory_space=pl.ANY)] * len(held),
            out_specs=[w_spec] * 4,
        ),
        out_shape=[jax.ShapeDtypeStruct((rows, total), f32)] * 4,
        input_output_aliases={1 + pair + 3 + k: k for k in range(len(held))},
        name="adam_columns",
        **params((30 * rows * kinds * piece * HEADS, 30 * rows * kinds * piece * HEADS)),
    )(jnp.reshape(lay.c, (1,)).astype(jnp.int32), *operands)


class LineGather:
    def __init__(self, lay, own):
        self.lay = lay
        self.up = self.down = own
        self.fresh = [(own, lay.z, lambda z: True)]
        self.todo = []
        self.out = None
        self.count = own.shape[0]

    def step(self, k):
        lay, n = self.lay, self.lay.nz
        self.up = lay.hop(self.up, lambda g, c, z: (g, c, z + 1) if k - 1 <= z < n - 1 else None)
        self.down = lay.hop(self.down, lambda g, c, z: (g, c, z - 1) if 1 <= z <= n - k else None)
        self.fresh.append((self.up, lay.z - k, lambda z: z >= k))
        self.fresh.append((self.down, lay.z + k, lambda z: z + k < n))

    def cross(self, keep=0):
        lay = self.lay
        due = len(self.fresh) - keep
        now, self.fresh = self.fresh[:due], self.fresh[due:]
        for piece, where, valid in now:
            ok = jnp.logical_and(where >= 0, where < lay.nz)
            for r in range(lay.pair):
                got = piece
                if r:
                    got = lay.hop(piece, lambda g, c, z: (g, c ^ r, z) if valid(z) else None)
                for s in range(self.count):
                    slot = (r * self.count + s) * lay.nz + where
                    self.todo.append((got[s], jnp.where(ok, slot, -1)))

    @property
    def state(self):
        return (self.up, self.down, [v[0] for v in self.fresh], [v for v, _ in self.todo], self.out)

    @state.setter
    def state(self, state):
        self.up, self.down, fresh, blocks, self.out = state
        self.fresh = [(v,) + w[1:] for v, w in zip(fresh, self.fresh)]
        self.todo = [(v, w) for v, (_, w) in zip(blocks, self.todo)]

    def flush(self, keep=0):
        due = len(self.todo) - keep
        now, self.todo = self.todo[:due], self.todo[due:]
        total = self.lay.pair * self.lay.nz * self.count
        blocks, slots = [(v, 0) for v, _ in now], [w for _, w in now]
        self.out = place(blocks, slots, blocks[0][0].shape[0], total, self.out)
        return self.out


class SeqScatter:
    def __init__(self, lay, parts, count):
        _, length, width = parts[0].shape
        total = sum(p.astype(f32) for p in parts).astype(bf16)
        self.state = total.reshape(count, lay.nz, length // lay.nz, width)

    def send(self):
        self.state = lax.all_to_all(self.state, "seq", 1, 1, tiled=True)

    def result(self):
        return jnp.sum(self.state.astype(f32), axis=1)


def body(
    inputs,
    cotangent,
    attn_params,
    attn_first,
    attn_second,
    mlp_params,
    mlp_first,
    mlp_second,
    small,
    small_first,
    small_second,
):
    lay = Layout(lax.axis_size("dp"), lax.axis_size("seq"))
    groups, nz, pair = lay.groups, lay.nz, lay.pair
    count, span, width = inputs.shape
    rows = attn_params.shape[0]
    ff = mlp_params.shape[1] // 2
    hd = width // HEADS
    unit = ff // HEADS
    rot_dims = hd // 4
    score_scale = hd ** (-0.5)
    first_row = (lay.dp * nz + lay.z) * rows
    seqs, length = count * pair, span * nz
    tokens_here = seqs * length

    wide_small = jnp.pad(small, ((0, 0), (0, LANES - small.shape[1])))
    qu_sources = [(mlp_params, 0, unit)]
    qu_sources += [(attn_params, j * HEADS, hd) for j in range(3)]
    qu_sources += [(wide_small, None, LANES)]
    dn_sources = [(mlp_params, HEADS, unit)]

    def swap(sources, r):
        blocks = prepare(lay, r, sources)
        return lay.core_hop(blocks, r) if r else blocks

    def exchange(half):
        return lax.all_to_all(half, "seq", 0, 0, tiled=True).reshape(nz * rows, -1)

    class Whole:
        def __init__(self, halves, size=None, first=0):
            self.halves, self.seen, self.state = halves, set(), None
            self.size, self.first = size or halves[0].rows, first

        def flush(self):
            items = [
                (r, m, (v[0], v[1] + self.first))
                for r, half in enumerate(self.halves)
                for m, v in half.held.items()
                if (r, m) not in self.seen
            ]
            self.seen |= {(r, m) for r, m, _ in items}
            if items:
                count = len(self.halves)
                slots = [
                    (lay.g ^ m) * count + (lay.c ^ r if count > 1 else 0) for r, m, _ in items
                ]
                blocks = [v for _, _, v in items]
                self.state = place(blocks, slots, self.size, groups * count, self.state)

        def result(self):
            self.flush()
            return self.state.reshape(-1, self.state.shape[-1])

    def joined(parts, *values):
        *values, states = join(*values, [p.state for p in parts])
        for p, v in zip(parts, states):
            p.state = v
        return values

    def crossed(piece):
        return [piece] + [lay.core_hop(piece, r) for r in range(1, pair)]

    positions = jnp.arange(length, dtype=f32)
    frequency = 10000.0 ** (-(jnp.arange(rot_dims // 2, dtype=f32) * 2.0) / rot_dims)
    angles = positions[:, None] * frequency[None, :]
    cosine, sine = jnp.cos(angles), jnp.sin(angles)
    blank = jnp.zeros_like(sine)
    rest = jnp.zeros((length, LANES - rot_dims), f32)
    tables = jnp.stack(
        [
            jnp.concatenate([cosine, cosine, rest + 1.0], axis=1),
            jnp.concatenate([-sine, blank, rest], axis=1),
            jnp.concatenate([blank, sine, rest], axis=1),
        ]
    )

    first = exchange(swap(qu_sources, 0))
    rest = [swap(qu_sources, r) for r in range(1, pair)]
    w_out = attn_params[:, 3 * width :].astype(bf16)
    dn = jnp.stack([prepare(lay, r, dn_sources) for r in range(pair)], axis=1)
    first, rest, w_out, dn = join(first, rest, w_out, dn)

    qu = [GroupGather(lay, first, False)]
    w_out = lax.ppermute(w_out, AXES, lay.head_owner_perm())
    for r in range(1, pair):
        one = exchange(rest[r - 1])
        qu[-1].send(0)
        one, w_out, dn = joined(qu, one, w_out, dn)
        qu.append(GroupGather(lay, one, bool(r % 2)))
    dn = lax.all_to_all(dn, "seq", 0, 0, tiled=True)
    qu[-1].send(0)
    pieces = crossed(inputs)
    newest, dn, pieces, w_out = joined(qu, inputs, dn, pieces, w_out)

    w_qu = Whole(qu)
    newest = lay.ring(newest)
    dn = [lay.core_hop(dn[:, r], r) if r else dn[:, r] for r in range(pair)]
    dn = [v.reshape(nz * rows, unit) for v in dn]
    dn[-1] = jnp.concatenate([dn[-1], w_out.reshape(-1, unit)])
    dn = [GroupGather(lay, v, bool(r)) for r, v in enumerate(dn)]
    w_qu.flush()
    for v in qu:
        v.send(1)
    newest, pieces = joined(qu + dn + [w_qu], newest, pieces)
    for v in qu:
        v.rest(2)

    w_qkvu = w_qu.result()
    vectors = last_columns(w_qkvu)
    norm_vec = vectors[:8]
    qkv_bias = vectors[6:9].reshape(3, HEADS, hd)
    qkv_bias = lax.dynamic_index_in_dim(qkv_bias, lay.t, 1, keepdims=False).reshape(1, 3 * hd)
    up_bias = lax.dynamic_slice(vectors[9:13].reshape(-1), (lay.t * unit,), (unit,))[None]
    out_bias = vectors[4] + vectors[5]
    held = ()

    def forward_piece(pieces, steps_away, held):
        where = [(lay.z - k) % nz for k in steps_away]
        return piece_forward(
            lay, pieces, where, norm_vec, w_qkvu, qkv_bias, up_bias, tables, held
        )

    dy = LineGather(lay, cotangent)
    w_dn, w_wo = Whole(dn, nz * rows), Whole(dn[-1:], rows * width // unit, nz * rows)
    for k in range(2, nz):
        last, newest = newest, lay.ring(newest)
        if k == 2:
            GroupGather.send_first(dn)
        elif k == 3:
            for v in dn:
                v.send(1)
            w_dn.flush()
            w_wo.flush()
            dy.cross()
        next_pieces = crossed(last)
        held = forward_piece(pieces, [k - 2], held)
        newest, pieces, held = joined(dn + [w_dn, w_wo, dy], newest, next_pieces, held)
    for v in dn:
        v.rest(2)

    dy.step(1)
    last_pieces = crossed(newest)
    held = forward_piece(pieces + last_pieces, [nz - 2, nz - 1], held)
    w_down = w_dn.result()
    w_out = w_wo.result().reshape(hd, width)
    held, w_down, w_out = joined([dy], held, w_down, w_out)
    tile = min(512, length)
    flat = (tokens_here, width)
    x_flat, qkv, g, slope = (v.reshape(seqs, length, -1) for v in held)
    x_flat, g, slope = (v.reshape(tokens_here, -1) for v in (x_flat, g, slope))

    dy.cross()
    dy.step(2)
    o, lse = attn_forward(qkv, score_scale)
    o = o.reshape(tokens_here, hd)
    out_parts = {}

    def output_part(r):
        part = output_forward(g, w_down, o, w_out, tile, r, pair)
        return part.reshape(count, length, width)

    for r in range(1, pair):
        out_parts[r] = output_part(r)
    out_parts, o, lse, g = joined([dy], out_parts, o, lse, g)

    for k in range(3, nz):
        dy.step(k)
    for r in range(1, pair):
        out_parts[r] = lay.core_hop(out_parts[r], r)
    dy.cross(2 * (nz - 3))
    out_parts[0] = output_part(0)
    out_sum = SeqScatter(lay, [out_parts[r] for r in range(pair)], count)
    o, g = joined([dy, out_sum], o, g)

    def steps(*parts):
        for p in parts:
            p.step()

    def to_owners(blocks):
        return lax.all_to_all(blocks, "seq", 0, 0, tiled=True)

    def at_owner(blocks):
        parts = [blocks[:, r] for r in range(pair)]
        return [lay.core_hop(v, r) if r else v for r, v in enumerate(parts)]

    def more_rounds(parts):
        while parts[0].at < len(parts[0].bits):
            if len(parts) == pair and parts[0].keep.shape[2] < width:
                fold(parts)
            else:
                for p in parts:
                    p.fold()
            steps(*parts)

    out_sum.send()
    dy.cross()
    dy_all = dy.flush().reshape(seqs, length, width)
    dy_flat = dy_all.reshape(flat)
    du, du_sums = hidden_backward(dy_flat, w_down, slope, tile)
    dy_flat, du, du_sums = join(dy_flat, du, du_sums)

    dp, dp_sums = attn_backward(
        dy_flat.reshape(seqs, length, width), w_out, qkv, lse, tables, score_scale
    )
    dp = dp.reshape(tokens_here, 3 * hd)

    def input_part(r):
        part = input_backward(du, dp, w_qkvu, norm_vec, tile, r, pair)
        return part.reshape(count, length, width)

    z_parts = {r: input_part(r) for r in range(1, pair)}
    z_parts, du, dp, du_sums, dp_sums = join(z_parts, du, dp, du_sums, dp_sums)

    for r in range(1, pair):
        z_parts[r] = lay.core_hop(z_parts[r], r)
    z_parts[0] = input_part(0)
    up, lanes = folded_gradient(lay, x_flat, after(du, z_parts[0]), du_sums, w_qkvu, 0, 2)
    z_sum = SeqScatter(lay, [z_parts[r] for r in range(pair)], count)
    dy_flat, dp, du_sums, dp_sums, lanes = joined(
        up + [out_sum, z_sum], dy_flat, dp, du_sums, dp_sums, lanes
    )

    z_sum.send()
    upstream = cotangent.astype(f32)
    upstream_sum = jnp.sum(upstream, axis=(0, 1))[:, None]
    dp_sums = jnp.sum(dp_sums[:, 0], axis=0)
    qkv_columns = lax.dynamic_update_slice(
        jnp.zeros((width, 3), f32), dp_sums.reshape(3, hd).T, (lay.t * hd, 0)
    )
    up_columns = lax.dynamic_update_slice(jnp.zeros((ff,), f32), du_sums[0], (lay.t * unit,))
    up_columns = up_columns.reshape(ff // width, width).T
    others = jnp.concatenate(
        [jnp.zeros((width, 4), f32), upstream_sum, upstream_sum, qkv_columns, up_columns], axis=1
    )
    others = jnp.pad(others, ((0, 0), (0, LANES - others.shape[1])))
    dp_sums = jnp.broadcast_to(dp_sums[None], (8, 3 * hd))

    steps(*up)
    (dqkv,) = folded_gradient(lay, x_flat, dp, dp_sums, w_qkvu, unit, 0, (lanes, others))
    (dy_flat,) = joined(up + dqkv, dy_flat)

    more_rounds(up)
    steps(*dqkv)
    down = gradient(lay, dy_flat, g)
    outputs = (inputs.astype(f32) + out_sum.result() + out_bias).astype(bf16)
    dy_flat, outputs = joined(up + dqkv + down, dy_flat, outputs)

    more_rounds(dqkv)
    steps(*down)
    up_blocks = final_blocks(up, nz)
    out_whole = dot(o, dy_flat, 0, 0)
    out_whole = out_whole.astype(bf16).reshape(groups, rows, width)
    out_whole = jnp.stack(
        [
            lax.dynamic_index_in_dim(
                out_whole, lay.g ^ GroupScatter.member(lay, i, True), 0, keepdims=False
            )
            for i in range(groups)
        ]
    )
    wo = GroupScatter(lay, out_whole[: groups // 2], out_whole[groups // 2 :], True)
    (up_blocks,) = joined(dqkv + [wo, z_sum], up_blocks)

    mlp_state = (mlp_params, mlp_first, mlp_second)
    attn_state = (attn_params, attn_first, attn_second)
    up_blocks = to_owners(up_blocks)
    more_rounds(down)
    steps(wo)
    dqkv_blocks = final_blocks(dqkv, nz)
    normed_grad = z_sum.result()
    normed, scaling = normalize(inputs.astype(f32))
    grad_mean = jnp.mean(normed_grad, axis=-1, keepdims=True)
    grad_proj = jnp.mean(normed_grad * normed, axis=-1, keepdims=True)
    input_grad = upstream + scaling * (normed_grad - grad_mean - normed * grad_proj)
    up_blocks, dqkv_blocks, input_grad = joined(down + [wo], up_blocks, dqkv_blocks, input_grad)

    dqkv_blocks = to_owners(dqkv_blocks)
    more_rounds([wo])
    down_blocks = final_blocks(down, nz)
    up_parts = at_owner(up_blocks)
    mlp_result = adam_columns(lay, rate_mlp, up_parts, 0, unit, mlp_state, 0, 1, ())
    dqkv_blocks, down_blocks, mlp_result = joined([wo], dqkv_blocks, down_blocks, mlp_result)

    down_blocks = to_owners(down_blocks)
    out_grad = wo.result().astype(bf16)
    out_grad = lax.ppermute(out_grad, AXES, [(b, a) for a, b in lay.head_owner_perm()])
    dqkv_parts = at_owner(dqkv_blocks)
    attn_result = adam_columns(lay, rate_attention, dqkv_parts, 0, hd, attn_state, 0, 3, ())
    at = 3 * hd
    small_grad = sum(
        jnp.sum(v[:, :, at : at + small.shape[1]].astype(f32), axis=0) for v in dqkv_parts
    )
    small_result = adamw(small, small_grad, small_first, small_second, rate_vector)
    out_grad = [out_grad[None]]
    attn_result = adam_columns(
        lay, rate_attention, out_grad, 0, width, attn_state, 3 * width, 1, attn_result
    )
    down_blocks, attn_result, small_result, mlp_result = join(
        down_blocks, attn_result, small_result, mlp_result
    )

    mlp_result = adam_columns(
        lay, rate_mlp, at_owner(down_blocks), 0, unit, mlp_state, ff, 1, mlp_result
    )
    return (outputs, input_grad, *attn_result, *mlp_result, *small_result)


def solution(mesh):
    tokens, weights = P("dp", "seq", None), P(("dp", "seq"), None)
    return jax.shard_map(
        body,
        mesh=mesh,
        in_specs=(tokens,) * 2 + (weights,) * 9,
        out_specs=(tokens,) * 2 + (weights,) * 12,
        check_vma=False,
    )
```

```python
from functools import partial

import jax
import jax.numpy as jnp
from jax import lax
from jax.experimental import pallas as pl
from jax.experimental.pallas import tpu as pltpu
from jax.sharding import PartitionSpec as P

HEADS = 8
STEP = 10
AXES = ("dp", "seq")
LANES = 128
VMEM_LIMIT = 56 * 2**20

norm_eps = 1e-05
masked_value = -1e30
beta_first = 0.9
beta_second = 0.95
adam_eps = 1e-08
decay_rate = 0.01
rate_attention = 0.06
rate_mlp = 0.02
rate_vector = 0.2

f32 = jnp.float32
bf16 = jnp.bfloat16


def normalize(values):
    row_mean = jnp.mean(values, axis=-1, keepdims=True)
    centred = values - row_mean
    spread = jnp.mean(centred * centred, axis=-1, keepdims=True)
    scaling = lax.rsqrt(spread + norm_eps)
    return (centred * scaling, scaling)


def dot(left_op, right_op, left_dim=1, right_dim=0):
    return lax.dot_general(
        left_op,
        right_op,
        (((left_dim,), (right_dim,)), ((), ())),
        preferred_element_type=f32,
    )


def adamw(master, gradient, first_old, second_old, step_rate):
    first_new = beta_first * first_old + (1.0 - beta_first) * gradient
    second_new = beta_second * second_old + (1.0 - beta_second) * gradient * gradient
    first_hat = first_new / (1.0 - beta_first**STEP)
    second_hat = second_new / (1.0 - beta_second**STEP)
    updated = master - step_rate * (
        first_hat / (jnp.sqrt(second_hat) + adam_eps) + decay_rate * master
    )
    return (gradient, updated, first_new, second_new)


def params(cost=None, **kw):
    return dict(
        compiler_params=pltpu.CompilerParams(vmem_limit_bytes=VMEM_LIMIT, **kw),
        cost_estimate=cost and pl.CostEstimate(flops=cost[0] // 1000 + 1, bytes_accessed=cost[1] // 1000 + 1, transcendentals=0),
    )


class Layout:
    def __init__(self, nd, nz):
        self.nd, self.nz = nd, nz
        self.pair = HEADS // nz
        self.groups = nd // self.pair
        self.dp = lax.axis_index("dp")
        self.z = lax.axis_index("seq")
        self.g = self.dp // self.pair
        self.c = self.dp % self.pair
        self.t = self.z * self.pair + self.c

    def perm(self, target):
        pairs = []
        for dp in range(self.nd):
            for z in range(self.nz):
                goal = target(dp // self.pair, dp % self.pair, z)
                if goal is not None:
                    g, c, s = goal
                    pairs.append((dp * self.nz + z, (g * self.pair + c) * self.nz + s))
        return pairs

    def hop(self, value, target):
        return lax.ppermute(value, AXES, self.perm(target))

    def group_hop(self, value, bit):
        return self.hop(value, lambda g, c, z: (g ^ bit, c, z))

    def core_hop(self, value, r):
        return self.hop(value, lambda g, c, z: (g, c ^ r, z))

    def ring(self, value):
        return self.hop(value, lambda g, c, z: (g, c, (z + 1) % self.nz))

    def flat_hop(self, value, bit):
        return lax.ppermute(value, AXES, [(i, i ^ bit) for i in range(self.nd * self.nz)])

    def head_owner_perm(self):
        pairs = []
        for r in range(self.nd * self.nz):
            head, quarter = r // self.groups, r % self.groups
            s, c = head // self.pair, head % self.pair
            pairs.append((r, ((quarter ^ s) * self.pair + c) * self.nz + s))
        return pairs


def after(values, *deps):
    flat, tree = jax.tree.flatten((values, deps))
    return jax.tree.unflatten(tree, lax.optimization_barrier(flat))[0]


def join(*values):
    return after(values)


def bits_of(count, descending):
    bits = []
    bit = 1
    while bit < count:
        bits.append(bit)
        bit *= 2
    return bits[::-1] if descending else bits


class GroupGather:
    def __init__(self, lay, block, descending):
        self.lay = lay
        self.rows = block.shape[0]
        self.held = {0: (block, 0)}
        self.rounds = [[] for _ in bits_of(lay.groups, False)]
        known = [0]
        for bit in bits_of(lay.groups, descending):
            for m in list(known):
                self.rounds[bin(m).count("1")].append((m, bit))
                known.append(m ^ bit)

    def block(self, m):
        array, first = self.held[m]
        return array[first : first + self.rows]

    def send(self, depth):
        if depth < len(self.rounds):
            for m, bit in self.rounds[depth]:
                self.held[m ^ bit] = (self.lay.group_hop(self.block(m), bit), 0)

    @staticmethod
    def stack(halves):
        return jnp.concatenate([h.block(0) for h in halves])

    @staticmethod
    def send_first(halves, stack):
        lay = halves[0].lay
        for bit in bits_of(lay.groups, False):
            got = lay.group_hop(stack, bit)
            first = 0
            for h in halves:
                h.held[bit] = (got, first)
                first += h.rows

    @property
    def state(self):
        return {m: v for m, (v, _) in self.held.items()}

    @state.setter
    def state(self, state):
        for m, v in state.items():
            self.held[m] = (v, self.held[m][1])

    def rest(self, depth):
        while depth < len(self.rounds):
            self.send(depth)
            depth += 1
        return self.held


class GroupScatter:
    def __init__(self, lay, keep, send, descending):
        self.lay = lay
        self.keep, self.send = keep, send
        self.bits = bits_of(lay.groups, descending)
        self.at = 0

    @staticmethod
    def member(lay, index, descending):
        bits = bits_of(lay.groups, descending)
        return sum(bit for j, bit in enumerate(bits) if index >> (len(bits) - 1 - j) & 1)

    @property
    def state(self):
        return (self.keep, self.send)

    @state.setter
    def state(self, state):
        self.keep, self.send = state

    def step(self):
        if self.at < len(self.bits):
            self.send = self.lay.group_hop(self.send, self.bits[self.at])
            self.at += 1

    def fold(self):
        total = self.keep.astype(f32) + self.send.astype(f32)
        half = total.shape[0] // 2
        self.keep, self.send = total[:half], total[half:].astype(bf16)

    def result(self):
        return (self.keep.astype(f32) + self.send.astype(f32))[0]


def cast_kernel(c_ref, *refs):
    out_ref = refs[-1]
    at = 0
    for ref in refs[:-1]:
        out_ref[0, :, at : at + ref.shape[1]] = ref[...].astype(bf16)
        at += ref.shape[1]


def prepare(lay, r, sources):
    rows, pair, nz = sources[0][0].shape[0], lay.pair, lay.nz

    def spec(first, width):
        if first is None:
            return pl.BlockSpec((rows, width), lambda z, c: (0, 0))
        return pl.BlockSpec((rows, width), lambda z, c: (0, first + z * pair + (c[0] ^ r)))

    total = sum(width for _, _, width in sources)
    return pl.pallas_call(
        cast_kernel,
        grid_spec=pltpu.PrefetchScalarGridSpec(
            num_scalar_prefetch=1,
            grid=(nz,),
            in_specs=[spec(first, width) for _, first, width in sources],
            out_specs=pl.BlockSpec((1, rows, total), lambda z, c: (z, 0, 0)),
        ),
        out_shape=jax.ShapeDtypeStruct((nz, rows, total), bf16),
        name="prepare",
        **params((rows * total * nz, rows * total * nz * 6)),
    )(jnp.reshape(lay.c, (1,)).astype(jnp.int32), *[v for v, _, _ in sources])


def place_kernel(count, tile, slot_ref, *refs):
    out_ref, sems = refs[-2], refs[-1]
    here = pl.ds(pl.multiple_of(pl.program_id(0) * tile, tile), tile)

    def copy(i):
        return pltpu.make_async_copy(refs[i], out_ref.at[slot_ref[i], here], sems.at[i])

    for i in range(count):

        @pl.when(slot_ref[i] >= 0)
        def _(i=i):
            copy(i).start()

    for i in range(count):

        @pl.when(slot_ref[i] >= 0)
        def _(i=i):
            copy(i).wait()


def place(blocks, slots, rows, total, held=None):
    count = len(blocks)
    width = blocks[0][0].shape[1]
    tile = max(min(64, rows), rows // 2)
    operands = [v for v, _ in blocks] + ([] if held is None else [held])
    any_spec = pl.BlockSpec(memory_space=pl.ANY)
    return pl.pallas_call(
        partial(place_kernel, count, tile),
        grid_spec=pltpu.PrefetchScalarGridSpec(
            num_scalar_prefetch=1,
            grid=(rows // tile,),
            in_specs=[
                pl.BlockSpec(
                    (tile, width),
                    lambda i, slot, first=first, j=j: (
                        first // tile + jnp.where(slot[j] >= 0, i, 0),
                        0,
                    ),
                )
                for j, (_, first) in enumerate(blocks)
            ]
            + [any_spec] * (len(operands) - count),
            out_specs=any_spec,
            scratch_shapes=[pltpu.SemaphoreType.DMA((count,))],
        ),
        out_shape=jax.ShapeDtypeStruct((total, rows, width), blocks[0][0].dtype),
        input_output_aliases={} if held is None else {count + 1: 0},
        name="place",
        **params((count, 4 * count * rows * width)),
    )(jnp.stack([jnp.asarray(v, jnp.int32) for v in slots]), *operands)


def flip_kernel(in_ref, out_ref):
    out_ref[...] = in_ref[...].astype(f32).T


def last_columns(array):
    rows, total = array.shape
    return pl.pallas_call(
        flip_kernel,
        grid=(1,),
        in_specs=[pl.BlockSpec((rows, LANES), lambda i: (0, total // LANES - 1))],
        out_specs=pl.BlockSpec((LANES, rows), lambda i: (0, 0)),
        out_shape=jax.ShapeDtypeStruct((LANES, rows), f32),
        name="last_columns",
        **params(),
    )(array)


def block_order(lay):
    order = []
    for part in (1, 0):
        for r in range(lay.pair):
            for i in range(lay.groups // 2):
                m = GroupScatter.member(lay, part * (lay.groups // 2) + i, bool(r))
                order.append((lay.g ^ m) * lay.pair + (lay.c ^ r))
    return jnp.stack(order).astype(jnp.int32)


def write_block(half, outs, at, value):
    i = pl.program_id(0)
    for k, out in enumerate(outs):

        @pl.when(jnp.logical_and(i >= k * half, i < (k + 1) * half))
        def _(out=out):
            out[0, :, at : at + value.shape[1]] = value


def gradient_kernel(half, block_ref, left_ref, right_ref, *outs):
    write_block(half, outs, 0, dot(left_ref[...], right_ref[...], 0, 0).astype(bf16))


def folded_kernel(half, first, gain, rides, block_ref, x_ref, right_ref, sums_ref, w_ref, small_ref, *refs):
    others, outs = (refs[:2], refs[2:]) if rides else ((), refs[:-1])
    vec = small_ref[...].astype(f32)
    raw = dot(x_ref[...], right_ref[...], 0, 0)
    sums = sums_ref[0:1]
    grad = raw * vec[:, gain : gain + 1] + sums * vec[:, gain + 1 : gain + 2]
    write_block(half, outs, 0, grad.astype(bf16))
    w = w_ref[:, first : first + raw.shape[1]].astype(f32)
    lane = lax.broadcasted_iota(jnp.int32, vec.shape, 1)
    moment = jnp.sum(w * raw, axis=1, keepdims=True)
    plain = jnp.sum(w * sums, axis=1, keepdims=True)
    lanes = jnp.where(lane == gain, moment, jnp.where(lane == gain + 1, plain, 0.0))
    if rides:
        lanes = lanes + others[0][...] + others[1][...]
        write_block(half, outs, raw.shape[1], lanes.astype(bf16))
    else:
        refs[-1][...] = lanes


def columns_kernel(unit, hd, t_ref, dy_ref, du_ref, *refs):
    out_ref = refs[-1]
    width = out_ref.shape[0]
    t = t_ref[0]
    place = lax.broadcasted_iota(jnp.int32, (1, width), 1)
    dy = jnp.sum(dy_ref[...].astype(f32), axis=0, keepdims=True)
    dp = sum(jnp.sum(ref[:, 0], axis=0, keepdims=True) for ref in refs[:-1])
    blank = jnp.zeros((1, width), f32)
    rows = [blank] * 4 + [dy, dy]
    for j in range(3):
        head = jnp.concatenate([dp[:, j * hd : (j + 1) * hd]] * (width // hd), axis=1)
        rows.append(jnp.where(place // hd == t, head, 0.0))
    share = width // unit
    units = jnp.concatenate([du_ref[0:1]] * share, axis=1)
    for k in range(HEADS // share):
        rows.append(jnp.where(place // unit + k * share == t, units, 0.0))
    rows += [blank] * (LANES - len(rows))
    out_ref[...] = jnp.concatenate(rows).T


def plain_columns(lay, dy, du_sums, dp_sums, unit, hd):
    tokens, width = dy.shape

    def whole(v):
        return pl.BlockSpec(v.shape, lambda i, t: (0,) * v.ndim)

    return pl.pallas_call(
        partial(columns_kernel, unit, hd),
        grid_spec=pltpu.PrefetchScalarGridSpec(
            num_scalar_prefetch=1,
            grid=(1,),
            in_specs=[whole(v) for v in (dy, du_sums, *dp_sums)],
            out_specs=pl.BlockSpec((width, LANES), lambda i, t: (0, 0)),
        ),
        out_shape=jax.ShapeDtypeStruct((width, LANES), f32),
        name="plain_columns",
        **params((tokens * width, 4 * tokens * width)),
    )(jnp.reshape(lay.t, (1,)).astype(jnp.int32), dy, du_sums, *dp_sums)


def gradient_call(lay, kernel, left, rights, by_rows, n, more=()):
    tokens, width = left.shape
    pair, half = lay.pair, lay.groups // 2
    rows = width // (lay.groups * pair)
    outs = 2 * pair

    def out_map(k):
        return lambda i, block: (jnp.clip(i - k * half, 0, half - 1), 0, 0)

    def row_map(column):
        return lambda i, block: (block[i], column)

    values = pl.pallas_call(
        partial(kernel, half),
        grid_spec=pltpu.PrefetchScalarGridSpec(
            num_scalar_prefetch=1,
            grid=(outs * half,),
            in_specs=[pl.BlockSpec((tokens, rows), lambda i, block: (0, block[i]))]
            + [pl.BlockSpec(v.shape, lambda i, block: (0, 0)) for v in rights]
            + [pl.BlockSpec((rows, size), row_map(column)) for _, size, column in by_rows],
            out_specs=[pl.BlockSpec((1, rows, n), out_map(k)) for k in range(outs)]
            + [pl.BlockSpec((rows, size), row_map(0)) for size in more],
        ),
        out_shape=[jax.ShapeDtypeStruct((half, rows, n), bf16)] * outs
        + [jax.ShapeDtypeStruct((width, size), f32) for size in more],
        name="gradient",
        **params((2 * tokens * width * n, 2 * (tokens * width + tokens * n + width * n))),
    )(block_order(lay), left, *rights, *[v for v, _, _ in by_rows])
    parts = [GroupScatter(lay, values[pair + r], values[r], bool(r)) for r in range(pair)]
    return (parts, *values[outs:])


def gradient(lay, left, right):
    return gradient_call(lay, gradient_kernel, left, [right], [], right.shape[1])[0]


def folded_gradient(lay, x, right, sums, w_qu, first, gain, others=()):
    total = w_qu.shape[1]
    by_rows = [(w_qu, total, 0), (w_qu, LANES, total // LANES - 1)]
    by_rows += [(v, LANES, 0) for v in others]
    rides = len(others) > 0

    def call(half, *refs):
        folded_kernel(half, first, gain, rides, *refs)

    n = right.shape[1] + (LANES if rides else 0)
    return gradient_call(lay, call, x, [right, sums], by_rows, n, () if rides else (LANES,))


def fold_kernel(*refs):
    count = len(refs) // 4
    for p in range(count):
        keep, got, next_keep, next_send = refs[p], refs[count + p], refs[2 * count + p], refs[3 * count + p]
        half = next_keep.shape[0]
        total = keep[...].astype(f32) + got[...].astype(f32)
        next_keep[...] = total[:half]
        next_send[...] = total[half:].astype(bf16)


def fold(parts):
    held, rows, n = parts[0].keep.shape
    half = held // 2
    tile = min(64, rows)
    full = pl.BlockSpec((held, tile, n), lambda i: (0, i, 0))
    part = pl.BlockSpec((half, tile, n), lambda i: (0, i, 0))
    count = len(parts)
    values = pl.pallas_call(
        fold_kernel,
        grid=(rows // tile,),
        in_specs=[full] * (2 * count),
        out_specs=[part] * (2 * count),
        out_shape=[jax.ShapeDtypeStruct((half, rows, n), f32)] * count
        + [jax.ShapeDtypeStruct((half, rows, n), bf16)] * count,
        name="fold",
        **params((held * rows * n, 8 * held * rows * n)),
    )(*[p.keep for p in parts], *[p.send for p in parts])
    for k, p in enumerate(parts):
        p.keep, p.send = values[k], values[count + k]


def blocks_kernel(count, *refs):
    out_ref = refs[-1]
    for p in range(count):
        out_ref[0, p] = (refs[p][0].astype(f32) + refs[count + p][0].astype(f32)).astype(bf16)


def final_blocks(parts, nz):
    _, total, n = parts[0].keep.shape
    rows, count = total // nz, len(parts)
    return pl.pallas_call(
        partial(blocks_kernel, count),
        grid=(nz,),
        in_specs=[pl.BlockSpec((1, rows, n), lambda i: (0, i, 0))] * (2 * count),
        out_specs=pl.BlockSpec((1, count, rows, n), lambda i: (i, 0, 0, 0)),
        out_shape=jax.ShapeDtypeStruct((nz, count, rows, n), bf16),
        name="final_blocks",
        **params((count * total * n, 8 * count * total * n)),
    )(*[p.keep for p in parts], *[p.send for p in parts])


def chunk_kernel(count, ways, slot_ref, *refs):
    for k in range(ways):

        @pl.when(slot_ref[k] >= 0)
        def _(k=k):
            total = sum(refs[k * count + p][...].astype(f32) for p in range(count))
            out = refs[-ways + k]
            out[...] = total.astype(out.dtype)


def chunk_sums(parts, slots, received):
    count, _, span, width = parts[0].shape
    tile = min(span, 128)
    ways = len(slots)

    def whole(k):
        return lambda i, slot: (0, jnp.where(slot[k] >= 0, i, 0), 0)

    def part(k):
        return lambda i, slot: (0, jnp.maximum(slot[k], 0), jnp.where(slot[k] >= 0, i, 0), 0)

    in_specs, operands = [], []
    for k in range(ways):
        for p in parts:
            in_specs.append(pl.BlockSpec((count, None, tile, width), part(k)))
            operands.append(p)
        if received:
            in_specs.append(pl.BlockSpec((count, tile, width), whole(k)))
            operands.append(received[k])
    shape = jax.ShapeDtypeStruct((count, span, width), bf16)
    return pl.pallas_call(
        partial(chunk_kernel, len(operands) // ways, ways),
        grid_spec=pltpu.PrefetchScalarGridSpec(
            num_scalar_prefetch=1,
            grid=(span // tile,),
            in_specs=in_specs,
            out_specs=[pl.BlockSpec((count, tile, width), whole(k)) for k in range(ways)],
        ),
        out_shape=[shape] * ways,
        name="chunk_sums",
        **params((8 * count * span * width, 16 * count * span * width)),
    )(jnp.stack(slots).astype(jnp.int32), *operands)


def turn(values, cosine, low_sine, high_sine, quarter):
    head = values[:, :LANES]
    turned = (
        head * cosine
        + pltpu.roll(head, LANES - quarter, 1) * low_sine
        + pltpu.roll(head, quarter, 1) * high_sine
    )
    return jnp.concatenate([turned, values[:, LANES:]], axis=1)


def piece_kernel(pair, places, quarter, pos_ref, *refs):
    x_refs, refs = refs[: pair * places], refs[pair * places :]
    for p in range(places):

        @pl.when(pl.program_id(1) == p)
        def _(p=p):
            piece_rows(pair, quarter, x_refs[p * pair : (p + 1) * pair], refs)


def piece_rows(pair, quarter, x_refs, refs):
    vec_ref, w_ref, qkv_bias_ref, up_bias_ref, tab_ref = refs[:5]
    x_out, qkv_out, g_out, slope_out = refs[-4:]
    tile = x_refs[0].shape[1]
    unit, wide = g_out.shape[-1], qkv_out.shape[-1]
    hd = wide // 3
    x = jnp.concatenate([ref[0].astype(f32) for ref in x_refs])
    normed, _ = normalize(x)
    a = (normed * vec_ref[0:1] + vec_ref[1:2]).astype(bf16)
    m = (normed * vec_ref[2:3] + vec_ref[3:4]).astype(bf16)
    cosine, low_sine, high_sine = (jnp.concatenate([tab_ref[k]] * pair) for k in range(3))

    def put(out, at, value):
        value = value.astype(bf16)
        for r in range(pair):
            out[r, 0, 0, :, at : at + value.shape[1]] = value[r * tile : (r + 1) * tile]

    put(x_out, 0, normed)
    for j in range(3):
        part = dot(a, w_ref[:, unit + j * hd : unit + (j + 1) * hd])
        part = part + qkv_bias_ref[0:1, j * hd : (j + 1) * hd]
        put(qkv_out, j * hd, turn(part, cosine, low_sine, high_sine, quarter) if j < 2 else part)
    u = dot(m, w_ref[:, :unit]) + up_bias_ref[0:1]
    half = 0.5 * (1.0 + lax.erf(u * (0.5**0.5)))
    put(g_out, 0, u * half)
    put(slope_out, 0, half + u * (jnp.exp(-0.5 * u * u) * 0.3989422804014327))


def piece_forward(lay, pieces, where, vec, w_qu, qkv_bias, up_bias, tables, held):
    count, span, width = pieces[0].shape
    pair, nz, places = lay.pair, lay.nz, len(where)
    unit, wide = up_bias.shape[1], qkv_bias.shape[1]
    tile = min(span, 128)
    steps = span // tile

    def out(n):
        return (
            jax.ShapeDtypeStruct((pair, count, nz, span, n), bf16),
            pl.BlockSpec((pair, 1, 1, tile, n), lambda i, p, j, pos: (0, i, pos[p], j, 0)),
        )

    def whole(v):
        return pl.BlockSpec(v.shape, lambda i, p, j, pos: (0,) * v.ndim)

    def row_map(q):
        return lambda i, p, j, pos: (i, jnp.where(p == q, j, jnp.where(p < q, 0, steps - 1)), 0)

    outs = [out(n) for n in (width, wide, unit, unit)]
    in_specs = [pl.BlockSpec((1, tile, width), row_map(q)) for q in range(places) for _ in range(pair)]
    in_specs += [pl.BlockSpec((8, width), lambda i, p, j, pos: (0, 0))]
    in_specs += [whole(v) for v in (w_qu, qkv_bias, up_bias)]
    in_specs += [pl.BlockSpec((3, tile, LANES), lambda i, p, j, pos: (0, pos[p] * steps + j, 0))]
    in_specs += [pl.BlockSpec(memory_space=pl.ANY)] * len(held)
    tokens = pair * places * count * span
    return pl.pallas_call(
        partial(piece_kernel, pair, places, wide // 24),
        grid_spec=pltpu.PrefetchScalarGridSpec(
            num_scalar_prefetch=1,
            grid=(count, places, steps),
            in_specs=in_specs,
            out_specs=[o[1] for o in outs],
        ),
        out_shape=[o[0] for o in outs],
        input_output_aliases={pair * places + 6 + k: k for k in range(len(held))},
        name="piece_forward",
        **params((2 * tokens * width * (unit + wide), 12 * tokens * width)),
    )(
        jnp.stack(where).astype(jnp.int32),
        *pieces,
        vec,
        w_qu,
        qkv_bias,
        up_bias,
        tables,
        *held,
    )


def attn_fwd_kernel(scale, tile, qkv_ref, o_ref, lse_ref):
    length, hd = o_ref.shape[1:]
    for i in range(length // tile):
        end = (i + 1) * tile
        q_i = qkv_ref[0, i * tile : end, :hd]
        scores = dot(q_i, qkv_ref[0, :end, hd : 2 * hd], 1, 1) * scale
        row = lax.broadcasted_iota(jnp.int32, scores.shape, 0) + i * tile
        col = lax.broadcasted_iota(jnp.int32, scores.shape, 1)
        scores = jnp.where(col <= row, scores, masked_value)
        row_max = jnp.max(scores, axis=1, keepdims=True)
        terms = jnp.exp(scores - row_max)
        row_sum = jnp.sum(terms, axis=1, keepdims=True)
        probs = (terms / row_sum).astype(bf16)
        o_ref[0, i * tile : end] = dot(probs, qkv_ref[0, :end, 2 * hd :]).astype(bf16)
        lse_ref[0, i * tile : end] = jnp.broadcast_to(row_max + jnp.log(row_sum), (tile, LANES))


def attn_forward(qkv, scale):
    seqs, length, wide = qkv.shape
    hd = wide // 3
    return pl.pallas_call(
        partial(attn_fwd_kernel, scale, min(256, length)),
        grid=(seqs,),
        in_specs=[pl.BlockSpec((1, length, wide), lambda s: (s, 0, 0))],
        out_specs=[
            pl.BlockSpec((1, length, hd), lambda s: (s, 0, 0)),
            pl.BlockSpec((1, length, LANES), lambda s: (s, 0, 0)),
        ],
        out_shape=[
            jax.ShapeDtypeStruct((seqs, length, hd), bf16),
            jax.ShapeDtypeStruct((seqs, length, LANES), f32),
        ],
        name="attn_forward",
        **params((4 * seqs * length * length * hd, 8 * seqs * length * wide)),
    )(qkv)


def attn_bwd_kernel(quarter, scale, tile, dy_ref, wo_ref, qkv_ref, lse_ref, tab_ref, *refs):
    dp_ref, sum_ref, do_s, dk_s, dv_s = refs[-5:]
    length = dy_ref.shape[1]
    hd = wo_ref.shape[0]
    cosine, low_sine, high_sine = tab_ref[0], -tab_ref[1], -tab_ref[2]
    do_s[...] = dot(dy_ref[0], wo_ref[...], 1, 1).astype(bf16)
    steps = length // tile
    for i in reversed(range(steps)):
        end = (i + 1) * tile
        q_i = qkv_ref[0, i * tile : end, :hd]
        k = qkv_ref[0, :end, hd : 2 * hd]
        do_i = do_s[i * tile : end]
        scores = dot(q_i, k, 1, 1) * scale
        row = lax.broadcasted_iota(jnp.int32, scores.shape, 0) + i * tile
        col = lax.broadcasted_iota(jnp.int32, scores.shape, 1)
        probs = jnp.where(col <= row, jnp.exp(scores - lse_ref[0, i * tile : end, 0:1]), 0.0)
        probs_grad = dot(do_i, qkv_ref[0, :end, 2 * hd :], 1, 1)
        row_dot = jnp.sum(probs * probs_grad, axis=1, keepdims=True)
        score_grad = (probs * (probs_grad - row_dot)).astype(bf16)
        dq = dot(score_grad, k) * scale
        dp_ref[0, i * tile : end, :hd] = turn(
            dq,
            cosine[i * tile : end],
            low_sine[i * tile : end],
            high_sine[i * tile : end],
            quarter,
        ).astype(bf16)
        dk = dot(score_grad, q_i, 0, 0)
        dv = dot(probs.astype(bf16), do_i, 0, 0)
        if i == steps - 1:
            dk_s[...] = dk
            dv_s[...] = dv
        else:
            dk_s[:end] += dk
            dv_s[:end] += dv
    dp_ref[0, :, hd : 2 * hd] = turn(
        dk_s[...] * scale, cosine, low_sine, high_sine, quarter
    ).astype(bf16)
    dp_ref[0, :, 2 * hd :] = dv_s[...].astype(bf16)
    total = jnp.sum(dp_ref[0].astype(f32), axis=0, keepdims=True)
    sum_ref[0] = jnp.broadcast_to(total, sum_ref.shape[1:])


def attn_backward(dy, w_out, qkv, lse, tables, scale, part, parts, held):
    seqs, length, width = dy.shape
    hd = w_out.shape[0]
    share = seqs // parts
    first = part * share
    flops = 2 * share * length * (hd * width + 5 * length * hd)

    def row_map(s):
        return (first + s, 0, 0)

    return pl.pallas_call(
        partial(attn_bwd_kernel, hd // 8, scale, min(256, length)),
        grid=(share,),
        in_specs=[
            pl.BlockSpec((1, length, width), row_map),
            pl.BlockSpec(w_out.shape, lambda s: (0, 0)),
            pl.BlockSpec((1, length, 3 * hd), row_map),
            pl.BlockSpec((1, length, LANES), row_map),
            pl.BlockSpec(tables.shape, lambda s: (0, 0, 0)),
        ]
        + [pl.BlockSpec(memory_space=pl.ANY)] * len(held),
        out_specs=[
            pl.BlockSpec((1, length, 3 * hd), row_map),
            pl.BlockSpec((1, 8, 3 * hd), lambda s: (s, 0, 0)),
        ],
        out_shape=[
            jax.ShapeDtypeStruct((seqs, length, 3 * hd), bf16),
            jax.ShapeDtypeStruct((share, 8, 3 * hd), f32),
        ],
        input_output_aliases={5 + k: k for k in range(len(held))},
        scratch_shapes=[
            pltpu.VMEM((length, hd), bf16),
            pltpu.VMEM((length, hd), f32),
            pltpu.VMEM((length, hd), f32),
        ],
        name="attn_backward",
        **params((flops, 8 * share * length * width)),
    )(dy, w_out, qkv, lse, tables, *held)


def write_chunk(outs, more, total):
    for ref in more:
        total = total + ref[0].astype(f32)
    total = total.astype(bf16)
    if len(outs) == 1:
        outs[0][0] = total
    else:
        for k, out in enumerate(outs):

            @pl.when(pl.program_id(0) == k)
            def _(out=out):
                out[0] = total


def chunk_outputs(order_len, span, width, separate):
    if separate:
        specs = [pl.BlockSpec((1, span, width), lambda i, order: (0, 0, 0))] * order_len
        return specs, [jax.ShapeDtypeStruct((1, span, width), bf16)] * order_len
    specs = [pl.BlockSpec((1, span, width), lambda i, order: (i, 0, 0))]
    return specs, [jax.ShapeDtypeStruct((order_len, span, width), bf16)]


def output_kernel(count, order_ref, g_ref, wd_ref, o_ref, wo_ref, *refs):
    total = dot(g_ref[...], wd_ref[...], 1, 1) + dot(o_ref[...], wo_ref[...])
    write_chunk(refs[count:], refs[:count], total)


def output_forward(g, w_down, o, w_out, span, order, first, more=(), separate=False):
    unit, width, hd = g.shape[1], w_down.shape[0], o.shape[1]
    steps = order.shape[0]
    out_specs, out_shape = chunk_outputs(steps, span, width, separate)
    return pl.pallas_call(
        partial(output_kernel, len(more)),
        grid_spec=pltpu.PrefetchScalarGridSpec(
            num_scalar_prefetch=1,
            grid=(steps,),
            in_specs=[
                pl.BlockSpec((span, unit), lambda i, order: (first + order[i], 0)),
                pl.BlockSpec(w_down.shape, lambda i, order: (0, 0)),
                pl.BlockSpec((span, hd), lambda i, order: (first + order[i], 0)),
                pl.BlockSpec(w_out.shape, lambda i, order: (0, 0)),
            ]
            + [pl.BlockSpec((1, span, width), lambda i, order: (i, 0, 0))] * len(more),
            out_specs=out_specs,
        ),
        out_shape=out_shape,
        name="output_forward",
        **params((2 * steps * span * width * (unit + hd), 8 * steps * span * width)),
    )(order, g, w_down, o, w_out, *more)


def hidden_kernel(dy_ref, wd_ref, slope_ref, du_ref, sum_ref):
    dg = dot(dy_ref[...], wd_ref[...])
    du_ref[...] = (dg * slope_ref[...].astype(f32)).astype(bf16)
    total = jnp.sum(du_ref[...].astype(f32), axis=0, keepdims=True)
    total = jnp.broadcast_to(total, sum_ref.shape)

    @pl.when(pl.program_id(0) == 0)
    def _():
        sum_ref[...] = total

    @pl.when(pl.program_id(0) > 0)
    def _():
        sum_ref[...] += total


def hidden_backward(dy, w_down, slope, tile):
    tokens, width = dy.shape
    unit = w_down.shape[1]
    return pl.pallas_call(
        hidden_kernel,
        grid=(tokens // tile,),
        in_specs=[
            pl.BlockSpec((tile, width), lambda i: (i, 0)),
            pl.BlockSpec(w_down.shape, lambda i: (0, 0)),
            pl.BlockSpec((tile, unit), lambda i: (i, 0)),
        ],
        out_specs=[
            pl.BlockSpec((tile, unit), lambda i: (i, 0)),
            pl.BlockSpec((8, unit), lambda i: (0, 0)),
        ],
        out_shape=[
            jax.ShapeDtypeStruct((tokens, unit), bf16),
            jax.ShapeDtypeStruct((8, unit), f32),
        ],
        name="hidden_backward",
        **params((2 * tokens * width * unit, 6 * tokens * width)),
    )(dy, w_down, slope)


def input_kernel(count, hd, order_ref, du_ref, dp_ref, wu_ref, wq_ref, wk_ref, wv_ref, vec_ref, *refs):
    da = (
        dot(dp_ref[:, :hd], wq_ref[...], 1, 1)
        + dot(dp_ref[:, hd : 2 * hd], wk_ref[...], 1, 1)
        + dot(dp_ref[:, 2 * hd :], wv_ref[...], 1, 1)
    )
    dm = dot(du_ref[...], wu_ref[...], 1, 1)
    write_chunk(refs[count:], refs[:count], da * vec_ref[0:1] + dm * vec_ref[2:3])


def input_backward(du, dp, w_qu, vec, span, order, first, more=(), separate=False):
    unit, width, hd = du.shape[1], w_qu.shape[0], dp.shape[1] // 3
    columns = unit // hd
    steps = order.shape[0]
    out_specs, out_shape = chunk_outputs(steps, span, width, separate)
    return pl.pallas_call(
        partial(input_kernel, len(more), hd),
        grid_spec=pltpu.PrefetchScalarGridSpec(
            num_scalar_prefetch=1,
            grid=(steps,),
            in_specs=[
                pl.BlockSpec((span, unit), lambda i, order: (first + order[i], 0)),
                pl.BlockSpec((span, 3 * hd), lambda i, order: (first + order[i], 0)),
                pl.BlockSpec((width, unit), lambda i, order: (0, 0)),
            ]
            + [pl.BlockSpec((width, hd), lambda i, order, j=j: (0, columns + j)) for j in range(3)]
            + [pl.BlockSpec((8, width), lambda i, order: (0, 0))]
            + [pl.BlockSpec((1, span, width), lambda i, order: (i, 0, 0))] * len(more),
            out_specs=out_specs,
        ),
        out_shape=out_shape,
        name="input_backward",
        **params((2 * steps * span * width * (unit + 3 * hd), 12 * steps * span * width)),
    )(order, du, dp, w_qu, w_qu, w_qu, w_qu, vec, *more)


def adam_kernel(pair, places, rate, c_ref, *refs):
    g_refs, (w_ref, m_ref, v_ref), outs = refs[:pair], refs[pair : pair + 3], refs[-4:]
    pieces = []
    for z in range(places):
        parts = [ref[z].astype(f32) for ref in g_refs]
        if pair == 2:
            swapped = c_ref[0] == 1
            parts = [jnp.where(swapped, parts[1], parts[0]), jnp.where(swapped, parts[0], parts[1])]
        pieces += parts
    grad = pieces[0] if len(pieces) == 1 else jnp.concatenate(pieces, axis=1)
    result = adamw(w_ref[...], grad, m_ref[...], v_ref[...], rate)
    for ref, value in zip(outs, result, strict=True):
        ref[...] = value


def adam_columns(lay, rate, parts, at, piece, state, start, kinds, held):
    nz, rows, _ = parts[0].shape
    pair = len(parts)
    total = state[0].shape[1]
    places = max(1, min(nz, 2048 // (pair * piece)))
    wide = places * pair * piece
    steps = nz // places
    first = start // wide

    w_spec = pl.BlockSpec((rows, wide), lambda j, z, c: (0, first + j * steps + z))
    g_spec = pl.BlockSpec((places, rows, piece), lambda j, z, c: (z, 0, at // piece + j))
    operands = list(parts) + list(state) + list(held)
    return pl.pallas_call(
        partial(adam_kernel, pair, places, rate),
        grid_spec=pltpu.PrefetchScalarGridSpec(
            num_scalar_prefetch=1,
            grid=(kinds, steps),
            in_specs=[g_spec] * pair
            + [w_spec] * 3
            + [pl.BlockSpec(memory_space=pl.ANY)] * len(held),
            out_specs=[w_spec] * 4,
        ),
        out_shape=[jax.ShapeDtypeStruct((rows, total), f32)] * 4,
        input_output_aliases={1 + pair + 3 + k: k for k in range(len(held))},
        name="adam_columns",
        **params((30 * rows * kinds * piece * HEADS, 30 * rows * kinds * piece * HEADS)),
    )(jnp.reshape(lay.c, (1,)).astype(jnp.int32), *operands)


class SeqGather:
    def __init__(self, lay, own):
        self.lay = lay
        self.rounds, self.at = lay.nz - 1, 0
        self.newest = own
        self.places, self.fresh = [lay.z], [own]

    def step(self):
        self.at += 1
        self.newest = self.lay.ring(self.newest)
        self.fresh.append(self.newest)
        self.places.append((self.lay.z - self.at) % self.lay.nz)

    def take(self):
        items = list(zip(self.fresh, self.places))
        self.fresh, self.places = [], []
        return items

    @property
    def state(self):
        return (self.newest, self.fresh)

    @state.setter
    def state(self, state):
        self.newest, self.fresh = state


class TokenBuffer:
    def __init__(self, lay):
        self.lay, self.todo, self.out = lay, [], None

    def add(self, items):
        for pieces, where in items:
            for r, piece in enumerate(pieces):
                for s in range(piece.shape[0]):
                    self.todo.append((piece[s], (r * piece.shape[0] + s) * self.lay.nz + where))

    def flush(self, count):
        blocks, slots = [(v, 0) for v, _ in self.todo], [w for _, w in self.todo]
        total = self.lay.pair * self.lay.nz * count
        self.out = place(blocks, slots, blocks[0][0].shape[0], total, self.out)
        self.todo = []
        return self.out

    @property
    def state(self):
        return ([v for v, _ in self.todo], self.out)

    @state.setter
    def state(self, state):
        blocks, self.out = state
        self.todo = [(v, w) for v, (_, w) in zip(blocks, self.todo)]


class SeqScatter:
    def __init__(self, lay):
        self.lay = lay
        self.four = lay.nz == 4
        if self.four:
            roles = [[3, 2, 1, 0], [0, 2, 3, 1], [3, 1, 0, 2], [0, 1, 2, 3]]
        else:
            roles = [list(range(lay.nz))] * lay.nz
        self.order = jnp.array(roles, jnp.int32)[lay.z]

    def load(self, chunks):
        self.state = list(chunks)

    def move(self, value, targets):
        return self.lay.hop(value, lambda g, c, z: (g, c, targets[z]) if z in targets else None)

    def send(self):
        if not self.four:
            self.state = [lax.all_to_all(self.state[0], "seq", 0, 0, tiled=True)]
            return
        near, far, last, own = self.state
        near = self.move(near, {0: 1, 3: 2, 2: 3, 1: 0})
        across = self.move(far, {0: 2, 3: 1})
        beside = self.move(far, {1: 2, 2: 1})
        self.state = [near, across, beside, last, own]

    def finish(self):
        if not self.four:
            return
        near, across, beside, last, own = self.state
        inner = jnp.logical_and(self.lay.z > 0, self.lay.z < 3)
        passed = jnp.where(inner, last.astype(f32) + near.astype(f32), last.astype(f32)).astype(bf16)
        came = self.move(passed, {1: 3, 2: 0, 0: 1, 3: 2})
        self.state = [near, across, beside, came, own]

    def result(self):
        if not self.four:
            return jnp.sum(self.state[0].astype(f32), axis=0)
        near, across, beside, came, own = (v[0].astype(f32) for v in self.state)
        inner = jnp.logical_and(self.lay.z > 0, self.lay.z < 3)
        return own + came + jnp.where(inner, across + beside, near)


def body(
    inputs,
    cotangent,
    attn_params,
    attn_first,
    attn_second,
    mlp_params,
    mlp_first,
    mlp_second,
    small,
    small_first,
    small_second,
):
    lay = Layout(lax.axis_size("dp"), lax.axis_size("seq"))
    groups, nz, pair = lay.groups, lay.nz, lay.pair
    count, span, width = inputs.shape
    rows = attn_params.shape[0]
    ff = mlp_params.shape[1] // 2
    hd = width // HEADS
    unit = ff // HEADS
    rot_dims = hd // 4
    score_scale = hd ** (-0.5)
    first_row = (lay.dp * nz + lay.z) * rows
    seqs, length = count * pair, span * nz
    tokens_here = seqs * length

    wide_small = jnp.pad(small, ((0, 0), (0, LANES - small.shape[1])))
    qu_sources = [(mlp_params, 0, unit)]
    qu_sources += [(attn_params, j * HEADS, hd) for j in range(3)]
    qu_sources += [(wide_small, None, LANES)]
    dn_sources = [(mlp_params, HEADS, unit)]

    def swap(sources, r):
        blocks = prepare(lay, r, sources)
        return lay.core_hop(blocks, r) if r else blocks

    def exchange(half):
        return lax.all_to_all(half, "seq", 0, 0, tiled=True).reshape(nz * rows, -1)

    class Whole:
        def __init__(self, halves, size=None, first=0, turn=0):
            self.halves, self.seen, self.state = halves, set(), None
            self.size, self.first, self.turn = size or halves[0].rows, first, turn

        def flush(self):
            items = [
                (r, m, (v[0], v[1] + self.first))
                for r, half in enumerate(self.halves)
                for m, v in half.held.items()
                if (r, m) not in self.seen
            ]
            self.seen |= {(r, m) for r, m, _ in items}
            if items:
                count = len(self.halves)
                slots = [
                    (lay.g ^ m ^ self.turn) * count + (lay.c ^ r if count > 1 else 0)
                    for r, m, _ in items
                ]
                blocks = [v for _, _, v in items]
                self.state = place(blocks, slots, self.size, groups * count, self.state)

        def result(self):
            self.flush()
            return self.state.reshape(-1, self.state.shape[-1])

    def joined(parts, *values):
        *values, states = join(*values, [p.state for p in parts])
        for p, v in zip(parts, states):
            p.state = v
        return values

    def crossed(piece):
        return [piece] + [lay.core_hop(piece, r) for r in range(1, pair)]

    positions = jnp.arange(length, dtype=f32)
    frequency = 10000.0 ** (-(jnp.arange(rot_dims // 2, dtype=f32) * 2.0) / rot_dims)
    angles = positions[:, None] * frequency[None, :]
    cosine, sine = jnp.cos(angles), jnp.sin(angles)
    blank = jnp.zeros_like(sine)
    rest = jnp.zeros((length, LANES - rot_dims), f32)
    tables = jnp.stack(
        [
            jnp.concatenate([cosine, cosine, rest + 1.0], axis=1),
            jnp.concatenate([-sine, blank, rest], axis=1),
            jnp.concatenate([blank, sine, rest], axis=1),
        ]
    )

    first = exchange(swap(qu_sources, 0))
    rest = [swap(qu_sources, r) for r in range(1, pair)]
    w_out = attn_params[:, 3 * width :].astype(bf16)
    dn = jnp.stack([prepare(lay, r, dn_sources) for r in range(pair)], axis=1)
    w_out = lax.ppermute(w_out, AXES, lay.head_owner_perm())
    first, rest, w_out, dn, tables = join(first, rest, w_out, dn, tables)

    qu = [GroupGather(lay, first, False)]
    for r in range(1, pair):
        one = exchange(rest[r - 1])
        qu[-1].send(0)
        one, w_out, dn = joined(qu, one, w_out, dn)
        qu.append(GroupGather(lay, one, bool(r % 2)))
    dn = lax.all_to_all(dn, "seq", 0, 0, tiled=True)
    qu[-1].send(0)
    xs, dy, dy_buffer = SeqGather(lay, inputs), SeqGather(lay, cotangent), TokenBuffer(lay)

    def crossing(items):
        return [(crossed(v), place) for v, place in items]

    (own,) = crossing(xs.take())
    own_pieces, dn, w_out = joined(qu + [xs], own[0], dn, w_out)
    ready = [(own_pieces, own[1])]

    w_qu = Whole(qu)
    xs.step()
    dn = [lay.core_hop(dn[:, r], r) if r else dn[:, r] for r in range(pair)]
    dn = [v.reshape(nz * rows, unit) for v in dn]
    dn[-1] = jnp.concatenate([dn[-1], w_out.reshape(-1, unit)])
    dn = [GroupGather(lay, v, bool(r)) for r, v in enumerate(dn)]
    w_qu.flush()
    for v in qu:
        v.send(1)
    (dn_stack,) = joined(qu + dn + [w_qu, xs], GroupGather.stack(dn))
    for v in qu:
        v.rest(2)

    w_qkvu = w_qu.result()
    vectors = last_columns(w_qkvu)
    norm_vec = vectors
    qkv_bias = vectors[6:9].reshape(3, HEADS, hd)
    qkv_bias = lax.dynamic_index_in_dim(qkv_bias, lay.t, 1, keepdims=False).reshape(1, 3 * hd)
    up_bias = lax.dynamic_slice(vectors[9:13].reshape(-1), (lay.t * unit,), (unit,))[None]
    out_bias = vectors[4] + vectors[5]
    held = ()

    def forward_pieces(items, held):
        where = [place for _, place in items]
        pieces = [v for pieces, _ in items for v in pieces]
        return piece_forward(
            lay, pieces, where, norm_vec, w_qkvu, qkv_bias, up_bias, tables, held
        )

    w_dn, w_wo = Whole(dn, nz * rows), Whole(dn[-1:], rows * width // unit, nz * rows, lay.z)
    tick = 0
    while xs.at < xs.rounds:
        taken = xs.take()
        xs.step()
        if tick == 0:
            GroupGather.send_first(dn, dn_stack)
        elif tick == 1:
            w_dn.flush()
            w_wo.flush()
            for v in dn:
                v.send(1)
        held = forward_pieces(ready, held)
        ready = crossing(taken)
        ready_pieces, held = joined(dn + [w_dn, w_wo, xs], [v for v, _ in ready], held)
        ready = list(zip(ready_pieces, [place for _, place in ready]))
        tick += 1
    for v in dn:
        v.rest(2)

    taken = xs.take()
    own_dy = dy.take()
    dy.step()
    held = forward_pieces(ready + crossing(taken), held)
    dy_buffer.add(crossing(own_dy))
    (held,) = joined([dy, dy_buffer, w_dn, w_wo] + dn, held)
    w_down = w_dn.result()
    w_out = w_wo.result().reshape(hd, width)
    tile = min(512, length)
    flat = (tokens_here, width)
    x_flat, qkv, g, slope = (v.reshape(seqs, length, -1) for v in held)
    x_flat, g, slope = (v.reshape(tokens_here, -1) for v in (x_flat, g, slope))

    taken = dy.take()
    dy.step()
    dy_buffer.add(crossing(taken))
    o, lse = attn_forward(qkv, score_scale)
    o = o.reshape(tokens_here, hd)
    out_sum = SeqScatter(lay)
    parts = {}
    for r in range(1, pair):
        (parts[r],) = output_forward(g, w_down, o, w_out, span, out_sum.order, r * count * nz)
    o, lse, g, parts, w_down, w_out = joined([dy, dy_buffer], o, lse, g, parts, w_down, w_out)

    taken = dy.take()
    while dy.at < dy.rounds:
        dy.step()
    dy_buffer.flush(count)
    more = [lay.core_hop(parts[r], r) for r in range(1, pair)]
    dy_buffer.add(crossing(taken))
    out_sum.load(
        output_forward(g, w_down, o, w_out, span, out_sum.order, 0, more, separate=out_sum.four)
    )
    o, lse, g = joined([dy, dy_buffer, out_sum], o, lse, g)

    def steps(*parts):
        for p in parts:
            p.step()

    def to_owners(blocks):
        return lax.all_to_all(blocks, "seq", 0, 0, tiled=True)

    def at_owner(blocks):
        parts = [blocks[:, r] for r in range(pair)]
        return [lay.core_hop(v, r) if r else v for r, v in enumerate(parts)]

    def more_rounds(parts):
        while parts[0].at < len(parts[0].bits):
            if len(parts) == pair and parts[0].keep.shape[2] < width:
                fold(parts)
            else:
                for p in parts:
                    p.fold()
            steps(*parts)

    out_sum.send()
    dy_buffer.add(crossing(dy.take()))
    dy_all = dy_buffer.flush(count).reshape(seqs, length, width)
    down = gradient(lay, dy_all.reshape(flat), g)
    (dy_all,) = joined(down, dy_all)

    z_sum = SeqScatter(lay)
    dp, dp_sums, z_parts = (), {}, {}

    def attention_part(r, held):
        *held, dp_sums[r] = attn_backward(
            dy_all, w_out, qkv, lse, tables, score_scale, r, pair, held
        )
        return held

    def input_part(r, more=(), separate=False):
        return input_backward(
            du,
            dp[0].reshape(tokens_here, 3 * hd),
            w_qkvu,
            norm_vec,
            span,
            z_sum.order,
            r * count * nz,
            more,
            separate,
        )

    steps(*down)
    du, du_sums = hidden_backward(dy_all.reshape(flat), w_down, slope, tile)
    dy_all = after(dy_all, du)
    for r in range(1, pair):
        dp = attention_part(r, dp)
    dy_all, du, du_sums, dp, dp_sums = joined([out_sum] + down, dy_all, du, du_sums, dp, dp_sums)

    out_sum.finish()
    more_rounds(down)
    for r in range(1, pair):
        (z_parts[r],) = input_part(r)
    down_blocks = final_blocks(down, nz)
    dy_all, dp, z_parts, down_blocks = joined([out_sum], dy_all, dp, z_parts, down_blocks)

    for r in range(1, pair):
        z_parts[r] = lay.core_hop(z_parts[r], r)
    down_blocks = to_owners(down_blocks)
    dp = attention_part(0, dp)
    z_sum.load(input_part(0, [z_parts[r] for r in range(1, pair)], z_sum.four))
    dp = dp[0].reshape(tokens_here, 3 * hd)
    dy_flat, du, dp, dp_sums, down_blocks = joined(
        [z_sum], dy_all.reshape(flat), du, dp, dp_sums, down_blocks
    )

    z_sum.send()
    up, lanes = folded_gradient(lay, x_flat, du, du_sums, w_qkvu, 0, 2)
    dp, lanes = joined(up, dp, lanes)

    steps(*up)
    upstream = cotangent.astype(f32)
    flat_cotangent = cotangent.reshape(count * span, width)
    others = plain_columns(lay, flat_cotangent, du_sums, list(dp_sums.values()), unit, hd)
    dp_sums = sum(jnp.sum(v[:, 0], axis=0) for v in dp_sums.values())
    dp_sums = jnp.broadcast_to(dp_sums[None], (8, 3 * hd))
    (dqkv,) = folded_gradient(lay, x_flat, dp, dp_sums, w_qkvu, unit, 0, (lanes, others))
    dy_flat, upstream = joined(up + dqkv + [z_sum], dy_flat, upstream)

    z_sum.finish()
    more_rounds(up)
    steps(*dqkv)
    out_whole = dot(o, dy_flat, 0, 0)
    out_whole = out_whole.astype(bf16).reshape(groups, rows, width)
    out_whole = jnp.stack(
        [
            lax.dynamic_index_in_dim(
                out_whole, lay.g ^ lay.z ^ GroupScatter.member(lay, i, True), 0, keepdims=False
            )
            for i in range(groups)
        ]
    )
    wo = GroupScatter(lay, out_whole[: groups // 2], out_whole[groups // 2 :], True)
    up_blocks = final_blocks(up, nz)
    (up_blocks,) = joined([wo, z_sum, out_sum], up_blocks)

    mlp_state = (mlp_params, mlp_first, mlp_second)
    attn_state = (attn_params, attn_first, attn_second)
    up_blocks = to_owners(up_blocks)
    more_rounds(dqkv)
    steps(wo)
    dqkv_blocks = final_blocks(dqkv, nz)
    outputs = (inputs.astype(f32) + out_sum.result().reshape(inputs.shape) + out_bias).astype(bf16)
    up_blocks, dqkv_blocks, down_blocks, outputs = joined(
        [wo], up_blocks, dqkv_blocks, down_blocks, outputs
    )

    dqkv_blocks = to_owners(dqkv_blocks)
    more_rounds([wo])
    mlp_result = adam_columns(
        lay, rate_mlp, at_owner(down_blocks), 0, unit, mlp_state, ff, 1, ()
    )
    normed_grad = z_sum.result().reshape(inputs.shape)
    normed, scaling = normalize(inputs.astype(f32))
    grad_mean = jnp.mean(normed_grad, axis=-1, keepdims=True)
    grad_proj = jnp.mean(normed_grad * normed, axis=-1, keepdims=True)
    input_grad = upstream + scaling * (normed_grad - grad_mean - normed * grad_proj)
    up_parts = at_owner(up_blocks)
    mlp_result = adam_columns(lay, rate_mlp, up_parts, 0, unit, mlp_state, 0, 1, mlp_result)
    dqkv_blocks, mlp_result, input_grad = joined([wo], dqkv_blocks, mlp_result, input_grad)

    out_grad = wo.result().astype(bf16)
    out_grad = lax.ppermute(out_grad, AXES, [(b, a) for a, b in lay.head_owner_perm()])
    dqkv_parts = at_owner(dqkv_blocks)
    attn_result = adam_columns(lay, rate_attention, dqkv_parts, 0, hd, attn_state, 0, 3, ())
    at = 3 * hd
    small_grad = sum(
        jnp.sum(v[:, :, at : at + small.shape[1]].astype(f32), axis=0) for v in dqkv_parts
    )
    small_result = adamw(small, small_grad, small_first, small_second, rate_vector)
    out_grad = [out_grad[None]]
    attn_result = adam_columns(
        lay, rate_attention, out_grad, 0, width, attn_state, 3 * width, 1, attn_result
    )
    return (outputs, input_grad, *attn_result, *mlp_result, *small_result)


def solution(mesh):
    tokens, weights = P("dp", "seq", None), P(("dp", "seq"), None)
    return jax.shard_map(
        body,
        mesh=mesh,
        in_specs=(tokens,) * 2 + (weights,) * 9,
        out_specs=(tokens,) * 2 + (weights,) * 12,
        check_vma=False,
    )
```

```python
from functools import partial

import jax
import jax.numpy as jnp
from jax import lax
from jax.experimental import pallas as pl
from jax.experimental.pallas import tpu as pltpu
from jax.sharding import PartitionSpec as P

HEADS = 8
STEP = 10
AXES = ("dp", "seq")
LANES = 128
VMEM_LIMIT = 56 * 2**20

norm_eps = 1e-05
masked_value = -1e30
beta_first = 0.9
beta_second = 0.95
adam_eps = 1e-08
decay_rate = 0.01
rate_attention = 0.06
rate_mlp = 0.02
rate_vector = 0.2

f32 = jnp.float32
bf16 = jnp.bfloat16


def normalize(values):
    row_mean = jnp.mean(values, axis=-1, keepdims=True)
    centred = values - row_mean
    spread = jnp.mean(centred * centred, axis=-1, keepdims=True)
    scaling = lax.rsqrt(spread + norm_eps)
    return (centred * scaling, scaling)


def dot(left_op, right_op, left_dim=1, right_dim=0):
    return lax.dot_general(
        left_op,
        right_op,
        (((left_dim,), (right_dim,)), ((), ())),
        preferred_element_type=f32,
    )


def adamw(master, gradient, first_old, second_old, step_rate):
    first_new = beta_first * first_old + (1.0 - beta_first) * gradient
    second_new = beta_second * second_old + (1.0 - beta_second) * gradient * gradient
    first_hat = first_new / (1.0 - beta_first**STEP)
    second_hat = second_new / (1.0 - beta_second**STEP)
    updated = master - step_rate * (
        first_hat / (jnp.sqrt(second_hat) + adam_eps) + decay_rate * master
    )
    return (gradient, updated, first_new, second_new)


def params(cost=None, **kw):
    return dict(
        compiler_params=pltpu.CompilerParams(vmem_limit_bytes=VMEM_LIMIT, **kw),
        cost_estimate=cost and pl.CostEstimate(flops=cost[0] // 1000 + 1, bytes_accessed=cost[1] // 1000 + 1, transcendentals=0),
    )


class Layout:
    def __init__(self, nd, nz):
        self.nd, self.nz = nd, nz
        self.pair = HEADS // nz
        self.groups = nd // self.pair
        self.dp = lax.axis_index("dp")
        self.z = lax.axis_index("seq")
        self.g = self.dp // self.pair
        self.c = self.dp % self.pair
        self.t = self.z * self.pair + self.c

    def perm(self, target):
        pairs = []
        for dp in range(self.nd):
            for z in range(self.nz):
                goal = target(dp // self.pair, dp % self.pair, z)
                if goal is not None:
                    g, c, s = goal
                    pairs.append((dp * self.nz + z, (g * self.pair + c) * self.nz + s))
        return pairs

    def hop(self, value, target):
        return lax.ppermute(value, AXES, self.perm(target))

    def group_hop(self, value, bit):
        return self.hop(value, lambda g, c, z: (g ^ bit, c, z))

    def core_hop(self, value, r):
        return self.hop(value, lambda g, c, z: (g, c ^ r, z))

    def ring(self, value):
        return self.hop(value, lambda g, c, z: (g, c, (z + 1) % self.nz))

    def flat_hop(self, value, bit):
        return lax.ppermute(value, AXES, [(i, i ^ bit) for i in range(self.nd * self.nz)])

    def head_owner_perm(self):
        pairs = []
        for r in range(self.nd * self.nz):
            head, quarter = r // self.groups, r % self.groups
            s, c = head // self.pair, head % self.pair
            pairs.append((r, ((quarter ^ s) * self.pair + c) * self.nz + s))
        return pairs


def after(values, *deps):
    flat, tree = jax.tree.flatten((values, deps))
    return jax.tree.unflatten(tree, lax.optimization_barrier(flat))[0]


def join(*values):
    return after(values)


def bits_of(count, descending):
    bits = []
    bit = 1
    while bit < count:
        bits.append(bit)
        bit *= 2
    return bits[::-1] if descending else bits


class GroupGather:
    def __init__(self, lay, block, descending):
        self.lay = lay
        self.rows = block.shape[0]
        self.held = {0: (block, 0)}
        self.rounds = [[] for _ in bits_of(lay.groups, False)]
        known = [0]
        for bit in bits_of(lay.groups, descending):
            for m in list(known):
                self.rounds[bin(m).count("1")].append((m, bit))
                known.append(m ^ bit)

    def block(self, m):
        array, first = self.held[m]
        return array[first : first + self.rows]

    def send(self, depth):
        if depth < len(self.rounds):
            for m, bit in self.rounds[depth]:
                self.held[m ^ bit] = (self.lay.group_hop(self.block(m), bit), 0)

    @staticmethod
    def stack(halves):
        return jnp.concatenate([h.block(0) for h in halves])

    @staticmethod
    def send_first(halves, stack):
        lay = halves[0].lay
        for bit in bits_of(lay.groups, False):
            got = lay.group_hop(stack, bit)
            first = 0
            for h in halves:
                h.held[bit] = (got, first)
                first += h.rows

    @property
    def state(self):
        return {m: v for m, (v, _) in self.held.items()}

    @state.setter
    def state(self, state):
        for m, v in state.items():
            self.held[m] = (v, self.held[m][1])

    def rest(self, depth):
        while depth < len(self.rounds):
            self.send(depth)
            depth += 1
        return self.held


class GroupScatter:
    def __init__(self, lay, keep, send, descending):
        self.lay = lay
        self.keep, self.send = keep, send
        self.bits = bits_of(lay.groups, descending)
        self.at = 0

    @staticmethod
    def member(lay, index, descending):
        bits = bits_of(lay.groups, descending)
        return sum(bit for j, bit in enumerate(bits) if index >> (len(bits) - 1 - j) & 1)

    @property
    def state(self):
        return (self.keep, self.send)

    @state.setter
    def state(self, state):
        self.keep, self.send = state

    def step(self):
        if self.at < len(self.bits):
            self.send = self.lay.group_hop(self.send, self.bits[self.at])
            self.at += 1

    def fold(self):
        total = self.keep.astype(f32) + self.send.astype(f32)
        half = total.shape[0] // 2
        self.keep, self.send = total[:half], total[half:].astype(bf16)

    def result(self):
        return (self.keep.astype(f32) + self.send.astype(f32))[0]


def cast_kernel(c_ref, *refs):
    out_ref = refs[-1]
    at = 0
    for ref in refs[:-1]:
        out_ref[0, :, at : at + ref.shape[1]] = ref[...].astype(bf16)
        at += ref.shape[1]


def prepare(lay, r, sources):
    rows, pair, nz = sources[0][0].shape[0], lay.pair, lay.nz

    def spec(first, width):
        if first is None:
            return pl.BlockSpec((rows, width), lambda z, c: (0, 0))
        return pl.BlockSpec((rows, width), lambda z, c: (0, first + z * pair + (c[0] ^ r)))

    total = sum(width for _, _, width in sources)
    return pl.pallas_call(
        cast_kernel,
        grid_spec=pltpu.PrefetchScalarGridSpec(
            num_scalar_prefetch=1,
            grid=(nz,),
            in_specs=[spec(first, width) for _, first, width in sources],
            out_specs=pl.BlockSpec((1, rows, total), lambda z, c: (z, 0, 0)),
        ),
        out_shape=jax.ShapeDtypeStruct((nz, rows, total), bf16),
        name="prepare",
        **params((rows * total * nz, rows * total * nz * 6)),
    )(jnp.reshape(lay.c, (1,)).astype(jnp.int32), *[v for v, _, _ in sources])


def place_kernel(count, tile, slot_ref, *refs):
    out_ref, sems = refs[-2], refs[-1]
    here = pl.ds(pl.multiple_of(pl.program_id(0) * tile, tile), tile)

    def copy(i):
        return pltpu.make_async_copy(refs[i], out_ref.at[slot_ref[i], here], sems.at[i])

    for i in range(count):

        @pl.when(slot_ref[i] >= 0)
        def _(i=i):
            copy(i).start()

    for i in range(count):

        @pl.when(slot_ref[i] >= 0)
        def _(i=i):
            copy(i).wait()


def place(blocks, slots, rows, total, held=None):
    count = len(blocks)
    width = blocks[0][0].shape[1]
    tile = rows if count * rows * width <= 2**21 else max(min(64, rows), rows // 2)
    operands = [v for v, _ in blocks] + ([] if held is None else [held])
    any_spec = pl.BlockSpec(memory_space=pl.ANY)
    return pl.pallas_call(
        partial(place_kernel, count, tile),
        grid_spec=pltpu.PrefetchScalarGridSpec(
            num_scalar_prefetch=1,
            grid=(rows // tile,),
            in_specs=[
                pl.BlockSpec(
                    (tile, width),
                    lambda i, slot, first=first, j=j: (
                        first // tile + jnp.where(slot[j] >= 0, i, 0),
                        0,
                    ),
                )
                for j, (_, first) in enumerate(blocks)
            ]
            + [any_spec] * (len(operands) - count),
            out_specs=any_spec,
            scratch_shapes=[pltpu.SemaphoreType.DMA((count,))],
        ),
        out_shape=jax.ShapeDtypeStruct((total, rows, width), blocks[0][0].dtype),
        input_output_aliases={} if held is None else {count + 1: 0},
        name="place",
        **params((count, 4 * count * rows * width)),
    )(jnp.stack([jnp.asarray(v, jnp.int32) for v in slots]), *operands)


def flip_kernel(in_ref, out_ref):
    out_ref[...] = in_ref[...].astype(f32).T


def last_columns(array):
    rows, total = array.shape
    return pl.pallas_call(
        flip_kernel,
        grid=(1,),
        in_specs=[pl.BlockSpec((rows, LANES), lambda i: (0, total // LANES - 1))],
        out_specs=pl.BlockSpec((LANES, rows), lambda i: (0, 0)),
        out_shape=jax.ShapeDtypeStruct((LANES, rows), f32),
        name="last_columns",
        **params(),
    )(array)


def block_order(lay):
    order = []
    for part in (1, 0):
        for r in range(lay.pair):
            for i in range(lay.groups // 2):
                m = GroupScatter.member(lay, part * (lay.groups // 2) + i, bool(r))
                order.append((lay.g ^ m) * lay.pair + (lay.c ^ r))
    return jnp.stack(order).astype(jnp.int32)


def write_block(half, outs, at, value):
    i = pl.program_id(0)
    for k, out in enumerate(outs):

        @pl.when(jnp.logical_and(i >= k * half, i < (k + 1) * half))
        def _(out=out):
            out[0, :, at : at + value.shape[1]] = value


def gradient_kernel(half, block_ref, left_ref, right_ref, *outs):
    write_block(half, outs, 0, dot(left_ref[...], right_ref[...], 0, 0).astype(bf16))


def folded_kernel(half, first, gain, rides, block_ref, x_ref, right_ref, sums_ref, w_ref, small_ref, *refs):
    others, outs = (refs[:2], refs[2:]) if rides else ((), refs[:-1])
    vec = small_ref[...].astype(f32)
    raw = dot(x_ref[...], right_ref[...], 0, 0)
    sums = sums_ref[0:1]
    grad = raw * vec[:, gain : gain + 1] + sums * vec[:, gain + 1 : gain + 2]
    write_block(half, outs, 0, grad.astype(bf16))
    w = w_ref[:, first : first + raw.shape[1]].astype(f32)
    lane = lax.broadcasted_iota(jnp.int32, vec.shape, 1)
    moment = jnp.sum(w * raw, axis=1, keepdims=True)
    plain = jnp.sum(w * sums, axis=1, keepdims=True)
    lanes = jnp.where(lane == gain, moment, jnp.where(lane == gain + 1, plain, 0.0))
    if rides:
        lanes = lanes + others[0][...] + others[1][...]
        write_block(half, outs, raw.shape[1], lanes.astype(bf16))
    else:
        refs[-1][...] = lanes


def columns_kernel(unit, hd, t_ref, dy_ref, du_ref, *refs):
    out_ref = refs[-1]
    width = out_ref.shape[0]
    t = t_ref[0]
    place = lax.broadcasted_iota(jnp.int32, (1, width), 1)
    dy = jnp.sum(dy_ref[...].astype(f32), axis=0, keepdims=True)
    dp = sum(jnp.sum(ref[:, 0], axis=0, keepdims=True) for ref in refs[:-1])
    blank = jnp.zeros((1, width), f32)
    rows = [blank] * 4 + [dy, dy]
    for j in range(3):
        head = jnp.concatenate([dp[:, j * hd : (j + 1) * hd]] * (width // hd), axis=1)
        rows.append(jnp.where(place // hd == t, head, 0.0))
    share = width // unit
    units = jnp.concatenate([du_ref[0:1]] * share, axis=1)
    for k in range(HEADS // share):
        rows.append(jnp.where(place // unit + k * share == t, units, 0.0))
    rows += [blank] * (LANES - len(rows))
    out_ref[...] = jnp.concatenate(rows).T


def plain_columns(lay, dy, du_sums, dp_sums, unit, hd):
    tokens, width = dy.shape

    def whole(v):
        return pl.BlockSpec(v.shape, lambda i, t: (0,) * v.ndim)

    return pl.pallas_call(
        partial(columns_kernel, unit, hd),
        grid_spec=pltpu.PrefetchScalarGridSpec(
            num_scalar_prefetch=1,
            grid=(1,),
            in_specs=[whole(v) for v in (dy, du_sums, *dp_sums)],
            out_specs=pl.BlockSpec((width, LANES), lambda i, t: (0, 0)),
        ),
        out_shape=jax.ShapeDtypeStruct((width, LANES), f32),
        name="plain_columns",
        **params((tokens * width, 4 * tokens * width)),
    )(jnp.reshape(lay.t, (1,)).astype(jnp.int32), dy, du_sums, *dp_sums)


def gradient_call(lay, kernel, left, rights, by_rows, n, more=()):
    tokens, width = left.shape
    pair, half = lay.pair, lay.groups // 2
    rows = width // (lay.groups * pair)
    outs = 2 * pair

    def out_map(k):
        return lambda i, block: (jnp.clip(i - k * half, 0, half - 1), 0, 0)

    def row_map(column):
        return lambda i, block: (block[i], column)

    values = pl.pallas_call(
        partial(kernel, half),
        grid_spec=pltpu.PrefetchScalarGridSpec(
            num_scalar_prefetch=1,
            grid=(outs * half,),
            in_specs=[pl.BlockSpec((tokens, rows), lambda i, block: (0, block[i]))]
            + [pl.BlockSpec(v.shape, lambda i, block: (0, 0)) for v in rights]
            + [pl.BlockSpec((rows, size), row_map(column)) for _, size, column in by_rows],
            out_specs=[pl.BlockSpec((1, rows, n), out_map(k)) for k in range(outs)]
            + [pl.BlockSpec((rows, size), row_map(0)) for size in more],
        ),
        out_shape=[jax.ShapeDtypeStruct((half, rows, n), bf16)] * outs
        + [jax.ShapeDtypeStruct((width, size), f32) for size in more],
        name="gradient",
        **params((2 * tokens * width * n, 2 * (tokens * width + tokens * n + width * n))),
    )(block_order(lay), left, *rights, *[v for v, _, _ in by_rows])
    parts = [GroupScatter(lay, values[pair + r], values[r], bool(r)) for r in range(pair)]
    return (parts, *values[outs:])


def gradient(lay, left, right):
    return gradient_call(lay, gradient_kernel, left, [right], [], right.shape[1])[0]


def folded_gradient(lay, x, right, sums, w_qu, first, gain, others=()):
    total = w_qu.shape[1]
    by_rows = [(w_qu, total, 0), (w_qu, LANES, total // LANES - 1)]
    by_rows += [(v, LANES, 0) for v in others]
    rides = len(others) > 0

    def call(half, *refs):
        folded_kernel(half, first, gain, rides, *refs)

    n = right.shape[1] + (LANES if rides else 0)
    return gradient_call(lay, call, x, [right, sums], by_rows, n, () if rides else (LANES,))


def fold_kernel(*refs):
    count = len(refs) // 4
    for p in range(count):
        keep, got, next_keep, next_send = refs[p], refs[count + p], refs[2 * count + p], refs[3 * count + p]
        half = next_keep.shape[0]
        total = keep[...].astype(f32) + got[...].astype(f32)
        next_keep[...] = total[:half]
        next_send[...] = total[half:].astype(bf16)


def fold(parts):
    held, rows, n = parts[0].keep.shape
    half = held // 2
    tile = min(128, rows)
    full = pl.BlockSpec((held, tile, n), lambda i: (0, i, 0))
    part = pl.BlockSpec((half, tile, n), lambda i: (0, i, 0))
    count = len(parts)
    values = pl.pallas_call(
        fold_kernel,
        grid=(rows // tile,),
        in_specs=[full] * (2 * count),
        out_specs=[part] * (2 * count),
        out_shape=[jax.ShapeDtypeStruct((half, rows, n), f32)] * count
        + [jax.ShapeDtypeStruct((half, rows, n), bf16)] * count,
        name="fold",
        **params((held * rows * n, 8 * held * rows * n)),
    )(*[p.keep for p in parts], *[p.send for p in parts])
    for k, p in enumerate(parts):
        p.keep, p.send = values[k], values[count + k]


def blocks_kernel(count, *refs):
    out_ref = refs[-1]
    places, _, rows, _ = out_ref.shape
    for p in range(count):
        total = (refs[p][0].astype(f32) + refs[count + p][0].astype(f32)).astype(bf16)
        for z in range(places):
            out_ref[z, p] = total[z * rows : (z + 1) * rows]


def final_blocks(parts, nz):
    _, total, n = parts[0].keep.shape
    rows, count = total // nz, len(parts)
    steps = nz // 2 if nz % 2 == 0 else nz
    places = nz // steps
    return pl.pallas_call(
        partial(blocks_kernel, count),
        grid=(steps,),
        in_specs=[pl.BlockSpec((1, places * rows, n), lambda i: (0, i, 0))] * (2 * count),
        out_specs=pl.BlockSpec((places, count, rows, n), lambda i: (i, 0, 0, 0)),
        out_shape=jax.ShapeDtypeStruct((nz, count, rows, n), bf16),
        name="final_blocks",
        **params((count * total * n, 8 * count * total * n)),
    )(*[p.keep for p in parts], *[p.send for p in parts])


def chunk_kernel(count, ways, slot_ref, *refs):
    for k in range(ways):

        @pl.when(slot_ref[k] >= 0)
        def _(k=k):
            total = sum(refs[k * count + p][...].astype(f32) for p in range(count))
            out = refs[-ways + k]
            out[...] = total.astype(out.dtype)


def chunk_sums(parts, slots, received):
    count, _, span, width = parts[0].shape
    tile = min(span, 128)
    ways = len(slots)

    def whole(k):
        return lambda i, slot: (0, jnp.where(slot[k] >= 0, i, 0), 0)

    def part(k):
        return lambda i, slot: (0, jnp.maximum(slot[k], 0), jnp.where(slot[k] >= 0, i, 0), 0)

    in_specs, operands = [], []
    for k in range(ways):
        for p in parts:
            in_specs.append(pl.BlockSpec((count, None, tile, width), part(k)))
            operands.append(p)
        if received:
            in_specs.append(pl.BlockSpec((count, tile, width), whole(k)))
            operands.append(received[k])
    shape = jax.ShapeDtypeStruct((count, span, width), bf16)
    return pl.pallas_call(
        partial(chunk_kernel, len(operands) // ways, ways),
        grid_spec=pltpu.PrefetchScalarGridSpec(
            num_scalar_prefetch=1,
            grid=(span // tile,),
            in_specs=in_specs,
            out_specs=[pl.BlockSpec((count, tile, width), whole(k)) for k in range(ways)],
        ),
        out_shape=[shape] * ways,
        name="chunk_sums",
        **params((8 * count * span * width, 16 * count * span * width)),
    )(jnp.stack(slots).astype(jnp.int32), *operands)


def turn(values, cosine, low_sine, high_sine, quarter):
    head = values[:, :LANES]
    turned = (
        head * cosine
        + pltpu.roll(head, LANES - quarter, 1) * low_sine
        + pltpu.roll(head, quarter, 1) * high_sine
    )
    return jnp.concatenate([turned, values[:, LANES:]], axis=1)


def piece_kernel(pair, places, quarter, pos_ref, *refs):
    x_refs, refs = refs[: pair * places], refs[pair * places :]
    for p in range(places):

        @pl.when(pl.program_id(1) == p)
        def _(p=p):
            piece_rows(pair, quarter, x_refs[p * pair : (p + 1) * pair], refs)


def piece_rows(pair, quarter, x_refs, refs):
    vec_ref, w_ref, qkv_bias_ref, up_bias_ref, tab_ref = refs[:5]
    x_out, qkv_out, g_out, slope_out = refs[-4:]
    tile = x_refs[0].shape[1]
    unit, wide = g_out.shape[-1], qkv_out.shape[-1]
    hd = wide // 3
    x = jnp.concatenate([ref[0].astype(f32) for ref in x_refs])
    normed, _ = normalize(x)
    a = (normed * vec_ref[0:1] + vec_ref[1:2]).astype(bf16)
    m = (normed * vec_ref[2:3] + vec_ref[3:4]).astype(bf16)
    cosine, low_sine, high_sine = (jnp.concatenate([tab_ref[k]] * pair) for k in range(3))

    def put(out, at, value):
        value = value.astype(bf16)
        for r in range(pair):
            out[r, 0, 0, :, at : at + value.shape[1]] = value[r * tile : (r + 1) * tile]

    put(x_out, 0, normed)
    for j in range(3):
        part = dot(a, w_ref[:, unit + j * hd : unit + (j + 1) * hd])
        part = part + qkv_bias_ref[0:1, j * hd : (j + 1) * hd]
        put(qkv_out, j * hd, turn(part, cosine, low_sine, high_sine, quarter) if j < 2 else part)
    u = dot(m, w_ref[:, :unit]) + up_bias_ref[0:1]
    half = 0.5 * (1.0 + lax.erf(u * (0.5**0.5)))
    put(g_out, 0, u * half)
    put(slope_out, 0, half + u * (jnp.exp(-0.5 * u * u) * 0.3989422804014327))


def piece_forward(lay, pieces, where, vec, w_qu, qkv_bias, up_bias, tables, held):
    count, span, width = pieces[0].shape
    pair, nz, places = lay.pair, lay.nz, len(where)
    unit, wide = up_bias.shape[1], qkv_bias.shape[1]
    tile = min(span, 128)
    steps = span // tile

    def out(n):
        return (
            jax.ShapeDtypeStruct((pair, count, nz, span, n), bf16),
            pl.BlockSpec((pair, 1, 1, tile, n), lambda i, p, j, pos: (0, i, pos[p], j, 0)),
        )

    def whole(v):
        return pl.BlockSpec(v.shape, lambda i, p, j, pos: (0,) * v.ndim)

    def row_map(q):
        return lambda i, p, j, pos: (i, jnp.where(p == q, j, jnp.where(p < q, 0, steps - 1)), 0)

    outs = [out(n) for n in (width, wide, unit, unit)]
    in_specs = [pl.BlockSpec((1, tile, width), row_map(q)) for q in range(places) for _ in range(pair)]
    in_specs += [pl.BlockSpec((8, width), lambda i, p, j, pos: (0, 0))]
    in_specs += [whole(v) for v in (w_qu, qkv_bias, up_bias)]
    in_specs += [pl.BlockSpec((3, tile, LANES), lambda i, p, j, pos: (0, pos[p] * steps + j, 0))]
    in_specs += [pl.BlockSpec(memory_space=pl.ANY)] * len(held)
    tokens = pair * places * count * span
    return pl.pallas_call(
        partial(piece_kernel, pair, places, wide // 24),
        grid_spec=pltpu.PrefetchScalarGridSpec(
            num_scalar_prefetch=1,
            grid=(count, places, steps),
            in_specs=in_specs,
            out_specs=[o[1] for o in outs],
        ),
        out_shape=[o[0] for o in outs],
        input_output_aliases={pair * places + 6 + k: k for k in range(len(held))},
        name="piece_forward",
        **params((2 * tokens * width * (unit + wide), 12 * tokens * width)),
    )(
        jnp.stack(where).astype(jnp.int32),
        *pieces,
        vec,
        w_qu,
        qkv_bias,
        up_bias,
        tables,
        *held,
    )


def attn_fwd_kernel(scale, tile, qkv_ref, o_ref, lse_ref):
    length, hd = o_ref.shape[1:]
    for i in range(length // tile):
        end = (i + 1) * tile
        q_i = qkv_ref[0, i * tile : end, :hd]
        scores = dot(q_i, qkv_ref[0, :end, hd : 2 * hd], 1, 1) * scale
        row = lax.broadcasted_iota(jnp.int32, scores.shape, 0) + i * tile
        col = lax.broadcasted_iota(jnp.int32, scores.shape, 1)
        scores = jnp.where(col <= row, scores, masked_value)
        row_max = jnp.max(scores, axis=1, keepdims=True)
        terms = jnp.exp(scores - row_max)
        row_sum = jnp.sum(terms, axis=1, keepdims=True)
        probs = (terms / row_sum).astype(bf16)
        o_ref[0, i * tile : end] = dot(probs, qkv_ref[0, :end, 2 * hd :]).astype(bf16)
        lse_ref[0, i * tile : end] = jnp.broadcast_to(row_max + jnp.log(row_sum), (tile, LANES))


def attn_forward(qkv, scale):
    seqs, length, wide = qkv.shape
    hd = wide // 3
    return pl.pallas_call(
        partial(attn_fwd_kernel, scale, min(512, length)),
        grid=(seqs,),
        in_specs=[pl.BlockSpec((1, length, wide), lambda s: (s, 0, 0))],
        out_specs=[
            pl.BlockSpec((1, length, hd), lambda s: (s, 0, 0)),
            pl.BlockSpec((1, length, LANES), lambda s: (s, 0, 0)),
        ],
        out_shape=[
            jax.ShapeDtypeStruct((seqs, length, hd), bf16),
            jax.ShapeDtypeStruct((seqs, length, LANES), f32),
        ],
        name="attn_forward",
        **params((4 * seqs * length * length * hd, 8 * seqs * length * wide)),
    )(qkv)


def attn_bwd_kernel(quarter, scale, tile, dy_ref, wo_ref, qkv_ref, lse_ref, tab_ref, *refs):
    dp_ref, sum_ref, do_s, dk_s, dv_s = refs[-5:]
    length = dy_ref.shape[1]
    hd = wo_ref.shape[0]
    cosine, low_sine, high_sine = tab_ref[0], -tab_ref[1], -tab_ref[2]
    do_s[...] = dot(dy_ref[0], wo_ref[...], 1, 1).astype(bf16)
    steps = length // tile
    for i in reversed(range(steps)):
        end = (i + 1) * tile
        q_i = qkv_ref[0, i * tile : end, :hd]
        k = qkv_ref[0, :end, hd : 2 * hd]
        do_i = do_s[i * tile : end]
        scores = dot(q_i, k, 1, 1) * scale
        row = lax.broadcasted_iota(jnp.int32, scores.shape, 0) + i * tile
        col = lax.broadcasted_iota(jnp.int32, scores.shape, 1)
        probs = jnp.where(col <= row, jnp.exp(scores - lse_ref[0, i * tile : end, 0:1]), 0.0)
        probs_grad = dot(do_i, qkv_ref[0, :end, 2 * hd :], 1, 1)
        row_dot = jnp.sum(probs * probs_grad, axis=1, keepdims=True)
        score_grad = (probs * (probs_grad - row_dot)).astype(bf16)
        dq = dot(score_grad, k) * scale
        dp_ref[0, i * tile : end, :hd] = turn(
            dq,
            cosine[i * tile : end],
            low_sine[i * tile : end],
            high_sine[i * tile : end],
            quarter,
        ).astype(bf16)
        dk = dot(score_grad, q_i, 0, 0)
        dv = dot(probs.astype(bf16), do_i, 0, 0)
        if i == steps - 1:
            dk_s[...] = dk
            dv_s[...] = dv
        else:
            dk_s[:end] += dk
            dv_s[:end] += dv
    dp_ref[0, :, hd : 2 * hd] = turn(
        dk_s[...] * scale, cosine, low_sine, high_sine, quarter
    ).astype(bf16)
    dp_ref[0, :, 2 * hd :] = dv_s[...].astype(bf16)
    total = jnp.sum(dp_ref[0].astype(f32), axis=0, keepdims=True)
    sum_ref[0] = jnp.broadcast_to(total, sum_ref.shape[1:])


def attn_backward(dy, w_out, qkv, lse, tables, scale, part, parts, held):
    seqs, length, width = dy.shape
    hd = w_out.shape[0]
    share = seqs // parts
    first = part * share
    flops = 2 * share * length * (hd * width + 5 * length * hd)

    def row_map(s):
        return (first + s, 0, 0)

    return pl.pallas_call(
        partial(attn_bwd_kernel, hd // 8, scale, min(512, length)),
        grid=(share,),
        in_specs=[
            pl.BlockSpec((1, length, width), row_map),
            pl.BlockSpec(w_out.shape, lambda s: (0, 0)),
            pl.BlockSpec((1, length, 3 * hd), row_map),
            pl.BlockSpec((1, length, LANES), row_map),
            pl.BlockSpec(tables.shape, lambda s: (0, 0, 0)),
        ]
        + [pl.BlockSpec(memory_space=pl.ANY)] * len(held),
        out_specs=[
            pl.BlockSpec((1, length, 3 * hd), row_map),
            pl.BlockSpec((1, 8, 3 * hd), lambda s: (s, 0, 0)),
        ],
        out_shape=[
            jax.ShapeDtypeStruct((seqs, length, 3 * hd), bf16),
            jax.ShapeDtypeStruct((share, 8, 3 * hd), f32),
        ],
        input_output_aliases={5 + k: k for k in range(len(held))},
        scratch_shapes=[
            pltpu.VMEM((length, hd), bf16),
            pltpu.VMEM((length, hd), f32),
            pltpu.VMEM((length, hd), f32),
        ],
        name="attn_backward",
        **params((flops, 8 * share * length * width)),
    )(dy, w_out, qkv, lse, tables, *held)


def write_chunk(outs, more, total):
    for ref in more:
        total = total + ref[0].astype(f32)
    total = total.astype(bf16)
    if len(outs) == 1:
        outs[0][0] = total
    else:
        for k, out in enumerate(outs):

            @pl.when(pl.program_id(0) == k)
            def _(out=out):
                out[0] = total


def chunk_outputs(order_len, span, width, separate):
    if separate:
        specs = [pl.BlockSpec((1, span, width), lambda i, order: (0, 0, 0))] * order_len
        return specs, [jax.ShapeDtypeStruct((1, span, width), bf16)] * order_len
    specs = [pl.BlockSpec((1, span, width), lambda i, order: (i, 0, 0))]
    return specs, [jax.ShapeDtypeStruct((order_len, span, width), bf16)]


def output_kernel(count, order_ref, g_ref, wd_ref, o_ref, wo_ref, *refs):
    total = dot(g_ref[...], wd_ref[...], 1, 1) + dot(o_ref[...], wo_ref[...])
    write_chunk(refs[count:], refs[:count], total)


def output_forward(g, w_down, o, w_out, span, order, first, more=(), separate=False):
    unit, width, hd = g.shape[1], w_down.shape[0], o.shape[1]
    steps = order.shape[0]
    out_specs, out_shape = chunk_outputs(steps, span, width, separate)
    return pl.pallas_call(
        partial(output_kernel, len(more)),
        grid_spec=pltpu.PrefetchScalarGridSpec(
            num_scalar_prefetch=1,
            grid=(steps,),
            in_specs=[
                pl.BlockSpec((span, unit), lambda i, order: (first + order[i], 0)),
                pl.BlockSpec(w_down.shape, lambda i, order: (0, 0)),
                pl.BlockSpec((span, hd), lambda i, order: (first + order[i], 0)),
                pl.BlockSpec(w_out.shape, lambda i, order: (0, 0)),
            ]
            + [pl.BlockSpec((1, span, width), lambda i, order: (i, 0, 0))] * len(more),
            out_specs=out_specs,
        ),
        out_shape=out_shape,
        name="output_forward",
        **params((2 * steps * span * width * (unit + hd), 8 * steps * span * width)),
    )(order, g, w_down, o, w_out, *more)


def hidden_kernel(dy_ref, wd_ref, slope_ref, du_ref, sum_ref):
    dg = dot(dy_ref[...], wd_ref[...])
    du_ref[...] = (dg * slope_ref[...].astype(f32)).astype(bf16)
    total = jnp.sum(du_ref[...].astype(f32), axis=0, keepdims=True)
    total = jnp.broadcast_to(total, sum_ref.shape)

    @pl.when(pl.program_id(0) == 0)
    def _():
        sum_ref[...] = total

    @pl.when(pl.program_id(0) > 0)
    def _():
        sum_ref[...] += total


def hidden_backward(dy, w_down, slope, tile):
    tokens, width = dy.shape
    unit = w_down.shape[1]
    return pl.pallas_call(
        hidden_kernel,
        grid=(tokens // tile,),
        in_specs=[
            pl.BlockSpec((tile, width), lambda i: (i, 0)),
            pl.BlockSpec(w_down.shape, lambda i: (0, 0)),
            pl.BlockSpec((tile, unit), lambda i: (i, 0)),
        ],
        out_specs=[
            pl.BlockSpec((tile, unit), lambda i: (i, 0)),
            pl.BlockSpec((8, unit), lambda i: (0, 0)),
        ],
        out_shape=[
            jax.ShapeDtypeStruct((tokens, unit), bf16),
            jax.ShapeDtypeStruct((8, unit), f32),
        ],
        name="hidden_backward",
        **params((2 * tokens * width * unit, 6 * tokens * width)),
    )(dy, w_down, slope)


def input_kernel(count, hd, order_ref, du_ref, dp_ref, wu_ref, wq_ref, wk_ref, wv_ref, vec_ref, *refs):
    da = (
        dot(dp_ref[:, :hd], wq_ref[...], 1, 1)
        + dot(dp_ref[:, hd : 2 * hd], wk_ref[...], 1, 1)
        + dot(dp_ref[:, 2 * hd :], wv_ref[...], 1, 1)
    )
    dm = dot(du_ref[...], wu_ref[...], 1, 1)
    write_chunk(refs[count:], refs[:count], da * vec_ref[0:1] + dm * vec_ref[2:3])


def input_backward(du, dp, w_qu, vec, span, order, first, more=(), separate=False):
    unit, width, hd = du.shape[1], w_qu.shape[0], dp.shape[1] // 3
    columns = unit // hd
    steps = order.shape[0]
    out_specs, out_shape = chunk_outputs(steps, span, width, separate)
    return pl.pallas_call(
        partial(input_kernel, len(more), hd),
        grid_spec=pltpu.PrefetchScalarGridSpec(
            num_scalar_prefetch=1,
            grid=(steps,),
            in_specs=[
                pl.BlockSpec((span, unit), lambda i, order: (first + order[i], 0)),
                pl.BlockSpec((span, 3 * hd), lambda i, order: (first + order[i], 0)),
                pl.BlockSpec((width, unit), lambda i, order: (0, 0)),
            ]
            + [pl.BlockSpec((width, hd), lambda i, order, j=j: (0, columns + j)) for j in range(3)]
            + [pl.BlockSpec((8, width), lambda i, order: (0, 0))]
            + [pl.BlockSpec((1, span, width), lambda i, order: (i, 0, 0))] * len(more),
            out_specs=out_specs,
        ),
        out_shape=out_shape,
        name="input_backward",
        **params((2 * steps * span * width * (unit + 3 * hd), 12 * steps * span * width)),
    )(order, du, dp, w_qu, w_qu, w_qu, w_qu, vec, *more)


def adam_kernel(pair, places, rate, c_ref, *refs):
    g_refs, (w_ref, m_ref, v_ref), outs = refs[:pair], refs[pair : pair + 3], refs[-4:]
    pieces = []
    for z in range(places):
        parts = [ref[z].astype(f32) for ref in g_refs]
        if pair == 2:
            swapped = c_ref[0] == 1
            parts = [jnp.where(swapped, parts[1], parts[0]), jnp.where(swapped, parts[0], parts[1])]
        pieces += parts
    grad = pieces[0] if len(pieces) == 1 else jnp.concatenate(pieces, axis=1)
    result = adamw(w_ref[...], grad, m_ref[...], v_ref[...], rate)
    for ref, value in zip(outs, result, strict=True):
        ref[...] = value


def adam_columns(lay, rate, parts, at, piece, state, start, kinds, held):
    nz, rows, _ = parts[0].shape
    pair = len(parts)
    total = state[0].shape[1]
    places = max(1, min(nz, 2048 // (pair * piece)))
    wide = places * pair * piece
    steps = nz // places
    first = start // wide

    w_spec = pl.BlockSpec((rows, wide), lambda j, z, c: (0, first + j * steps + z))
    g_spec = pl.BlockSpec((places, rows, piece), lambda j, z, c: (z, 0, at // piece + j))
    operands = list(parts) + list(state) + list(held)
    return pl.pallas_call(
        partial(adam_kernel, pair, places, rate),
        grid_spec=pltpu.PrefetchScalarGridSpec(
            num_scalar_prefetch=1,
            grid=(kinds, steps),
            in_specs=[g_spec] * pair
            + [w_spec] * 3
            + [pl.BlockSpec(memory_space=pl.ANY)] * len(held),
            out_specs=[w_spec] * 4,
        ),
        out_shape=[jax.ShapeDtypeStruct((rows, total), f32)] * 4,
        input_output_aliases={1 + pair + 3 + k: k for k in range(len(held))},
        name="adam_columns",
        **params((30 * rows * kinds * piece * HEADS, 30 * rows * kinds * piece * HEADS)),
    )(jnp.reshape(lay.c, (1,)).astype(jnp.int32), *operands)


class SeqGather:
    def __init__(self, lay, own):
        self.lay = lay
        self.rounds, self.at = lay.nz - 1, 0
        self.newest = own
        self.places, self.fresh = [lay.z], [own]

    def step(self):
        self.at += 1
        self.newest = self.lay.ring(self.newest)
        self.fresh.append(self.newest)
        self.places.append((self.lay.z - self.at) % self.lay.nz)

    def take(self):
        items = list(zip(self.fresh, self.places))
        self.fresh, self.places = [], []
        return items

    @property
    def state(self):
        return (self.newest, self.fresh)

    @state.setter
    def state(self, state):
        self.newest, self.fresh = state


class TokenBuffer:
    def __init__(self, lay):
        self.lay, self.todo, self.out = lay, [], None

    def add(self, items):
        for pieces, where in items:
            for r, piece in enumerate(pieces):
                for s in range(piece.shape[0]):
                    self.todo.append((piece[s], (r * piece.shape[0] + s) * self.lay.nz + where))

    def flush(self, count):
        blocks, slots = [(v, 0) for v, _ in self.todo], [w for _, w in self.todo]
        total = self.lay.pair * self.lay.nz * count
        self.out = place(blocks, slots, blocks[0][0].shape[0], total, self.out)
        self.todo = []
        return self.out

    @property
    def state(self):
        return ([v for v, _ in self.todo], self.out)

    @state.setter
    def state(self, state):
        blocks, self.out = state
        self.todo = [(v, w) for v, (_, w) in zip(blocks, self.todo)]


class SeqScatter:
    def __init__(self, lay):
        self.lay = lay
        self.four = lay.nz == 4
        if self.four:
            roles = [[3, 2, 1, 0], [0, 2, 3, 1], [3, 1, 0, 2], [0, 1, 2, 3]]
        else:
            roles = [list(range(lay.nz))] * lay.nz
        self.order = jnp.array(roles, jnp.int32)[lay.z]

    def load(self, chunks):
        self.state = list(chunks)

    def move(self, value, targets):
        return self.lay.hop(value, lambda g, c, z: (g, c, targets[z]) if z in targets else None)

    def send(self):
        if not self.four:
            self.state = [lax.all_to_all(self.state[0], "seq", 0, 0, tiled=True)]
            return
        near, far, last, own = self.state
        near = self.move(near, {0: 1, 3: 2, 2: 3, 1: 0})
        across = self.move(far, {0: 2, 3: 1})
        beside = self.move(far, {1: 2, 2: 1})
        self.state = [near, across, beside, last, own]

    def finish(self):
        if not self.four:
            return
        near, across, beside, last, own = self.state
        inner = jnp.logical_and(self.lay.z > 0, self.lay.z < 3)
        passed = jnp.where(inner, last.astype(f32) + near.astype(f32), last.astype(f32)).astype(bf16)
        came = self.move(passed, {1: 3, 2: 0, 0: 1, 3: 2})
        self.state = [near, across, beside, came, own]

    def result(self):
        if not self.four:
            return jnp.sum(self.state[0].astype(f32), axis=0)
        near, across, beside, came, own = (v[0].astype(f32) for v in self.state)
        inner = jnp.logical_and(self.lay.z > 0, self.lay.z < 3)
        return own + came + jnp.where(inner, across + beside, near)


def body(
    inputs,
    cotangent,
    attn_params,
    attn_first,
    attn_second,
    mlp_params,
    mlp_first,
    mlp_second,
    small,
    small_first,
    small_second,
):
    lay = Layout(lax.axis_size("dp"), lax.axis_size("seq"))
    groups, nz, pair = lay.groups, lay.nz, lay.pair
    count, span, width = inputs.shape
    rows = attn_params.shape[0]
    ff = mlp_params.shape[1] // 2
    hd = width // HEADS
    unit = ff // HEADS
    rot_dims = hd // 4
    score_scale = hd ** (-0.5)
    first_row = (lay.dp * nz + lay.z) * rows
    seqs, length = count * pair, span * nz
    tokens_here = seqs * length

    wide_small = jnp.pad(small, ((0, 0), (0, LANES - small.shape[1])))
    qu_sources = [(mlp_params, 0, unit)]
    qu_sources += [(attn_params, j * HEADS, hd) for j in range(3)]
    qu_sources += [(wide_small, None, LANES)]
    dn_sources = [(mlp_params, HEADS, unit)]

    def swap(sources, r):
        blocks = prepare(lay, r, sources)
        return lay.core_hop(blocks, r) if r else blocks

    def exchange(half):
        return lax.all_to_all(half, "seq", 0, 0, tiled=True).reshape(nz * rows, -1)

    class Whole:
        def __init__(self, halves, size=None, first=0, turn=0):
            self.halves, self.seen, self.state = halves, set(), None
            self.size, self.first, self.turn = size or halves[0].rows, first, turn

        def flush(self):
            items = [
                (r, m, (v[0], v[1] + self.first))
                for r, half in enumerate(self.halves)
                for m, v in half.held.items()
                if (r, m) not in self.seen
            ]
            self.seen |= {(r, m) for r, m, _ in items}
            if items:
                count = len(self.halves)
                slots = [
                    (lay.g ^ m ^ self.turn) * count + (lay.c ^ r if count > 1 else 0)
                    for r, m, _ in items
                ]
                blocks = [v for _, _, v in items]
                self.state = place(blocks, slots, self.size, groups * count, self.state)

        def result(self):
            self.flush()
            return self.state.reshape(-1, self.state.shape[-1])

    def joined(parts, *values):
        *values, states = join(*values, [p.state for p in parts])
        for p, v in zip(parts, states):
            p.state = v
        return values

    def crossed(piece):
        return [piece] + [lay.core_hop(piece, r) for r in range(1, pair)]

    positions = jnp.arange(length, dtype=f32)
    frequency = 10000.0 ** (-(jnp.arange(rot_dims // 2, dtype=f32) * 2.0) / rot_dims)
    angles = positions[:, None] * frequency[None, :]
    cosine, sine = jnp.cos(angles), jnp.sin(angles)
    blank = jnp.zeros_like(sine)
    rest = jnp.zeros((length, LANES - rot_dims), f32)
    tables = jnp.stack(
        [
            jnp.concatenate([cosine, cosine, rest + 1.0], axis=1),
            jnp.concatenate([-sine, blank, rest], axis=1),
            jnp.concatenate([blank, sine, rest], axis=1),
        ]
    )

    first = exchange(swap(qu_sources, 0))
    rest = [swap(qu_sources, r) for r in range(1, pair)]
    w_out = attn_params[:, 3 * width :].astype(bf16)
    dn = jnp.stack([prepare(lay, r, dn_sources) for r in range(pair)], axis=1)
    w_out = lax.ppermute(w_out, AXES, lay.head_owner_perm())
    first, rest, w_out, dn, tables = join(first, rest, w_out, dn, tables)

    qu = [GroupGather(lay, first, False)]
    for r in range(1, pair):
        one = exchange(rest[r - 1])
        qu[-1].send(0)
        one, w_out, dn = joined(qu, one, w_out, dn)
        qu.append(GroupGather(lay, one, bool(r % 2)))
    dn = lax.all_to_all(dn, "seq", 0, 0, tiled=True)
    qu[-1].send(0)
    xs, dy, dy_buffer = SeqGather(lay, inputs), SeqGather(lay, cotangent), TokenBuffer(lay)

    def crossing(items):
        return [(crossed(v), place) for v, place in items]

    (own,) = crossing(xs.take())
    own_pieces, dn, w_out = joined(qu + [xs], own[0], dn, w_out)
    ready = [(own_pieces, own[1])]

    w_qu = Whole(qu)
    xs.step()
    dn = [lay.core_hop(dn[:, r], r) if r else dn[:, r] for r in range(pair)]
    dn = [v.reshape(nz * rows, unit) for v in dn]
    dn[-1] = jnp.concatenate([dn[-1], w_out.reshape(-1, unit)])
    dn = [GroupGather(lay, v, bool(r)) for r, v in enumerate(dn)]
    w_qu.flush()
    for v in qu:
        v.send(1)
    (dn_stack,) = joined(qu + dn + [w_qu, xs], GroupGather.stack(dn))
    for v in qu:
        v.rest(2)

    w_qkvu = w_qu.result()
    vectors = last_columns(w_qkvu)
    norm_vec = vectors
    qkv_bias = vectors[6:9].reshape(3, HEADS, hd)
    qkv_bias = lax.dynamic_index_in_dim(qkv_bias, lay.t, 1, keepdims=False).reshape(1, 3 * hd)
    up_bias = lax.dynamic_slice(vectors[9:13].reshape(-1), (lay.t * unit,), (unit,))[None]
    out_bias = vectors[4] + vectors[5]
    held = ()

    def forward_pieces(items, held):
        where = [place for _, place in items]
        pieces = [v for pieces, _ in items for v in pieces]
        return piece_forward(
            lay, pieces, where, norm_vec, w_qkvu, qkv_bias, up_bias, tables, held
        )

    w_dn, w_wo = Whole(dn, nz * rows), Whole(dn[-1:], rows * width // unit, nz * rows, lay.z)
    tick = 0
    while xs.at < xs.rounds:
        taken = xs.take()
        xs.step()
        if tick == 0:
            GroupGather.send_first(dn, dn_stack)
        elif tick == 1:
            w_dn.flush()
            w_wo.flush()
            for v in dn:
                v.send(1)
        held = forward_pieces(ready, held)
        ready = crossing(taken)
        ready_pieces, held = joined(dn + [w_dn, w_wo, xs], [v for v, _ in ready], held)
        ready = list(zip(ready_pieces, [place for _, place in ready]))
        tick += 1
    for v in dn:
        v.rest(2)

    taken = xs.take()
    own_dy = dy.take()
    dy.step()
    held = forward_pieces(ready + crossing(taken), held)
    dy_buffer.add(crossing(own_dy))
    (held,) = joined([dy, dy_buffer, w_dn, w_wo] + dn, held)
    w_down = w_dn.result()
    w_out = w_wo.result().reshape(hd, width)
    tile = min(512, length)
    flat = (tokens_here, width)
    x_flat, qkv, g, slope = (v.reshape(seqs, length, -1) for v in held)
    x_flat, g, slope = (v.reshape(tokens_here, -1) for v in (x_flat, g, slope))

    taken = dy.take()
    dy.step()
    dy_buffer.add(crossing(taken))
    o, lse = attn_forward(qkv, score_scale)
    o = o.reshape(tokens_here, hd)
    out_sum = SeqScatter(lay)
    parts = {}
    for r in range(1, pair):
        (parts[r],) = output_forward(g, w_down, o, w_out, span, out_sum.order, r * count * nz)
    o, lse, g, parts, w_down, w_out = joined([dy, dy_buffer], o, lse, g, parts, w_down, w_out)

    taken = dy.take()
    while dy.at < dy.rounds:
        dy.step()
    dy_buffer.flush(count)
    more = [lay.core_hop(parts[r], r) for r in range(1, pair)]
    dy_buffer.add(crossing(taken))
    out_sum.load(
        output_forward(g, w_down, o, w_out, span, out_sum.order, 0, more, separate=out_sum.four)
    )
    o, lse, g = joined([dy, dy_buffer, out_sum], o, lse, g)

    def steps(*parts):
        for p in parts:
            p.step()

    def to_owners(blocks):
        return lax.all_to_all(blocks, "seq", 0, 0, tiled=True)

    def at_owner(blocks):
        parts = [blocks[:, r] for r in range(pair)]
        return [lay.core_hop(v, r) if r else v for r, v in enumerate(parts)]

    def more_rounds(parts):
        while parts[0].at < len(parts[0].bits):
            if len(parts) == pair and parts[0].keep.shape[2] < width:
                fold(parts)
            else:
                for p in parts:
                    p.fold()
            steps(*parts)

    out_sum.send()
    dy_buffer.add(crossing(dy.take()))
    dy_all = dy_buffer.flush(count).reshape(seqs, length, width)
    down = gradient(lay, dy_all.reshape(flat), g)
    (dy_all,) = joined(down, dy_all)

    z_sum = SeqScatter(lay)
    dp, dp_sums, z_parts = (), {}, {}

    def attention_part(r, held):
        *held, dp_sums[r] = attn_backward(
            dy_all, w_out, qkv, lse, tables, score_scale, r, pair, held
        )
        return held

    def input_part(r, more=(), separate=False):
        return input_backward(
            du,
            dp[0].reshape(tokens_here, 3 * hd),
            w_qkvu,
            norm_vec,
            span,
            z_sum.order,
            r * count * nz,
            more,
            separate,
        )

    steps(*down)
    du, du_sums = hidden_backward(dy_all.reshape(flat), w_down, slope, tile)
    dy_all = after(dy_all, du)
    for r in range(1, pair):
        dp = attention_part(r, dp)
    dy_all, du, du_sums, dp, dp_sums = joined([out_sum] + down, dy_all, du, du_sums, dp, dp_sums)

    out_sum.finish()
    more_rounds(down)
    for r in range(1, pair):
        (z_parts[r],) = input_part(r)
    down_blocks = final_blocks(down, nz)
    dy_all, dp, z_parts, down_blocks = joined([out_sum], dy_all, dp, z_parts, down_blocks)

    for r in range(1, pair):
        z_parts[r] = lay.core_hop(z_parts[r], r)
    down_blocks = to_owners(down_blocks)
    dp = attention_part(0, dp)
    z_sum.load(input_part(0, [z_parts[r] for r in range(1, pair)], z_sum.four))
    dp = dp[0].reshape(tokens_here, 3 * hd)
    dy_flat, du, dp, dp_sums, down_blocks = joined(
        [z_sum], dy_all.reshape(flat), du, dp, dp_sums, down_blocks
    )

    z_sum.send()
    up, lanes = folded_gradient(lay, x_flat, du, du_sums, w_qkvu, 0, 2)
    dp, lanes = joined(up, dp, lanes)

    steps(*up)
    upstream = cotangent.astype(f32)
    flat_cotangent = cotangent.reshape(count * span, width)
    others = plain_columns(lay, flat_cotangent, du_sums, list(dp_sums.values()), unit, hd)
    dp_sums = sum(jnp.sum(v[:, 0], axis=0) for v in dp_sums.values())
    dp_sums = jnp.broadcast_to(dp_sums[None], (8, 3 * hd))
    (dqkv,) = folded_gradient(lay, x_flat, dp, dp_sums, w_qkvu, unit, 0, (lanes, others))
    dy_flat, upstream = joined(up + dqkv + [z_sum], dy_flat, upstream)

    z_sum.finish()
    more_rounds(up)
    steps(*dqkv)
    out_whole = dot(o, dy_flat, 0, 0)
    out_whole = out_whole.astype(bf16).reshape(groups, rows, width)
    out_whole = jnp.stack(
        [
            lax.dynamic_index_in_dim(
                out_whole, lay.g ^ lay.z ^ GroupScatter.member(lay, i, True), 0, keepdims=False
            )
            for i in range(groups)
        ]
    )
    wo = GroupScatter(lay, out_whole[: groups // 2], out_whole[groups // 2 :], True)
    up_blocks = final_blocks(up, nz)
    (up_blocks,) = joined([wo, z_sum, out_sum], up_blocks)

    mlp_state = (mlp_params, mlp_first, mlp_second)
    attn_state = (attn_params, attn_first, attn_second)
    up_blocks = to_owners(up_blocks)
    more_rounds(dqkv)
    steps(wo)
    dqkv_blocks = final_blocks(dqkv, nz)
    outputs = (inputs.astype(f32) + out_sum.result().reshape(inputs.shape) + out_bias).astype(bf16)
    up_blocks, dqkv_blocks, down_blocks, outputs = joined(
        [wo], up_blocks, dqkv_blocks, down_blocks, outputs
    )

    dqkv_blocks = to_owners(dqkv_blocks)
    more_rounds([wo])
    mlp_result = adam_columns(
        lay, rate_mlp, at_owner(down_blocks), 0, unit, mlp_state, ff, 1, ()
    )
    normed_grad = z_sum.result().reshape(inputs.shape)
    normed, scaling = normalize(inputs.astype(f32))
    grad_mean = jnp.mean(normed_grad, axis=-1, keepdims=True)
    grad_proj = jnp.mean(normed_grad * normed, axis=-1, keepdims=True)
    input_grad = upstream + scaling * (normed_grad - grad_mean - normed * grad_proj)
    up_parts = at_owner(up_blocks)
    mlp_result = adam_columns(lay, rate_mlp, up_parts, 0, unit, mlp_state, 0, 1, mlp_result)
    dqkv_blocks, mlp_result, input_grad = joined([wo], dqkv_blocks, mlp_result, input_grad)

    out_grad = wo.result().astype(bf16)
    out_grad = lax.ppermute(out_grad, AXES, [(b, a) for a, b in lay.head_owner_perm()])
    dqkv_parts = at_owner(dqkv_blocks)
    attn_result = adam_columns(lay, rate_attention, dqkv_parts, 0, hd, attn_state, 0, 3, ())
    at = 3 * hd
    small_grad = sum(
        jnp.sum(v[:, :, at : at + small.shape[1]].astype(f32), axis=0) for v in dqkv_parts
    )
    small_result = adamw(small, small_grad, small_first, small_second, rate_vector)
    out_grad = [out_grad[None]]
    attn_result = adam_columns(
        lay, rate_attention, out_grad, 0, width, attn_state, 3 * width, 1, attn_result
    )
    return (outputs, input_grad, *attn_result, *mlp_result, *small_result)


def solution(mesh):
    tokens, weights = P("dp", "seq", None), P(("dp", "seq"), None)
    return jax.shard_map(
        body,
        mesh=mesh,
        in_specs=(tokens,) * 2 + (weights,) * 9,
        out_specs=(tokens,) * 2 + (weights,) * 12,
        check_vma=False,
    )
```

```python
from functools import partial

import jax
import jax.numpy as jnp
from jax import lax
from jax.experimental import pallas as pl
from jax.experimental.pallas import tpu as pltpu
from jax.sharding import PartitionSpec as P

HEADS = 8
STEP = 10
AXES = ("dp", "seq")
LANES = 128
VMEM_LIMIT = 56 * 2**20

norm_eps = 1e-05
masked_value = -1e30
beta_first = 0.9
beta_second = 0.95
adam_eps = 1e-08
decay_rate = 0.01
rate_attention = 0.06
rate_mlp = 0.02
rate_vector = 0.2

f32 = jnp.float32
bf16 = jnp.bfloat16


def normalize(values):
    row_mean = jnp.mean(values, axis=-1, keepdims=True)
    centred = values - row_mean
    spread = jnp.mean(centred * centred, axis=-1, keepdims=True)
    scaling = lax.rsqrt(spread + norm_eps)
    return (centred * scaling, scaling)


def dot(left_op, right_op, left_dim=1, right_dim=0):
    return lax.dot_general(
        left_op,
        right_op,
        (((left_dim,), (right_dim,)), ((), ())),
        preferred_element_type=f32,
    )


def adamw(master, gradient, first_old, second_old, step_rate):
    first_new = beta_first * first_old + (1.0 - beta_first) * gradient
    second_new = beta_second * second_old + (1.0 - beta_second) * gradient * gradient
    first_hat = first_new / (1.0 - beta_first**STEP)
    second_hat = second_new / (1.0 - beta_second**STEP)
    updated = master - step_rate * (
        first_hat / (jnp.sqrt(second_hat) + adam_eps) + decay_rate * master
    )
    return (gradient, updated, first_new, second_new)


def params(cost=None, **kw):
    return dict(
        compiler_params=pltpu.CompilerParams(vmem_limit_bytes=VMEM_LIMIT, **kw),
        cost_estimate=cost and pl.CostEstimate(flops=cost[0] // 1000 + 1, bytes_accessed=cost[1] // 1000 + 1, transcendentals=0),
    )


class Layout:
    def __init__(self, nd, nz):
        self.nd, self.nz = nd, nz
        self.pair = HEADS // nz
        self.groups = nd // self.pair
        self.dp = lax.axis_index("dp")
        self.z = lax.axis_index("seq")
        self.g = self.dp // self.pair
        self.c = self.dp % self.pair
        self.t = self.z * self.pair + self.c

    def perm(self, target):
        pairs = []
        for dp in range(self.nd):
            for z in range(self.nz):
                goal = target(dp // self.pair, dp % self.pair, z)
                if goal is not None:
                    g, c, s = goal
                    pairs.append((dp * self.nz + z, (g * self.pair + c) * self.nz + s))
        return pairs

    def hop(self, value, target):
        return lax.ppermute(value, AXES, self.perm(target))

    def group_hop(self, value, bit):
        return self.hop(value, lambda g, c, z: (g ^ bit, c, z))

    def core_hop(self, value, r):
        return self.hop(value, lambda g, c, z: (g, c ^ r, z))

    def ring(self, value):
        return self.hop(value, lambda g, c, z: (g, c, (z + 1) % self.nz))

    def flat_hop(self, value, bit):
        return lax.ppermute(value, AXES, [(i, i ^ bit) for i in range(self.nd * self.nz)])

    def head_owner_perm(self):
        pairs = []
        for r in range(self.nd * self.nz):
            head, quarter = r // self.groups, r % self.groups
            s, c = head // self.pair, head % self.pair
            pairs.append((r, ((quarter ^ s) * self.pair + c) * self.nz + s))
        return pairs


def after(values, *deps):
    flat, tree = jax.tree.flatten((values, deps))
    return jax.tree.unflatten(tree, lax.optimization_barrier(flat))[0]


def join(*values):
    return after(values)


def bits_of(count, descending):
    bits = []
    bit = 1
    while bit < count:
        bits.append(bit)
        bit *= 2
    return bits[::-1] if descending else bits


class GroupGather:
    def __init__(self, lay, block, descending):
        self.lay = lay
        self.rows = block.shape[0]
        self.held = {0: (block, 0)}
        self.rounds = [[] for _ in bits_of(lay.groups, False)]
        known = [0]
        for bit in bits_of(lay.groups, descending):
            for m in list(known):
                self.rounds[bin(m).count("1")].append((m, bit))
                known.append(m ^ bit)

    def block(self, m):
        array, first = self.held[m]
        return array[first : first + self.rows]

    def send(self, depth):
        if depth < len(self.rounds):
            for m, bit in self.rounds[depth]:
                self.held[m ^ bit] = (self.lay.group_hop(self.block(m), bit), 0)

    @staticmethod
    def stack(halves):
        return jnp.concatenate([h.block(0) for h in halves])

    @staticmethod
    def send_first(halves, stack):
        lay = halves[0].lay
        for bit in bits_of(lay.groups, False):
            got = lay.group_hop(stack, bit)
            first = 0
            for h in halves:
                h.held[bit] = (got, first)
                first += h.rows

    @property
    def state(self):
        return {m: v for m, (v, _) in self.held.items()}

    @state.setter
    def state(self, state):
        for m, v in state.items():
            self.held[m] = (v, self.held[m][1])

    def rest(self, depth):
        while depth < len(self.rounds):
            self.send(depth)
            depth += 1
        return self.held


class GroupScatter:
    def __init__(self, lay, keep, send, descending):
        self.lay = lay
        self.keep, self.send = keep, send
        self.bits = bits_of(lay.groups, descending)
        self.at = 0

    @staticmethod
    def member(lay, index, descending):
        bits = bits_of(lay.groups, descending)
        return sum(bit for j, bit in enumerate(bits) if index >> (len(bits) - 1 - j) & 1)

    @property
    def state(self):
        return (self.keep, self.send)

    @state.setter
    def state(self, state):
        self.keep, self.send = state

    def step(self):
        if self.at < len(self.bits):
            self.send = self.lay.group_hop(self.send, self.bits[self.at])
            self.at += 1

    def fold(self):
        total = self.keep.astype(f32) + self.send.astype(f32)
        half = total.shape[0] // 2
        self.keep, self.send = total[:half], total[half:].astype(bf16)

    def result(self):
        return (self.keep.astype(f32) + self.send.astype(f32))[0]


def cast_kernel(c_ref, *refs):
    out_ref = refs[-1]
    at = 0
    for ref in refs[:-1]:
        value = ref[...].astype(bf16)
        if value.shape[1] < LANES:
            value = jnp.pad(value, ((0, 0), (0, LANES - value.shape[1])))
        out_ref[0, :, at : at + value.shape[1]] = value
        at += value.shape[1]


def prepare(lay, r, sources):
    rows, pair, nz = sources[0][0].shape[0], lay.pair, lay.nz

    def spec(first, width):
        if first is None:
            return pl.BlockSpec((rows, width), lambda z, c: (0, 0))
        return pl.BlockSpec((rows, width), lambda z, c: (0, first + z * pair + (c[0] ^ r)))

    total = sum(max(width, LANES) for _, _, width in sources)
    return pl.pallas_call(
        cast_kernel,
        grid_spec=pltpu.PrefetchScalarGridSpec(
            num_scalar_prefetch=1,
            grid=(nz,),
            in_specs=[spec(first, width) for _, first, width in sources],
            out_specs=pl.BlockSpec((1, rows, total), lambda z, c: (z, 0, 0)),
        ),
        out_shape=jax.ShapeDtypeStruct((nz, rows, total), bf16),
        name="prepare",
        **params((rows * total * nz, rows * total * nz * 6)),
    )(jnp.reshape(lay.c, (1,)).astype(jnp.int32), *[v for v, _, _ in sources])


def place_kernel(count, tile, slot_ref, *refs):
    out_ref, sems = refs[-2], refs[-1]
    here = pl.ds(pl.multiple_of(pl.program_id(0) * tile, tile), tile)

    def copy(i):
        return pltpu.make_async_copy(refs[i], out_ref.at[slot_ref[i], here], sems.at[i])

    for i in range(count):

        @pl.when(slot_ref[i] >= 0)
        def _(i=i):
            copy(i).start()

    for i in range(count):

        @pl.when(slot_ref[i] >= 0)
        def _(i=i):
            copy(i).wait()


def place(blocks, slots, rows, total, held=None):
    count = len(blocks)
    width = blocks[0][0].shape[1]
    tile = rows if count * rows * width <= 2**21 else max(min(64, rows), rows // 2)
    operands = [v for v, _ in blocks] + ([] if held is None else [held])
    any_spec = pl.BlockSpec(memory_space=pl.ANY)
    return pl.pallas_call(
        partial(place_kernel, count, tile),
        grid_spec=pltpu.PrefetchScalarGridSpec(
            num_scalar_prefetch=1,
            grid=(rows // tile,),
            in_specs=[
                pl.BlockSpec(
                    (tile, width),
                    lambda i, slot, first=first, j=j: (
                        first // tile + jnp.where(slot[j] >= 0, i, 0),
                        0,
                    ),
                )
                for j, (_, first) in enumerate(blocks)
            ]
            + [any_spec] * (len(operands) - count),
            out_specs=any_spec,
            scratch_shapes=[pltpu.SemaphoreType.DMA((count,))],
        ),
        out_shape=jax.ShapeDtypeStruct((total, rows, width), blocks[0][0].dtype),
        input_output_aliases={} if held is None else {count + 1: 0},
        name="place",
        **params((count, 4 * count * rows * width)),
    )(jnp.stack([jnp.asarray(v, jnp.int32) for v in slots]), *operands)


def flip_kernel(in_ref, out_ref):
    out_ref[...] = in_ref[...].astype(f32).T


def last_columns(array):
    rows, total = array.shape
    return pl.pallas_call(
        flip_kernel,
        grid=(1,),
        in_specs=[pl.BlockSpec((rows, LANES), lambda i: (0, total // LANES - 1))],
        out_specs=pl.BlockSpec((LANES, rows), lambda i: (0, 0)),
        out_shape=jax.ShapeDtypeStruct((LANES, rows), f32),
        name="last_columns",
        **params(),
    )(array)


def block_order(lay):
    order = []
    for part in (1, 0):
        for r in range(lay.pair):
            for i in range(lay.groups // 2):
                m = GroupScatter.member(lay, part * (lay.groups // 2) + i, bool(r))
                order.append((lay.g ^ m) * lay.pair + (lay.c ^ r))
    return jnp.stack(order).astype(jnp.int32)


def write_block(half, outs, at, value):
    i = pl.program_id(0)
    for k, out in enumerate(outs):

        @pl.when(jnp.logical_and(i >= k * half, i < (k + 1) * half))
        def _(out=out):
            out[0, :, at : at + value.shape[1]] = value


def gradient_kernel(half, block_ref, left_ref, right_ref, *outs):
    write_block(half, outs, 0, dot(left_ref[...], right_ref[...], 0, 0).astype(bf16))


def folded_kernel(half, first, gain, rides, block_ref, x_ref, right_ref, sums_ref, w_ref, small_ref, *refs):
    others, outs = (refs[:2], refs[2:]) if rides else ((), refs[:-1])
    vec = small_ref[...].astype(f32)
    raw = dot(x_ref[...], right_ref[...], 0, 0)
    sums = sums_ref[0:1]
    grad = raw * vec[:, gain : gain + 1] + sums * vec[:, gain + 1 : gain + 2]
    write_block(half, outs, 0, grad.astype(bf16))
    w = w_ref[:, first : first + raw.shape[1]].astype(f32)
    lane = lax.broadcasted_iota(jnp.int32, vec.shape, 1)
    moment = jnp.sum(w * raw, axis=1, keepdims=True)
    plain = jnp.sum(w * sums, axis=1, keepdims=True)
    lanes = jnp.where(lane == gain, moment, jnp.where(lane == gain + 1, plain, 0.0))
    if rides:
        lanes = lanes + others[0][...] + others[1][...]
        write_block(half, outs, raw.shape[1], lanes.astype(bf16))
    else:
        refs[-1][...] = lanes


def columns_kernel(unit, hd, t_ref, dy_ref, du_ref, *refs):
    out_ref = refs[-1]
    width = out_ref.shape[0]
    t = t_ref[0]
    place = lax.broadcasted_iota(jnp.int32, (1, width), 1)
    dy = jnp.sum(dy_ref[...].astype(f32), axis=0, keepdims=True)
    dp = sum(jnp.sum(ref[:, 0], axis=0, keepdims=True) for ref in refs[:-1])
    blank = jnp.zeros((1, width), f32)
    rows = [blank] * 4 + [dy, dy]
    for j in range(3):
        head = jnp.concatenate([dp[:, j * hd : (j + 1) * hd]] * (width // hd), axis=1)
        rows.append(jnp.where(place // hd == t, head, 0.0))
    share = width // unit
    units = jnp.concatenate([du_ref[0:1]] * share, axis=1)
    for k in range(HEADS // share):
        rows.append(jnp.where(place // unit + k * share == t, units, 0.0))
    rows += [blank] * (LANES - len(rows))
    out_ref[...] = jnp.concatenate(rows).T


def plain_columns(lay, dy, du_sums, dp_sums, unit, hd):
    tokens, width = dy.shape

    def whole(v):
        return pl.BlockSpec(v.shape, lambda i, t: (0,) * v.ndim)

    return pl.pallas_call(
        partial(columns_kernel, unit, hd),
        grid_spec=pltpu.PrefetchScalarGridSpec(
            num_scalar_prefetch=1,
            grid=(1,),
            in_specs=[whole(v) for v in (dy, du_sums, *dp_sums)],
            out_specs=pl.BlockSpec((width, LANES), lambda i, t: (0, 0)),
        ),
        out_shape=jax.ShapeDtypeStruct((width, LANES), f32),
        name="plain_columns",
        **params((tokens * width, 4 * tokens * width)),
    )(jnp.reshape(lay.t, (1,)).astype(jnp.int32), dy, du_sums, *dp_sums)


def gradient_call(lay, kernel, left, rights, by_rows, n, more=()):
    tokens, width = left.shape
    pair, half = lay.pair, lay.groups // 2
    rows = width // (lay.groups * pair)
    outs = 2 * pair

    def out_map(k):
        return lambda i, block: (jnp.clip(i - k * half, 0, half - 1), 0, 0)

    def row_map(column):
        return lambda i, block: (block[i], column)

    values = pl.pallas_call(
        partial(kernel, half),
        grid_spec=pltpu.PrefetchScalarGridSpec(
            num_scalar_prefetch=1,
            grid=(outs * half,),
            in_specs=[pl.BlockSpec((tokens, rows), lambda i, block: (0, block[i]))]
            + [pl.BlockSpec(v.shape, lambda i, block: (0, 0)) for v in rights]
            + [pl.BlockSpec((rows, size), row_map(column)) for _, size, column in by_rows],
            out_specs=[pl.BlockSpec((1, rows, n), out_map(k)) for k in range(outs)]
            + [pl.BlockSpec((rows, size), row_map(0)) for size in more],
        ),
        out_shape=[jax.ShapeDtypeStruct((half, rows, n), bf16)] * outs
        + [jax.ShapeDtypeStruct((width, size), f32) for size in more],
        name="gradient",
        **params((2 * tokens * width * n, 2 * (tokens * width + tokens * n + width * n))),
    )(block_order(lay), left, *rights, *[v for v, _, _ in by_rows])
    parts = [GroupScatter(lay, values[pair + r], values[r], bool(r)) for r in range(pair)]
    return (parts, *values[outs:])


def gradient(lay, left, right):
    return gradient_call(lay, gradient_kernel, left, [right], [], right.shape[1])[0]


def folded_gradient(lay, x, right, sums, w_qu, first, gain, others=()):
    total = w_qu.shape[1]
    by_rows = [(w_qu, total, 0), (w_qu, LANES, total // LANES - 1)]
    by_rows += [(v, LANES, 0) for v in others]
    rides = len(others) > 0

    def call(half, *refs):
        folded_kernel(half, first, gain, rides, *refs)

    n = right.shape[1] + (LANES if rides else 0)
    return gradient_call(lay, call, x, [right, sums], by_rows, n, () if rides else (LANES,))


def fold_kernel(*refs):
    count = len(refs) // 4
    for p in range(count):
        keep, got, next_keep, next_send = refs[p], refs[count + p], refs[2 * count + p], refs[3 * count + p]
        half = next_keep.shape[0]
        total = keep[...].astype(f32) + got[...].astype(f32)
        next_keep[...] = total[:half]
        next_send[...] = total[half:].astype(bf16)


def fold(parts):
    held, rows, n = parts[0].keep.shape
    half = held // 2
    tile = min(128, rows)
    full = pl.BlockSpec((held, tile, n), lambda i: (0, i, 0))
    part = pl.BlockSpec((half, tile, n), lambda i: (0, i, 0))
    count = len(parts)
    values = pl.pallas_call(
        fold_kernel,
        grid=(rows // tile,),
        in_specs=[full] * (2 * count),
        out_specs=[part] * (2 * count),
        out_shape=[jax.ShapeDtypeStruct((half, rows, n), f32)] * count
        + [jax.ShapeDtypeStruct((half, rows, n), bf16)] * count,
        name="fold",
        **params((held * rows * n, 8 * held * rows * n)),
    )(*[p.keep for p in parts], *[p.send for p in parts])
    for k, p in enumerate(parts):
        p.keep, p.send = values[k], values[count + k]


def blocks_kernel(count, *refs):
    out_ref = refs[-1]
    places, _, rows, _ = out_ref.shape
    for p in range(count):
        total = (refs[p][0].astype(f32) + refs[count + p][0].astype(f32)).astype(bf16)
        for z in range(places):
            out_ref[z, p] = total[z * rows : (z + 1) * rows]


def final_blocks(parts, nz):
    _, total, n = parts[0].keep.shape
    rows, count = total // nz, len(parts)
    steps = nz // 2 if nz % 2 == 0 else nz
    places = nz // steps
    return pl.pallas_call(
        partial(blocks_kernel, count),
        grid=(steps,),
        in_specs=[pl.BlockSpec((1, places * rows, n), lambda i: (0, i, 0))] * (2 * count),
        out_specs=pl.BlockSpec((places, count, rows, n), lambda i: (i, 0, 0, 0)),
        out_shape=jax.ShapeDtypeStruct((nz, count, rows, n), bf16),
        name="final_blocks",
        **params((count * total * n, 8 * count * total * n)),
    )(*[p.keep for p in parts], *[p.send for p in parts])


def chunk_kernel(count, ways, slot_ref, *refs):
    for k in range(ways):

        @pl.when(slot_ref[k] >= 0)
        def _(k=k):
            total = sum(refs[k * count + p][...].astype(f32) for p in range(count))
            out = refs[-ways + k]
            out[...] = total.astype(out.dtype)


def chunk_sums(parts, slots, received):
    count, _, span, width = parts[0].shape
    tile = min(span, 128)
    ways = len(slots)

    def whole(k):
        return lambda i, slot: (0, jnp.where(slot[k] >= 0, i, 0), 0)

    def part(k):
        return lambda i, slot: (0, jnp.maximum(slot[k], 0), jnp.where(slot[k] >= 0, i, 0), 0)

    in_specs, operands = [], []
    for k in range(ways):
        for p in parts:
            in_specs.append(pl.BlockSpec((count, None, tile, width), part(k)))
            operands.append(p)
        if received:
            in_specs.append(pl.BlockSpec((count, tile, width), whole(k)))
            operands.append(received[k])
    shape = jax.ShapeDtypeStruct((count, span, width), bf16)
    return pl.pallas_call(
        partial(chunk_kernel, len(operands) // ways, ways),
        grid_spec=pltpu.PrefetchScalarGridSpec(
            num_scalar_prefetch=1,
            grid=(span // tile,),
            in_specs=in_specs,
            out_specs=[pl.BlockSpec((count, tile, width), whole(k)) for k in range(ways)],
        ),
        out_shape=[shape] * ways,
        name="chunk_sums",
        **params((8 * count * span * width, 16 * count * span * width)),
    )(jnp.stack(slots).astype(jnp.int32), *operands)


def turn(values, cosine, low_sine, high_sine, quarter):
    head = values[:, :LANES]
    turned = (
        head * cosine
        + pltpu.roll(head, LANES - quarter, 1) * low_sine
        + pltpu.roll(head, quarter, 1) * high_sine
    )
    return jnp.concatenate([turned, values[:, LANES:]], axis=1)


def piece_kernel(pair, places, quarter, pos_ref, *refs):
    x_refs, refs = refs[: pair * places], refs[pair * places :]
    for p in range(places):

        @pl.when(pl.program_id(1) == p)
        def _(p=p):
            piece_rows(pair, quarter, x_refs[p * pair : (p + 1) * pair], refs)


def piece_rows(pair, quarter, x_refs, refs):
    vec_ref, w_ref, qkv_bias_ref, up_bias_ref, tab_ref = refs[:5]
    x_out, qkv_out, g_out, slope_out = refs[-4:]
    tile = x_refs[0].shape[1]
    unit, wide = g_out.shape[-1], qkv_out.shape[-1]
    hd = wide // 3
    x = jnp.concatenate([ref[0].astype(f32) for ref in x_refs])
    normed, _ = normalize(x)
    a = (normed * vec_ref[0:1] + vec_ref[1:2]).astype(bf16)
    m = (normed * vec_ref[2:3] + vec_ref[3:4]).astype(bf16)
    cosine, low_sine, high_sine = (jnp.concatenate([tab_ref[k]] * pair) for k in range(3))

    def put(out, at, value):
        value = value.astype(bf16)
        for r in range(pair):
            out[r, 0, 0, :, at : at + value.shape[1]] = value[r * tile : (r + 1) * tile]

    put(x_out, 0, normed)
    for j in range(3):
        part = dot(a, w_ref[:, unit + j * hd : unit + (j + 1) * hd])
        part = part + qkv_bias_ref[0:1, j * hd : (j + 1) * hd]
        put(qkv_out, j * hd, turn(part, cosine, low_sine, high_sine, quarter) if j < 2 else part)
    u = dot(m, w_ref[:, :unit]) + up_bias_ref[0:1]
    half = 0.5 * (1.0 + lax.erf(u * (0.5**0.5)))
    put(g_out, 0, u * half)
    put(slope_out, 0, half + u * (jnp.exp(-0.5 * u * u) * 0.3989422804014327))


def piece_forward(lay, pieces, where, vec, w_qu, qkv_bias, up_bias, tables, held):
    count, span, width = pieces[0].shape
    pair, nz, places = lay.pair, lay.nz, len(where)
    unit, wide = up_bias.shape[1], qkv_bias.shape[1]
    tile = min(span, 128)
    steps = span // tile

    def out(n):
        return (
            jax.ShapeDtypeStruct((pair, count, nz, span, n), bf16),
            pl.BlockSpec((pair, 1, 1, tile, n), lambda i, p, j, pos: (0, i, pos[p], j, 0)),
        )

    def whole(v):
        return pl.BlockSpec(v.shape, lambda i, p, j, pos: (0,) * v.ndim)

    def row_map(q):
        return lambda i, p, j, pos: (i, jnp.where(p == q, j, jnp.where(p < q, 0, steps - 1)), 0)

    outs = [out(n) for n in (width, wide, unit, unit)]
    in_specs = [pl.BlockSpec((1, tile, width), row_map(q)) for q in range(places) for _ in range(pair)]
    in_specs += [pl.BlockSpec((8, width), lambda i, p, j, pos: (0, 0))]
    in_specs += [whole(v) for v in (w_qu, qkv_bias, up_bias)]
    in_specs += [pl.BlockSpec((3, tile, LANES), lambda i, p, j, pos: (0, pos[p] * steps + j, 0))]
    in_specs += [pl.BlockSpec(memory_space=pl.ANY)] * len(held)
    tokens = pair * places * count * span
    return pl.pallas_call(
        partial(piece_kernel, pair, places, wide // 24),
        grid_spec=pltpu.PrefetchScalarGridSpec(
            num_scalar_prefetch=1,
            grid=(count, places, steps),
            in_specs=in_specs,
            out_specs=[o[1] for o in outs],
        ),
        out_shape=[o[0] for o in outs],
        input_output_aliases={pair * places + 6 + k: k for k in range(len(held))},
        name="piece_forward",
        **params((2 * tokens * width * (unit + wide), 12 * tokens * width)),
    )(
        jnp.stack(where).astype(jnp.int32),
        *pieces,
        vec,
        w_qu,
        qkv_bias,
        up_bias,
        tables,
        *held,
    )


def attn_fwd_kernel(scale, tile, qkv_ref, o_ref, lse_ref):
    length, hd = o_ref.shape[1:]
    for i in range(length // tile):
        end = (i + 1) * tile
        q_i = qkv_ref[0, i * tile : end, :hd]
        scores = dot(q_i, qkv_ref[0, :end, hd : 2 * hd], 1, 1) * scale
        row = lax.broadcasted_iota(jnp.int32, scores.shape, 0) + i * tile
        col = lax.broadcasted_iota(jnp.int32, scores.shape, 1)
        scores = jnp.where(col <= row, scores, masked_value)
        row_max = jnp.max(scores, axis=1, keepdims=True)
        terms = jnp.exp(scores - row_max)
        row_sum = jnp.sum(terms, axis=1, keepdims=True)
        probs = (terms / row_sum).astype(bf16)
        o_ref[0, i * tile : end] = dot(probs, qkv_ref[0, :end, 2 * hd :]).astype(bf16)
        lse_ref[0, i * tile : end] = jnp.broadcast_to(row_max + jnp.log(row_sum), (tile, LANES))


def attn_forward(qkv, scale):
    seqs, length, wide = qkv.shape
    hd = wide // 3
    return pl.pallas_call(
        partial(attn_fwd_kernel, scale, min(512, length)),
        grid=(seqs,),
        in_specs=[pl.BlockSpec((1, length, wide), lambda s: (s, 0, 0))],
        out_specs=[
            pl.BlockSpec((1, length, hd), lambda s: (s, 0, 0)),
            pl.BlockSpec((1, length, LANES), lambda s: (s, 0, 0)),
        ],
        out_shape=[
            jax.ShapeDtypeStruct((seqs, length, hd), bf16),
            jax.ShapeDtypeStruct((seqs, length, LANES), f32),
        ],
        name="attn_forward",
        **params((4 * seqs * length * length * hd, 8 * seqs * length * wide)),
    )(qkv)


def attn_bwd_kernel(quarter, scale, tile, dy_ref, wo_ref, qkv_ref, lse_ref, tab_ref, *refs):
    dp_ref, sum_ref, do_s, dk_s, dv_s = refs[-5:]
    length = dy_ref.shape[1]
    hd = wo_ref.shape[0]
    cosine, low_sine, high_sine = tab_ref[0], -tab_ref[1], -tab_ref[2]
    do_s[...] = dot(dy_ref[0], wo_ref[...], 1, 1).astype(bf16)
    steps = length // tile
    for i in reversed(range(steps)):
        end = (i + 1) * tile
        q_i = qkv_ref[0, i * tile : end, :hd]
        k = qkv_ref[0, :end, hd : 2 * hd]
        do_i = do_s[i * tile : end]
        scores = dot(q_i, k, 1, 1) * scale
        row = lax.broadcasted_iota(jnp.int32, scores.shape, 0) + i * tile
        col = lax.broadcasted_iota(jnp.int32, scores.shape, 1)
        probs = jnp.where(col <= row, jnp.exp(scores - lse_ref[0, i * tile : end, 0:1]), 0.0)
        probs_grad = dot(do_i, qkv_ref[0, :end, 2 * hd :], 1, 1)
        row_dot = jnp.sum(probs * probs_grad, axis=1, keepdims=True)
        score_grad = (probs * (probs_grad - row_dot)).astype(bf16)
        dq = dot(score_grad, k) * scale
        dp_ref[0, i * tile : end, :hd] = turn(
            dq,
            cosine[i * tile : end],
            low_sine[i * tile : end],
            high_sine[i * tile : end],
            quarter,
        ).astype(bf16)
        dk = dot(score_grad, q_i, 0, 0)
        dv = dot(probs.astype(bf16), do_i, 0, 0)
        if i == steps - 1:
            dk_s[...] = dk
            dv_s[...] = dv
        else:
            dk_s[:end] += dk
            dv_s[:end] += dv
    dp_ref[0, :, hd : 2 * hd] = turn(
        dk_s[...] * scale, cosine, low_sine, high_sine, quarter
    ).astype(bf16)
    dp_ref[0, :, 2 * hd :] = dv_s[...].astype(bf16)
    total = jnp.sum(dp_ref[0].astype(f32), axis=0, keepdims=True)
    sum_ref[0] = jnp.broadcast_to(total, sum_ref.shape[1:])


def attn_backward(dy, w_out, qkv, lse, tables, scale, part, parts, held):
    seqs, length, width = dy.shape
    hd = w_out.shape[0]
    share = seqs // parts
    first = part * share
    flops = 2 * share * length * (hd * width + 5 * length * hd)

    def row_map(s):
        return (first + s, 0, 0)

    return pl.pallas_call(
        partial(attn_bwd_kernel, hd // 8, scale, min(512, length)),
        grid=(share,),
        in_specs=[
            pl.BlockSpec((1, length, width), row_map),
            pl.BlockSpec(w_out.shape, lambda s: (0, 0)),
            pl.BlockSpec((1, length, 3 * hd), row_map),
            pl.BlockSpec((1, length, LANES), row_map),
            pl.BlockSpec(tables.shape, lambda s: (0, 0, 0)),
        ]
        + [pl.BlockSpec(memory_space=pl.ANY)] * len(held),
        out_specs=[
            pl.BlockSpec((1, length, 3 * hd), row_map),
            pl.BlockSpec((1, 8, 3 * hd), lambda s: (s, 0, 0)),
        ],
        out_shape=[
            jax.ShapeDtypeStruct((seqs, length, 3 * hd), bf16),
            jax.ShapeDtypeStruct((share, 8, 3 * hd), f32),
        ],
        input_output_aliases={5 + k: k for k in range(len(held))},
        scratch_shapes=[
            pltpu.VMEM((length, hd), bf16),
            pltpu.VMEM((length, hd), f32),
            pltpu.VMEM((length, hd), f32),
        ],
        name="attn_backward",
        **params((flops, 8 * share * length * width)),
    )(dy, w_out, qkv, lse, tables, *held)


def write_chunk(outs, more, total):
    for ref in more:
        total = total + ref[0].astype(f32)
    total = total.astype(bf16)
    if len(outs) == 1:
        outs[0][0] = total
    else:
        for k, out in enumerate(outs):

            @pl.when(pl.program_id(0) == k)
            def _(out=out):
                out[0] = total


def chunk_outputs(order_len, span, width, separate):
    if separate:
        specs = [pl.BlockSpec((1, span, width), lambda i, order: (0, 0, 0))] * order_len
        return specs, [jax.ShapeDtypeStruct((1, span, width), bf16)] * order_len
    specs = [pl.BlockSpec((1, span, width), lambda i, order: (i, 0, 0))]
    return specs, [jax.ShapeDtypeStruct((order_len, span, width), bf16)]


def output_kernel(count, order_ref, g_ref, wd_ref, o_ref, wo_ref, *refs):
    total = dot(g_ref[...], wd_ref[...], 1, 1) + dot(o_ref[...], wo_ref[...])
    write_chunk(refs[count:], refs[:count], total)


def output_forward(g, w_down, o, w_out, span, order, first, more=(), separate=False):
    unit, width, hd = g.shape[1], w_down.shape[0], o.shape[1]
    steps = order.shape[0]
    out_specs, out_shape = chunk_outputs(steps, span, width, separate)
    return pl.pallas_call(
        partial(output_kernel, len(more)),
        grid_spec=pltpu.PrefetchScalarGridSpec(
            num_scalar_prefetch=1,
            grid=(steps,),
            in_specs=[
                pl.BlockSpec((span, unit), lambda i, order: (first + order[i], 0)),
                pl.BlockSpec(w_down.shape, lambda i, order: (0, 0)),
                pl.BlockSpec((span, hd), lambda i, order: (first + order[i], 0)),
                pl.BlockSpec(w_out.shape, lambda i, order: (0, 0)),
            ]
            + [pl.BlockSpec((1, span, width), lambda i, order: (i, 0, 0))] * len(more),
            out_specs=out_specs,
        ),
        out_shape=out_shape,
        name="output_forward",
        **params((2 * steps * span * width * (unit + hd), 8 * steps * span * width)),
    )(order, g, w_down, o, w_out, *more)


def hidden_kernel(dy_ref, wd_ref, slope_ref, du_ref, sum_ref):
    dg = dot(dy_ref[...], wd_ref[...])
    du_ref[...] = (dg * slope_ref[...].astype(f32)).astype(bf16)
    total = jnp.sum(du_ref[...].astype(f32), axis=0, keepdims=True)
    total = jnp.broadcast_to(total, sum_ref.shape)

    @pl.when(pl.program_id(0) == 0)
    def _():
        sum_ref[...] = total

    @pl.when(pl.program_id(0) > 0)
    def _():
        sum_ref[...] += total


def hidden_backward(dy, w_down, slope, tile):
    tokens, width = dy.shape
    unit = w_down.shape[1]
    return pl.pallas_call(
        hidden_kernel,
        grid=(tokens // tile,),
        in_specs=[
            pl.BlockSpec((tile, width), lambda i: (i, 0)),
            pl.BlockSpec(w_down.shape, lambda i: (0, 0)),
            pl.BlockSpec((tile, unit), lambda i: (i, 0)),
        ],
        out_specs=[
            pl.BlockSpec((tile, unit), lambda i: (i, 0)),
            pl.BlockSpec((8, unit), lambda i: (0, 0)),
        ],
        out_shape=[
            jax.ShapeDtypeStruct((tokens, unit), bf16),
            jax.ShapeDtypeStruct((8, unit), f32),
        ],
        name="hidden_backward",
        **params((2 * tokens * width * unit, 6 * tokens * width)),
    )(dy, w_down, slope)


def input_kernel(count, hd, order_ref, du_ref, dp_ref, wu_ref, wq_ref, wk_ref, wv_ref, vec_ref, *refs):
    da = (
        dot(dp_ref[:, :hd], wq_ref[...], 1, 1)
        + dot(dp_ref[:, hd : 2 * hd], wk_ref[...], 1, 1)
        + dot(dp_ref[:, 2 * hd :], wv_ref[...], 1, 1)
    )
    dm = dot(du_ref[...], wu_ref[...], 1, 1)
    write_chunk(refs[count:], refs[:count], da * vec_ref[0:1] + dm * vec_ref[2:3])


def input_backward(du, dp, w_qu, vec, span, order, first, more=(), separate=False):
    unit, width, hd = du.shape[1], w_qu.shape[0], dp.shape[1] // 3
    columns = unit // hd
    steps = order.shape[0]
    out_specs, out_shape = chunk_outputs(steps, span, width, separate)
    return pl.pallas_call(
        partial(input_kernel, len(more), hd),
        grid_spec=pltpu.PrefetchScalarGridSpec(
            num_scalar_prefetch=1,
            grid=(steps,),
            in_specs=[
                pl.BlockSpec((span, unit), lambda i, order: (first + order[i], 0)),
                pl.BlockSpec((span, 3 * hd), lambda i, order: (first + order[i], 0)),
                pl.BlockSpec((width, unit), lambda i, order: (0, 0)),
            ]
            + [pl.BlockSpec((width, hd), lambda i, order, j=j: (0, columns + j)) for j in range(3)]
            + [pl.BlockSpec((8, width), lambda i, order: (0, 0))]
            + [pl.BlockSpec((1, span, width), lambda i, order: (i, 0, 0))] * len(more),
            out_specs=out_specs,
        ),
        out_shape=out_shape,
        name="input_backward",
        **params((2 * steps * span * width * (unit + 3 * hd), 12 * steps * span * width)),
    )(order, du, dp, w_qu, w_qu, w_qu, w_qu, vec, *more)


def adam_kernel(pair, places, rate, c_ref, *refs):
    g_refs, (w_ref, m_ref, v_ref), outs = refs[:pair], refs[pair : pair + 3], refs[-4:]
    pieces = []
    for z in range(places):
        parts = [ref[z].astype(f32) for ref in g_refs]
        if pair == 2:
            swapped = c_ref[0] == 1
            parts = [jnp.where(swapped, parts[1], parts[0]), jnp.where(swapped, parts[0], parts[1])]
        pieces += parts
    grad = pieces[0] if len(pieces) == 1 else jnp.concatenate(pieces, axis=1)
    result = adamw(w_ref[...], grad, m_ref[...], v_ref[...], rate)
    for ref, value in zip(outs, result, strict=True):
        ref[...] = value


def adam_columns(lay, rate, parts, at, piece, state, start, kinds, held):
    nz, rows, _ = parts[0].shape
    pair = len(parts)
    total = state[0].shape[1]
    places = max(1, min(nz, 1024 // (pair * piece)))
    wide = places * pair * piece
    steps = nz // places
    first = start // wide

    w_spec = pl.BlockSpec((rows, wide), lambda j, z, c: (0, first + j * steps + z))
    g_spec = pl.BlockSpec((places, rows, piece), lambda j, z, c: (z, 0, at // piece + j))
    operands = list(parts) + list(state) + list(held)
    return pl.pallas_call(
        partial(adam_kernel, pair, places, rate),
        grid_spec=pltpu.PrefetchScalarGridSpec(
            num_scalar_prefetch=1,
            grid=(kinds, steps),
            in_specs=[g_spec] * pair
            + [w_spec] * 3
            + [pl.BlockSpec(memory_space=pl.ANY)] * len(held),
            out_specs=[w_spec] * 4,
        ),
        out_shape=[jax.ShapeDtypeStruct((rows, total), f32)] * 4,
        input_output_aliases={1 + pair + 3 + k: k for k in range(len(held))},
        name="adam_columns",
        **params((30 * rows * kinds * piece * HEADS, 30 * rows * kinds * piece * HEADS)),
    )(jnp.reshape(lay.c, (1,)).astype(jnp.int32), *operands)


class SeqGather:
    def __init__(self, lay, own):
        self.lay = lay
        self.rounds, self.at = lay.nz - 1, 0
        self.newest = own
        self.places, self.fresh = [lay.z], [own]

    def step(self):
        self.at += 1
        self.newest = self.lay.ring(self.newest)
        self.fresh.append(self.newest)
        self.places.append((self.lay.z - self.at) % self.lay.nz)

    def take(self):
        items = list(zip(self.fresh, self.places))
        self.fresh, self.places = [], []
        return items

    @property
    def state(self):
        return (self.newest, self.fresh)

    @state.setter
    def state(self, state):
        self.newest, self.fresh = state


class TokenBuffer:
    def __init__(self, lay):
        self.lay, self.todo, self.out = lay, [], None

    def add(self, items):
        for pieces, where in items:
            for r, piece in enumerate(pieces):
                for s in range(piece.shape[0]):
                    self.todo.append((piece[s], (r * piece.shape[0] + s) * self.lay.nz + where))

    def flush(self, count):
        blocks, slots = [(v, 0) for v, _ in self.todo], [w for _, w in self.todo]
        total = self.lay.pair * self.lay.nz * count
        self.out = place(blocks, slots, blocks[0][0].shape[0], total, self.out)
        self.todo = []
        return self.out

    @property
    def state(self):
        return ([v for v, _ in self.todo], self.out)

    @state.setter
    def state(self, state):
        blocks, self.out = state
        self.todo = [(v, w) for v, (_, w) in zip(blocks, self.todo)]


class SeqScatter:
    def __init__(self, lay):
        self.lay = lay
        self.four = lay.nz == 4
        if self.four:
            roles = [[3, 2, 1, 0], [0, 2, 3, 1], [3, 1, 0, 2], [0, 1, 2, 3]]
        else:
            roles = [list(range(lay.nz))] * lay.nz
        self.order = jnp.array(roles, jnp.int32)[lay.z]

    def load(self, chunks):
        self.state = list(chunks)

    def move(self, value, targets):
        return self.lay.hop(value, lambda g, c, z: (g, c, targets[z]) if z in targets else None)

    def send(self):
        if not self.four:
            self.state = [lax.all_to_all(self.state[0], "seq", 0, 0, tiled=True)]
            return
        near, far, last, own = self.state
        near = self.move(near, {0: 1, 3: 2, 2: 3, 1: 0})
        across = self.move(far, {0: 2, 3: 1})
        beside = self.move(far, {1: 2, 2: 1})
        self.state = [near, across, beside, last, own]

    def finish(self):
        if not self.four:
            return
        near, across, beside, last, own = self.state
        inner = jnp.logical_and(self.lay.z > 0, self.lay.z < 3)
        passed = jnp.where(inner, last.astype(f32) + near.astype(f32), last.astype(f32)).astype(bf16)
        came = self.move(passed, {1: 3, 2: 0, 0: 1, 3: 2})
        self.state = [near, across, beside, came, own]

    def result(self):
        if not self.four:
            return jnp.sum(self.state[0].astype(f32), axis=0)
        near, across, beside, came, own = (v[0].astype(f32) for v in self.state)
        inner = jnp.logical_and(self.lay.z > 0, self.lay.z < 3)
        return own + came + jnp.where(inner, across + beside, near)


def body(
    inputs,
    cotangent,
    attn_params,
    attn_first,
    attn_second,
    mlp_params,
    mlp_first,
    mlp_second,
    small,
    small_first,
    small_second,
):
    lay = Layout(lax.axis_size("dp"), lax.axis_size("seq"))
    groups, nz, pair = lay.groups, lay.nz, lay.pair
    count, span, width = inputs.shape
    rows = attn_params.shape[0]
    ff = mlp_params.shape[1] // 2
    hd = width // HEADS
    unit = ff // HEADS
    rot_dims = hd // 4
    score_scale = hd ** (-0.5)
    first_row = (lay.dp * nz + lay.z) * rows
    seqs, length = count * pair, span * nz
    tokens_here = seqs * length

    qu_sources = [(mlp_params, 0, unit)]
    qu_sources += [(attn_params, j * HEADS, hd) for j in range(3)]
    qu_sources += [(small, None, small.shape[1])]
    dn_sources = [(mlp_params, HEADS, unit)]

    def swap(sources, r):
        blocks = prepare(lay, r, sources)
        return lay.core_hop(blocks, r) if r else blocks

    def exchange(half):
        return lax.all_to_all(half, "seq", 0, 0, tiled=True).reshape(nz * rows, -1)

    class Whole:
        def __init__(self, halves, size=None, first=0, turn=0):
            self.halves, self.seen, self.state = halves, set(), None
            self.size, self.first, self.turn = size or halves[0].rows, first, turn

        def flush(self):
            items = [
                (r, m, (v[0], v[1] + self.first))
                for r, half in enumerate(self.halves)
                for m, v in half.held.items()
                if (r, m) not in self.seen
            ]
            self.seen |= {(r, m) for r, m, _ in items}
            if items:
                count = len(self.halves)
                slots = [
                    (lay.g ^ m ^ self.turn) * count + (lay.c ^ r if count > 1 else 0)
                    for r, m, _ in items
                ]
                blocks = [v for _, _, v in items]
                self.state = place(blocks, slots, self.size, groups * count, self.state)

        def result(self):
            self.flush()
            return self.state.reshape(-1, self.state.shape[-1])

    def joined(parts, *values):
        *values, states = join(*values, [p.state for p in parts])
        for p, v in zip(parts, states):
            p.state = v
        return values

    def crossed(piece):
        return [piece] + [lay.core_hop(piece, r) for r in range(1, pair)]

    positions = jnp.arange(length, dtype=f32)
    frequency = 10000.0 ** (-(jnp.arange(rot_dims // 2, dtype=f32) * 2.0) / rot_dims)
    angles = positions[:, None] * frequency[None, :]
    cosine, sine = jnp.cos(angles), jnp.sin(angles)
    blank = jnp.zeros_like(sine)
    rest = jnp.zeros((length, LANES - rot_dims), f32)
    tables = jnp.stack(
        [
            jnp.concatenate([cosine, cosine, rest + 1.0], axis=1),
            jnp.concatenate([-sine, blank, rest], axis=1),
            jnp.concatenate([blank, sine, rest], axis=1),
        ]
    )

    first = exchange(swap(qu_sources, 0))
    rest = [swap(qu_sources, r) for r in range(1, pair)]
    w_out = attn_params[:, 3 * width :].astype(bf16)
    dn = jnp.stack([prepare(lay, r, dn_sources) for r in range(pair)], axis=1)
    w_out = lax.ppermute(w_out, AXES, lay.head_owner_perm())
    first, rest, w_out, dn, tables = join(first, rest, w_out, dn, tables)

    qu = [GroupGather(lay, first, False)]
    for r in range(1, pair):
        one = exchange(rest[r - 1])
        qu[-1].send(0)
        one, w_out, dn = joined(qu, one, w_out, dn)
        qu.append(GroupGather(lay, one, bool(r % 2)))
    dn = lax.all_to_all(dn, "seq", 0, 0, tiled=True)
    qu[-1].send(0)
    xs, dy, dy_buffer = SeqGather(lay, inputs), SeqGather(lay, cotangent), TokenBuffer(lay)

    def crossing(items):
        return [(crossed(v), place) for v, place in items]

    (own,) = crossing(xs.take())
    own_pieces, dn, w_out = joined(qu + [xs], own[0], dn, w_out)
    ready = [(own_pieces, own[1])]

    w_qu = Whole(qu)
    xs.step()
    dn = [lay.core_hop(dn[:, r], r) if r else dn[:, r] for r in range(pair)]
    dn = [v.reshape(nz * rows, unit) for v in dn]
    dn[-1] = jnp.concatenate([dn[-1], w_out.reshape(-1, unit)])
    dn = [GroupGather(lay, v, bool(r)) for r, v in enumerate(dn)]
    w_qu.flush()
    for v in qu:
        v.send(1)
    (dn_stack,) = joined(qu + dn + [w_qu, xs], GroupGather.stack(dn))
    for v in qu:
        v.rest(2)

    w_qkvu = w_qu.result()
    vectors = last_columns(w_qkvu)
    norm_vec = vectors
    qkv_bias = vectors[6:9].reshape(3, HEADS, hd)
    qkv_bias = lax.dynamic_index_in_dim(qkv_bias, lay.t, 1, keepdims=False).reshape(1, 3 * hd)
    up_bias = lax.dynamic_slice(vectors[9:13].reshape(-1), (lay.t * unit,), (unit,))[None]
    out_bias = vectors[4] + vectors[5]
    held = ()

    def forward_pieces(items, held):
        where = [place for _, place in items]
        pieces = [v for pieces, _ in items for v in pieces]
        return piece_forward(
            lay, pieces, where, norm_vec, w_qkvu, qkv_bias, up_bias, tables, held
        )

    w_dn, w_wo = Whole(dn, nz * rows), Whole(dn[-1:], rows * width // unit, nz * rows, lay.z)
    tick = 0
    while xs.at < xs.rounds:
        taken = xs.take()
        xs.step()
        if tick == 0:
            GroupGather.send_first(dn, dn_stack)
        elif tick == 1:
            w_dn.flush()
            w_wo.flush()
            for v in dn:
                v.send(1)
        held = forward_pieces(ready, held)
        ready = crossing(taken)
        ready_pieces, held = joined(dn + [w_dn, w_wo, xs], [v for v, _ in ready], held)
        ready = list(zip(ready_pieces, [place for _, place in ready]))
        tick += 1
    for v in dn:
        v.rest(2)

    taken = xs.take()
    own_dy = dy.take()
    dy.step()
    held = forward_pieces(ready + crossing(taken), held)
    dy_buffer.add(crossing(own_dy))
    (held,) = joined([dy, dy_buffer, w_dn, w_wo] + dn, held)
    w_down = w_dn.result()
    w_out = w_wo.result().reshape(hd, width)
    tile = min(512, length)
    flat = (tokens_here, width)
    x_flat, qkv, g, slope = (v.reshape(seqs, length, -1) for v in held)
    x_flat, g, slope = (v.reshape(tokens_here, -1) for v in (x_flat, g, slope))

    taken = dy.take()
    dy.step()
    dy_buffer.add(crossing(taken))
    o, lse = attn_forward(qkv, score_scale)
    o = o.reshape(tokens_here, hd)
    out_sum = SeqScatter(lay)
    parts = {}
    for r in range(1, pair):
        (parts[r],) = output_forward(g, w_down, o, w_out, span, out_sum.order, r * count * nz)
    o, lse, g, parts, w_down, w_out = joined([dy, dy_buffer], o, lse, g, parts, w_down, w_out)

    taken = dy.take()
    while dy.at < dy.rounds:
        dy.step()
    dy_buffer.flush(count)
    more = [lay.core_hop(parts[r], r) for r in range(1, pair)]
    dy_buffer.add(crossing(taken))
    out_sum.load(
        output_forward(g, w_down, o, w_out, span, out_sum.order, 0, more, separate=out_sum.four)
    )
    o, lse, g = joined([dy, dy_buffer, out_sum], o, lse, g)

    def steps(*parts):
        for p in parts:
            p.step()

    def to_owners(blocks):
        return lax.all_to_all(blocks, "seq", 0, 0, tiled=True)

    def at_owner(blocks):
        parts = [blocks[:, r] for r in range(pair)]
        return [lay.core_hop(v, r) if r else v for r, v in enumerate(parts)]

    def more_rounds(parts):
        while parts[0].at < len(parts[0].bits):
            if len(parts) == pair and parts[0].keep.shape[2] < width:
                fold(parts)
            else:
                for p in parts:
                    p.fold()
            steps(*parts)

    out_sum.send()
    dy_buffer.add(crossing(dy.take()))
    dy_all = dy_buffer.flush(count).reshape(seqs, length, width)
    down = gradient(lay, dy_all.reshape(flat), g)
    (dy_all,) = joined(down, dy_all)

    z_sum = SeqScatter(lay)
    dp, dp_sums, z_parts = (), {}, {}

    def attention_part(r, held):
        *held, dp_sums[r] = attn_backward(
            dy_all, w_out, qkv, lse, tables, score_scale, r, pair, held
        )
        return held

    def input_part(r, more=(), separate=False):
        return input_backward(
            du,
            dp[0].reshape(tokens_here, 3 * hd),
            w_qkvu,
            norm_vec,
            span,
            z_sum.order,
            r * count * nz,
            more,
            separate,
        )

    steps(*down)
    du, du_sums = hidden_backward(dy_all.reshape(flat), w_down, slope, tile)
    dy_all = after(dy_all, du)
    for r in range(1, pair):
        dp = attention_part(r, dp)
    dy_all, du, du_sums, dp, dp_sums = joined([out_sum] + down, dy_all, du, du_sums, dp, dp_sums)

    out_sum.finish()
    more_rounds(down)
    for r in range(1, pair):
        (z_parts[r],) = input_part(r)
    down_blocks = final_blocks(down, nz)
    dy_all, dp, z_parts, down_blocks = joined([out_sum], dy_all, dp, z_parts, down_blocks)

    for r in range(1, pair):
        z_parts[r] = lay.core_hop(z_parts[r], r)
    down_blocks = to_owners(down_blocks)
    dp = attention_part(0, dp)
    z_sum.load(input_part(0, [z_parts[r] for r in range(1, pair)], z_sum.four))
    dp = dp[0].reshape(tokens_here, 3 * hd)
    dy_flat, du, dp, dp_sums, down_blocks = joined(
        [z_sum], dy_all.reshape(flat), du, dp, dp_sums, down_blocks
    )

    z_sum.send()
    up, lanes = folded_gradient(lay, x_flat, du, du_sums, w_qkvu, 0, 2)
    dp, lanes = joined(up, dp, lanes)

    steps(*up)
    upstream = cotangent.astype(f32)
    flat_cotangent = cotangent.reshape(count * span, width)
    others = plain_columns(lay, flat_cotangent, du_sums, list(dp_sums.values()), unit, hd)
    dp_sums = sum(jnp.sum(v[:, 0], axis=0) for v in dp_sums.values())
    dp_sums = jnp.broadcast_to(dp_sums[None], (8, 3 * hd))
    (dqkv,) = folded_gradient(lay, x_flat, dp, dp_sums, w_qkvu, unit, 0, (lanes, others))
    dy_flat, upstream = joined(up + dqkv + [z_sum], dy_flat, upstream)

    z_sum.finish()
    more_rounds(up)
    steps(*dqkv)
    out_whole = dot(o, dy_flat, 0, 0)
    out_whole = out_whole.astype(bf16).reshape(groups, rows, width)
    out_whole = jnp.stack(
        [
            lax.dynamic_index_in_dim(
                out_whole, lay.g ^ lay.z ^ GroupScatter.member(lay, i, True), 0, keepdims=False
            )
            for i in range(groups)
        ]
    )
    wo = GroupScatter(lay, out_whole[: groups // 2], out_whole[groups // 2 :], True)
    up_blocks = final_blocks(up, nz)
    (up_blocks,) = joined([wo, z_sum, out_sum], up_blocks)

    mlp_state = (mlp_params, mlp_first, mlp_second)
    attn_state = (attn_params, attn_first, attn_second)
    up_blocks = to_owners(up_blocks)
    more_rounds(dqkv)
    steps(wo)
    dqkv_blocks = final_blocks(dqkv, nz)
    outputs = (inputs.astype(f32) + out_sum.result().reshape(inputs.shape) + out_bias).astype(bf16)
    up_blocks, dqkv_blocks, down_blocks, outputs = joined(
        [wo], up_blocks, dqkv_blocks, down_blocks, outputs
    )

    dqkv_blocks = to_owners(dqkv_blocks)
    more_rounds([wo])
    mlp_result = adam_columns(
        lay, rate_mlp, at_owner(down_blocks), 0, unit, mlp_state, ff, 1, ()
    )
    normed_grad = z_sum.result().reshape(inputs.shape)
    normed, scaling = normalize(inputs.astype(f32))
    grad_mean = jnp.mean(normed_grad, axis=-1, keepdims=True)
    grad_proj = jnp.mean(normed_grad * normed, axis=-1, keepdims=True)
    input_grad = upstream + scaling * (normed_grad - grad_mean - normed * grad_proj)
    up_parts = at_owner(up_blocks)
    mlp_result = adam_columns(lay, rate_mlp, up_parts, 0, unit, mlp_state, 0, 1, mlp_result)
    dqkv_blocks, mlp_result, input_grad = joined([wo], dqkv_blocks, mlp_result, input_grad)

    out_grad = wo.result().astype(bf16)
    out_grad = lax.ppermute(out_grad, AXES, [(b, a) for a, b in lay.head_owner_perm()])
    dqkv_parts = at_owner(dqkv_blocks)
    attn_result = adam_columns(lay, rate_attention, dqkv_parts, 0, hd, attn_state, 0, 3, ())
    at = 3 * hd
    small_grad = sum(
        jnp.sum(v[:, :, at : at + small.shape[1]].astype(f32), axis=0) for v in dqkv_parts
    )
    small_result = adamw(small, small_grad, small_first, small_second, rate_vector)
    out_grad = [out_grad[None]]
    attn_result = adam_columns(
        lay, rate_attention, out_grad, 0, width, attn_state, 3 * width, 1, attn_result
    )
    return (outputs, input_grad, *attn_result, *mlp_result, *small_result)


def solution(mesh):
    tokens, weights = P("dp", "seq", None), P(("dp", "seq"), None)
    return jax.shard_map(
        body,
        mesh=mesh,
        in_specs=(tokens,) * 2 + (weights,) * 9,
        out_specs=(tokens,) * 2 + (weights,) * 12,
        check_vma=False,
    )
```

```python
from functools import partial

import jax
import jax.numpy as jnp
from jax import lax
from jax.experimental import pallas as pl
from jax.experimental.pallas import tpu as pltpu
from jax.sharding import PartitionSpec as P

HEADS = 8
STEP = 10
AXES = ("dp", "seq")
LANES = 128
VMEM_LIMIT = 56 * 2**20

norm_eps = 1e-05
masked_value = -1e30
beta_first = 0.9
beta_second = 0.95
adam_eps = 1e-08
decay_rate = 0.01
rate_attention = 0.06
rate_mlp = 0.02
rate_vector = 0.2

f32 = jnp.float32
bf16 = jnp.bfloat16


def normalize(values):
    row_mean = jnp.mean(values, axis=-1, keepdims=True)
    centred = values - row_mean
    spread = jnp.mean(centred * centred, axis=-1, keepdims=True)
    scaling = lax.rsqrt(spread + norm_eps)
    return (centred * scaling, scaling)


def dot(left_op, right_op, left_dim=1, right_dim=0):
    return lax.dot_general(
        left_op,
        right_op,
        (((left_dim,), (right_dim,)), ((), ())),
        preferred_element_type=f32,
    )


def adamw(master, gradient, first_old, second_old, step_rate):
    first_new = beta_first * first_old + (1.0 - beta_first) * gradient
    second_new = beta_second * second_old + (1.0 - beta_second) * gradient * gradient
    first_hat = first_new / (1.0 - beta_first**STEP)
    second_hat = second_new / (1.0 - beta_second**STEP)
    updated = master - step_rate * (
        first_hat / (jnp.sqrt(second_hat) + adam_eps) + decay_rate * master
    )
    return (gradient, updated, first_new, second_new)


def params(cost=None, **kw):
    return dict(
        compiler_params=pltpu.CompilerParams(vmem_limit_bytes=VMEM_LIMIT, **kw),
        cost_estimate=cost and pl.CostEstimate(flops=cost[0] // 1000 + 1, bytes_accessed=cost[1] // 1000 + 1, transcendentals=0),
    )


class Layout:
    def __init__(self, nd, nz):
        self.nd, self.nz = nd, nz
        self.pair = HEADS // nz
        self.groups = nd // self.pair
        self.dp = lax.axis_index("dp")
        self.z = lax.axis_index("seq")
        self.g = self.dp // self.pair
        self.c = self.dp % self.pair
        self.t = self.z * self.pair + self.c

    def perm(self, target):
        pairs = []
        for dp in range(self.nd):
            for z in range(self.nz):
                goal = target(dp // self.pair, dp % self.pair, z)
                if goal is not None:
                    g, c, s = goal
                    pairs.append((dp * self.nz + z, (g * self.pair + c) * self.nz + s))
        return pairs

    def hop(self, value, target):
        return lax.ppermute(value, AXES, self.perm(target))

    def group_hop(self, value, bit):
        return self.hop(value, lambda g, c, z: (g ^ bit, c, z))

    def core_hop(self, value, r):
        return self.hop(value, lambda g, c, z: (g, c ^ r, z))

    def ring(self, value):
        return self.hop(value, lambda g, c, z: (g, c, (z + 1) % self.nz))

    def flat_hop(self, value, bit):
        return lax.ppermute(value, AXES, [(i, i ^ bit) for i in range(self.nd * self.nz)])

    def head_owner_perm(self):
        pairs = []
        for r in range(self.nd * self.nz):
            head, quarter = r // self.groups, r % self.groups
            s, c = head // self.pair, head % self.pair
            pairs.append((r, ((quarter ^ s) * self.pair + c) * self.nz + s))
        return pairs


def after(values, *deps):
    flat, tree = jax.tree.flatten((values, deps))
    return jax.tree.unflatten(tree, lax.optimization_barrier(flat))[0]


def join(*values):
    return after(values)


def bits_of(count, descending):
    bits = []
    bit = 1
    while bit < count:
        bits.append(bit)
        bit *= 2
    return bits[::-1] if descending else bits


class GroupGather:
    def __init__(self, lay, block, descending):
        self.lay = lay
        self.rows = block.shape[0]
        self.held = {0: (block, 0)}
        self.rounds = [[] for _ in bits_of(lay.groups, False)]
        known = [0]
        for bit in bits_of(lay.groups, descending):
            for m in list(known):
                self.rounds[bin(m).count("1")].append((m, bit))
                known.append(m ^ bit)

    def block(self, m):
        array, first = self.held[m]
        return array[first : first + self.rows]

    def send(self, depth):
        if depth < len(self.rounds):
            for m, bit in self.rounds[depth]:
                self.held[m ^ bit] = (self.lay.group_hop(self.block(m), bit), 0)

    @staticmethod
    def stack(halves):
        return jnp.concatenate([h.block(0) for h in halves])

    @staticmethod
    def send_first(halves, stack):
        lay = halves[0].lay
        for bit in bits_of(lay.groups, False):
            got = lay.group_hop(stack, bit)
            first = 0
            for h in halves:
                h.held[bit] = (got, first)
                first += h.rows

    @property
    def state(self):
        return {m: v for m, (v, _) in self.held.items()}

    @state.setter
    def state(self, state):
        for m, v in state.items():
            self.held[m] = (v, self.held[m][1])

    def rest(self, depth):
        while depth < len(self.rounds):
            self.send(depth)
            depth += 1
        return self.held


class GroupScatter:
    def __init__(self, lay, keep, send, descending):
        self.lay = lay
        self.keep, self.send = keep, send
        self.bits = bits_of(lay.groups, descending)
        self.at = 0

    @staticmethod
    def member(lay, index, descending):
        bits = bits_of(lay.groups, descending)
        return sum(bit for j, bit in enumerate(bits) if index >> (len(bits) - 1 - j) & 1)

    @property
    def state(self):
        return (self.keep, self.send)

    @state.setter
    def state(self, state):
        self.keep, self.send = state

    def step(self):
        if self.at < len(self.bits):
            self.send = self.lay.group_hop(self.send, self.bits[self.at])
            self.at += 1

    def fold(self):
        total = self.keep.astype(f32) + self.send.astype(f32)
        half = total.shape[0] // 2
        self.keep, self.send = total[:half], total[half:].astype(bf16)

    def result(self):
        return (self.keep.astype(f32) + self.send.astype(f32))[0]


def cast_kernel(c_ref, *refs):
    out_ref = refs[-1]
    at = 0
    for ref in refs[:-1]:
        value = ref[...].astype(bf16)
        if value.shape[1] < LANES:
            value = jnp.pad(value, ((0, 0), (0, LANES - value.shape[1])))
        out_ref[0, :, at : at + value.shape[1]] = value
        at += value.shape[1]


def prepare(lay, r, sources):
    rows, pair, nz = sources[0][0].shape[0], lay.pair, lay.nz

    def spec(first, width):
        if first is None:
            return pl.BlockSpec((rows, width), lambda z, c: (0, 0))
        return pl.BlockSpec((rows, width), lambda z, c: (0, first + z * pair + (c[0] ^ r)))

    total = sum(max(width, LANES) for _, _, width in sources)
    return pl.pallas_call(
        cast_kernel,
        grid_spec=pltpu.PrefetchScalarGridSpec(
            num_scalar_prefetch=1,
            grid=(nz,),
            in_specs=[spec(first, width) for _, first, width in sources],
            out_specs=pl.BlockSpec((1, rows, total), lambda z, c: (z, 0, 0)),
        ),
        out_shape=jax.ShapeDtypeStruct((nz, rows, total), bf16),
        name="prepare",
        **params((rows * total * nz, rows * total * nz * 6)),
    )(jnp.reshape(lay.c, (1,)).astype(jnp.int32), *[v for v, _, _ in sources])


def place_kernel(count, tile, slot_ref, *refs):
    out_ref, sems = refs[-2], refs[-1]
    here = pl.ds(pl.multiple_of(pl.program_id(0) * tile, tile), tile)

    def copy(i):
        return pltpu.make_async_copy(refs[i], out_ref.at[slot_ref[i], here], sems.at[i])

    for i in range(count):

        @pl.when(slot_ref[i] >= 0)
        def _(i=i):
            copy(i).start()

    for i in range(count):

        @pl.when(slot_ref[i] >= 0)
        def _(i=i):
            copy(i).wait()


def place(blocks, slots, rows, total, held=None):
    count = len(blocks)
    width = blocks[0][0].shape[1]
    tile = rows if count * rows * width <= 2**21 else max(min(64, rows), rows // 2)
    operands = [v for v, _ in blocks] + ([] if held is None else [held])
    any_spec = pl.BlockSpec(memory_space=pl.ANY)
    return pl.pallas_call(
        partial(place_kernel, count, tile),
        grid_spec=pltpu.PrefetchScalarGridSpec(
            num_scalar_prefetch=1,
            grid=(rows // tile,),
            in_specs=[
                pl.BlockSpec(
                    (tile, width),
                    lambda i, slot, first=first, j=j: (
                        first // tile + jnp.where(slot[j] >= 0, i, 0),
                        0,
                    ),
                )
                for j, (_, first) in enumerate(blocks)
            ]
            + [any_spec] * (len(operands) - count),
            out_specs=any_spec,
            scratch_shapes=[pltpu.SemaphoreType.DMA((count,))],
        ),
        out_shape=jax.ShapeDtypeStruct((total, rows, width), blocks[0][0].dtype),
        input_output_aliases={} if held is None else {count + 1: 0},
        name="place",
        **params((count, 4 * count * rows * width)),
    )(jnp.stack([jnp.asarray(v, jnp.int32) for v in slots]), *operands)


def flip_kernel(in_ref, out_ref):
    out_ref[...] = in_ref[...].astype(f32).T


def last_columns(array):
    rows, total = array.shape
    return pl.pallas_call(
        flip_kernel,
        grid=(1,),
        in_specs=[pl.BlockSpec((rows, LANES), lambda i: (0, total // LANES - 1))],
        out_specs=pl.BlockSpec((LANES, rows), lambda i: (0, 0)),
        out_shape=jax.ShapeDtypeStruct((LANES, rows), f32),
        name="last_columns",
        **params(),
    )(array)


def block_order(lay):
    order = []
    for part in (1, 0):
        for r in range(lay.pair):
            for i in range(lay.groups // 2):
                m = GroupScatter.member(lay, part * (lay.groups // 2) + i, bool(r))
                order.append((lay.g ^ m) * lay.pair + (lay.c ^ r))
    return jnp.stack(order).astype(jnp.int32)


def write_block(half, outs, at, value):
    i = pl.program_id(0)
    for k, out in enumerate(outs):

        @pl.when(jnp.logical_and(i >= k * half, i < (k + 1) * half))
        def _(out=out):
            out[0, :, at : at + value.shape[1]] = value


def gradient_kernel(half, block_ref, left_ref, right_ref, *outs):
    write_block(half, outs, 0, dot(left_ref[...], right_ref[...], 0, 0).astype(bf16))


def folded_kernel(half, first, gain, rides, block_ref, x_ref, right_ref, sums_ref, w_ref, small_ref, *refs):
    others, outs = (refs[:2], refs[2:]) if rides else ((), refs[:-1])
    vec = small_ref[...].astype(f32)
    raw = dot(x_ref[...], right_ref[...], 0, 0)
    sums = sums_ref[0:1]
    grad = raw * vec[:, gain : gain + 1] + sums * vec[:, gain + 1 : gain + 2]
    write_block(half, outs, 0, grad.astype(bf16))
    w = w_ref[:, first : first + raw.shape[1]].astype(f32)
    lane = lax.broadcasted_iota(jnp.int32, vec.shape, 1)
    moment = jnp.sum(w * raw, axis=1, keepdims=True)
    plain = jnp.sum(w * sums, axis=1, keepdims=True)
    lanes = jnp.where(lane == gain, moment, jnp.where(lane == gain + 1, plain, 0.0))
    if rides:
        lanes = lanes + others[0][...] + others[1][...]
        write_block(half, outs, raw.shape[1], lanes.astype(bf16))
    else:
        refs[-1][...] = lanes


def columns_kernel(unit, hd, t_ref, dy_ref, du_ref, *refs):
    out_ref = refs[-1]
    width = out_ref.shape[0]
    t = t_ref[0]
    place = lax.broadcasted_iota(jnp.int32, (1, width), 1)
    dy = jnp.sum(dy_ref[...].astype(f32), axis=0, keepdims=True)
    dp = sum(jnp.sum(ref[:, 0], axis=0, keepdims=True) for ref in refs[:-1])
    blank = jnp.zeros((1, width), f32)
    rows = [blank] * 4 + [dy, dy]
    for j in range(3):
        head = jnp.concatenate([dp[:, j * hd : (j + 1) * hd]] * (width // hd), axis=1)
        rows.append(jnp.where(place // hd == t, head, 0.0))
    share = width // unit
    units = jnp.concatenate([du_ref[0:1]] * share, axis=1)
    for k in range(HEADS // share):
        rows.append(jnp.where(place // unit + k * share == t, units, 0.0))
    rows += [blank] * (LANES - len(rows))
    out_ref[...] = jnp.concatenate(rows).T


def plain_columns(lay, dy, du_sums, dp_sums, unit, hd):
    tokens, width = dy.shape

    def whole(v):
        return pl.BlockSpec(v.shape, lambda i, t: (0,) * v.ndim)

    return pl.pallas_call(
        partial(columns_kernel, unit, hd),
        grid_spec=pltpu.PrefetchScalarGridSpec(
            num_scalar_prefetch=1,
            grid=(1,),
            in_specs=[whole(v) for v in (dy, du_sums, *dp_sums)],
            out_specs=pl.BlockSpec((width, LANES), lambda i, t: (0, 0)),
        ),
        out_shape=jax.ShapeDtypeStruct((width, LANES), f32),
        name="plain_columns",
        **params((tokens * width, 4 * tokens * width)),
    )(jnp.reshape(lay.t, (1,)).astype(jnp.int32), dy, du_sums, *dp_sums)


def gradient_call(lay, kernel, left, rights, by_rows, n, more=()):
    tokens, width = left.shape
    pair, half = lay.pair, lay.groups // 2
    rows = width // (lay.groups * pair)
    outs = 2 * pair

    def out_map(k):
        return lambda i, block: (jnp.clip(i - k * half, 0, half - 1), 0, 0)

    def row_map(column):
        return lambda i, block: (block[i], column)

    values = pl.pallas_call(
        partial(kernel, half),
        grid_spec=pltpu.PrefetchScalarGridSpec(
            num_scalar_prefetch=1,
            grid=(outs * half,),
            in_specs=[pl.BlockSpec((tokens, rows), lambda i, block: (0, block[i]))]
            + [pl.BlockSpec(v.shape, lambda i, block: (0, 0)) for v in rights]
            + [pl.BlockSpec((rows, size), row_map(column)) for _, size, column in by_rows],
            out_specs=[pl.BlockSpec((1, rows, n), out_map(k)) for k in range(outs)]
            + [pl.BlockSpec((rows, size), row_map(0)) for size in more],
        ),
        out_shape=[jax.ShapeDtypeStruct((half, rows, n), bf16)] * outs
        + [jax.ShapeDtypeStruct((width, size), f32) for size in more],
        name="gradient",
        **params((2 * tokens * width * n, 2 * (tokens * width + tokens * n + width * n))),
    )(block_order(lay), left, *rights, *[v for v, _, _ in by_rows])
    parts = [GroupScatter(lay, values[pair + r], values[r], bool(r)) for r in range(pair)]
    return (parts, *values[outs:])


def gradient(lay, left, right):
    return gradient_call(lay, gradient_kernel, left, [right], [], right.shape[1])[0]


def folded_gradient(lay, x, right, sums, w_qu, first, gain, others=()):
    total = w_qu.shape[1]
    by_rows = [(w_qu, total, 0), (w_qu, LANES, total // LANES - 1)]
    by_rows += [(v, LANES, 0) for v in others]
    rides = len(others) > 0

    def call(half, *refs):
        folded_kernel(half, first, gain, rides, *refs)

    n = right.shape[1] + (LANES if rides else 0)
    return gradient_call(lay, call, x, [right, sums], by_rows, n, () if rides else (LANES,))


def fold_kernel(*refs):
    count = len(refs) // 4
    for p in range(count):
        keep, got, next_keep, next_send = refs[p], refs[count + p], refs[2 * count + p], refs[3 * count + p]
        half = next_keep.shape[0]
        total = keep[...].astype(f32) + got[...].astype(f32)
        next_keep[...] = total[:half]
        next_send[...] = total[half:].astype(bf16)


def fold(parts):
    held, rows, n = parts[0].keep.shape
    half = held // 2
    tile = min(128, rows)
    full = pl.BlockSpec((held, tile, n), lambda i: (0, i, 0))
    part = pl.BlockSpec((half, tile, n), lambda i: (0, i, 0))
    count = len(parts)
    values = pl.pallas_call(
        fold_kernel,
        grid=(rows // tile,),
        in_specs=[full] * (2 * count),
        out_specs=[part] * (2 * count),
        out_shape=[jax.ShapeDtypeStruct((half, rows, n), f32)] * count
        + [jax.ShapeDtypeStruct((half, rows, n), bf16)] * count,
        name="fold",
        **params((held * rows * n, 8 * held * rows * n)),
    )(*[p.keep for p in parts], *[p.send for p in parts])
    for k, p in enumerate(parts):
        p.keep, p.send = values[k], values[count + k]


def blocks_kernel(count, *refs):
    out_ref = refs[-1]
    places, _, rows, _ = out_ref.shape
    for p in range(count):
        total = (refs[p][0].astype(f32) + refs[count + p][0].astype(f32)).astype(bf16)
        for z in range(places):
            out_ref[z, p] = total[z * rows : (z + 1) * rows]


def final_blocks(parts, nz):
    _, total, n = parts[0].keep.shape
    rows, count = total // nz, len(parts)
    steps = nz // 2 if nz % 2 == 0 else nz
    places = nz // steps
    return pl.pallas_call(
        partial(blocks_kernel, count),
        grid=(steps,),
        in_specs=[pl.BlockSpec((1, places * rows, n), lambda i: (0, i, 0))] * (2 * count),
        out_specs=pl.BlockSpec((places, count, rows, n), lambda i: (i, 0, 0, 0)),
        out_shape=jax.ShapeDtypeStruct((nz, count, rows, n), bf16),
        name="final_blocks",
        **params((count * total * n, 8 * count * total * n)),
    )(*[p.keep for p in parts], *[p.send for p in parts])


def chunk_kernel(count, ways, slot_ref, *refs):
    for k in range(ways):

        @pl.when(slot_ref[k] >= 0)
        def _(k=k):
            total = sum(refs[k * count + p][...].astype(f32) for p in range(count))
            out = refs[-ways + k]
            out[...] = total.astype(out.dtype)


def chunk_sums(parts, slots, received):
    count, _, span, width = parts[0].shape
    tile = min(span, 128)
    ways = len(slots)

    def whole(k):
        return lambda i, slot: (0, jnp.where(slot[k] >= 0, i, 0), 0)

    def part(k):
        return lambda i, slot: (0, jnp.maximum(slot[k], 0), jnp.where(slot[k] >= 0, i, 0), 0)

    in_specs, operands = [], []
    for k in range(ways):
        for p in parts:
            in_specs.append(pl.BlockSpec((count, None, tile, width), part(k)))
            operands.append(p)
        if received:
            in_specs.append(pl.BlockSpec((count, tile, width), whole(k)))
            operands.append(received[k])
    shape = jax.ShapeDtypeStruct((count, span, width), bf16)
    return pl.pallas_call(
        partial(chunk_kernel, len(operands) // ways, ways),
        grid_spec=pltpu.PrefetchScalarGridSpec(
            num_scalar_prefetch=1,
            grid=(span // tile,),
            in_specs=in_specs,
            out_specs=[pl.BlockSpec((count, tile, width), whole(k)) for k in range(ways)],
        ),
        out_shape=[shape] * ways,
        name="chunk_sums",
        **params((8 * count * span * width, 16 * count * span * width)),
    )(jnp.stack(slots).astype(jnp.int32), *operands)


def turn(values, cosine, low_sine, high_sine, quarter):
    head = values[:, :LANES]
    turned = (
        head * cosine
        + pltpu.roll(head, LANES - quarter, 1) * low_sine
        + pltpu.roll(head, quarter, 1) * high_sine
    )
    return jnp.concatenate([turned, values[:, LANES:]], axis=1)


def piece_kernel(pair, places, quarter, pos_ref, *refs):
    x_refs, refs = refs[: pair * places], refs[pair * places :]
    for p in range(places):

        @pl.when(pl.program_id(1) == p)
        def _(p=p):
            piece_rows(pair, quarter, x_refs[p * pair : (p + 1) * pair], refs)


def piece_rows(pair, quarter, x_refs, refs):
    vec_ref, w_ref, qkv_bias_ref, up_bias_ref, tab_ref = refs[:5]
    x_out, qkv_out, g_out, slope_out = refs[-4:]
    tile = x_refs[0].shape[1]
    unit, wide = g_out.shape[-1], qkv_out.shape[-1]
    hd = wide // 3
    x = jnp.concatenate([ref[0].astype(f32) for ref in x_refs])
    normed, _ = normalize(x)
    a = (normed * vec_ref[0:1] + vec_ref[1:2]).astype(bf16)
    m = (normed * vec_ref[2:3] + vec_ref[3:4]).astype(bf16)
    cosine, low_sine, high_sine = (jnp.concatenate([tab_ref[k]] * pair) for k in range(3))

    def put(out, at, value):
        value = value.astype(bf16)
        for r in range(pair):
            out[r, 0, 0, :, at : at + value.shape[1]] = value[r * tile : (r + 1) * tile]

    put(x_out, 0, normed)
    for j in range(3):
        part = dot(a, w_ref[:, unit + j * hd : unit + (j + 1) * hd])
        part = part + qkv_bias_ref[0:1, j * hd : (j + 1) * hd]
        put(qkv_out, j * hd, turn(part, cosine, low_sine, high_sine, quarter) if j < 2 else part)
    u = dot(m, w_ref[:, :unit]) + up_bias_ref[0:1]
    half = 0.5 * (1.0 + lax.erf(u * (0.5**0.5)))
    put(g_out, 0, u * half)
    put(slope_out, 0, half + u * (jnp.exp(-0.5 * u * u) * 0.3989422804014327))


def piece_forward(lay, pieces, where, vec, w_qu, qkv_bias, up_bias, tables, held):
    count, span, width = pieces[0].shape
    pair, nz, places = lay.pair, lay.nz, len(where)
    unit, wide = up_bias.shape[1], qkv_bias.shape[1]
    tile = min(span, 256)
    steps = span // tile

    def out(n):
        return (
            jax.ShapeDtypeStruct((pair, count, nz, span, n), bf16),
            pl.BlockSpec((pair, 1, 1, tile, n), lambda i, p, j, pos: (0, i, pos[p], j, 0)),
        )

    def whole(v):
        return pl.BlockSpec(v.shape, lambda i, p, j, pos: (0,) * v.ndim)

    def row_map(q):
        return lambda i, p, j, pos: (i, jnp.where(p == q, j, jnp.where(p < q, 0, steps - 1)), 0)

    outs = [out(n) for n in (width, wide, unit, unit)]
    in_specs = [pl.BlockSpec((1, tile, width), row_map(q)) for q in range(places) for _ in range(pair)]
    in_specs += [pl.BlockSpec((8, width), lambda i, p, j, pos: (0, 0))]
    in_specs += [whole(v) for v in (w_qu, qkv_bias, up_bias)]
    in_specs += [pl.BlockSpec((3, tile, LANES), lambda i, p, j, pos: (0, pos[p] * steps + j, 0))]
    in_specs += [pl.BlockSpec(memory_space=pl.ANY)] * len(held)
    tokens = pair * places * count * span
    return pl.pallas_call(
        partial(piece_kernel, pair, places, wide // 24),
        grid_spec=pltpu.PrefetchScalarGridSpec(
            num_scalar_prefetch=1,
            grid=(count, places, steps),
            in_specs=in_specs,
            out_specs=[o[1] for o in outs],
        ),
        out_shape=[o[0] for o in outs],
        input_output_aliases={pair * places + 6 + k: k for k in range(len(held))},
        name="piece_forward",
        **params((2 * tokens * width * (unit + wide), 12 * tokens * width)),
    )(
        jnp.stack(where).astype(jnp.int32),
        *pieces,
        vec,
        w_qu,
        qkv_bias,
        up_bias,
        tables,
        *held,
    )


def attn_fwd_kernel(scale, tile, qkv_ref, o_ref, lse_ref):
    length, hd = o_ref.shape[1:]
    for i in range(length // tile):
        end = (i + 1) * tile
        q_i = qkv_ref[0, i * tile : end, :hd]
        scores = dot(q_i, qkv_ref[0, :end, hd : 2 * hd], 1, 1) * scale
        row = lax.broadcasted_iota(jnp.int32, scores.shape, 0) + i * tile
        col = lax.broadcasted_iota(jnp.int32, scores.shape, 1)
        scores = jnp.where(col <= row, scores, masked_value)
        row_max = jnp.max(scores, axis=1, keepdims=True)
        terms = jnp.exp(scores - row_max)
        row_sum = jnp.sum(terms, axis=1, keepdims=True)
        probs = (terms / row_sum).astype(bf16)
        o_ref[0, i * tile : end] = dot(probs, qkv_ref[0, :end, 2 * hd :]).astype(bf16)
        lse_ref[0, i * tile : end] = jnp.broadcast_to(row_max + jnp.log(row_sum), (tile, LANES))


def attn_forward(qkv, scale):
    seqs, length, wide = qkv.shape
    hd = wide // 3
    return pl.pallas_call(
        partial(attn_fwd_kernel, scale, min(512, length)),
        grid=(seqs,),
        in_specs=[pl.BlockSpec((1, length, wide), lambda s: (s, 0, 0))],
        out_specs=[
            pl.BlockSpec((1, length, hd), lambda s: (s, 0, 0)),
            pl.BlockSpec((1, length, LANES), lambda s: (s, 0, 0)),
        ],
        out_shape=[
            jax.ShapeDtypeStruct((seqs, length, hd), bf16),
            jax.ShapeDtypeStruct((seqs, length, LANES), f32),
        ],
        name="attn_forward",
        **params((4 * seqs * length * length * hd, 8 * seqs * length * wide)),
    )(qkv)


def attn_bwd_kernel(quarter, scale, tile, dy_ref, wo_ref, qkv_ref, lse_ref, tab_ref, *refs):
    dp_ref, sum_ref, do_s, dk_s, dv_s = refs[-5:]
    length = dy_ref.shape[1]
    hd = wo_ref.shape[0]
    cosine, low_sine, high_sine = tab_ref[0], -tab_ref[1], -tab_ref[2]
    do_s[...] = dot(dy_ref[0], wo_ref[...], 1, 1).astype(bf16)
    steps = length // tile
    for i in reversed(range(steps)):
        end = (i + 1) * tile
        q_i = qkv_ref[0, i * tile : end, :hd]
        k = qkv_ref[0, :end, hd : 2 * hd]
        do_i = do_s[i * tile : end]
        scores = dot(q_i, k, 1, 1) * scale
        row = lax.broadcasted_iota(jnp.int32, scores.shape, 0) + i * tile
        col = lax.broadcasted_iota(jnp.int32, scores.shape, 1)
        probs = jnp.where(col <= row, jnp.exp(scores - lse_ref[0, i * tile : end, 0:1]), 0.0)
        probs_grad = dot(do_i, qkv_ref[0, :end, 2 * hd :], 1, 1)
        row_dot = jnp.sum(probs * probs_grad, axis=1, keepdims=True)
        score_grad = (probs * (probs_grad - row_dot)).astype(bf16)
        dq = dot(score_grad, k) * scale
        dp_ref[0, i * tile : end, :hd] = turn(
            dq,
            cosine[i * tile : end],
            low_sine[i * tile : end],
            high_sine[i * tile : end],
            quarter,
        ).astype(bf16)
        dk = dot(score_grad, q_i, 0, 0)
        dv = dot(probs.astype(bf16), do_i, 0, 0)
        if i == steps - 1:
            dk_s[...] = dk
            dv_s[...] = dv
        else:
            dk_s[:end] += dk
            dv_s[:end] += dv
    dp_ref[0, :, hd : 2 * hd] = turn(
        dk_s[...] * scale, cosine, low_sine, high_sine, quarter
    ).astype(bf16)
    dp_ref[0, :, 2 * hd :] = dv_s[...].astype(bf16)
    total = jnp.sum(dp_ref[0].astype(f32), axis=0, keepdims=True)
    sum_ref[0] = jnp.broadcast_to(total, sum_ref.shape[1:])


def attn_backward(dy, w_out, qkv, lse, tables, scale, part, parts, held):
    seqs, length, width = dy.shape
    hd = w_out.shape[0]
    share = seqs // parts
    first = part * share
    flops = 2 * share * length * (hd * width + 5 * length * hd)

    def row_map(s):
        return (first + s, 0, 0)

    return pl.pallas_call(
        partial(attn_bwd_kernel, hd // 8, scale, min(512, length)),
        grid=(share,),
        in_specs=[
            pl.BlockSpec((1, length, width), row_map),
            pl.BlockSpec(w_out.shape, lambda s: (0, 0)),
            pl.BlockSpec((1, length, 3 * hd), row_map),
            pl.BlockSpec((1, length, LANES), row_map),
            pl.BlockSpec(tables.shape, lambda s: (0, 0, 0)),
        ]
        + [pl.BlockSpec(memory_space=pl.ANY)] * len(held),
        out_specs=[
            pl.BlockSpec((1, length, 3 * hd), row_map),
            pl.BlockSpec((1, 8, 3 * hd), lambda s: (s, 0, 0)),
        ],
        out_shape=[
            jax.ShapeDtypeStruct((seqs, length, 3 * hd), bf16),
            jax.ShapeDtypeStruct((share, 8, 3 * hd), f32),
        ],
        input_output_aliases={5 + k: k for k in range(len(held))},
        scratch_shapes=[
            pltpu.VMEM((length, hd), bf16),
            pltpu.VMEM((length, hd), f32),
            pltpu.VMEM((length, hd), f32),
        ],
        name="attn_backward",
        **params((flops, 8 * share * length * width)),
    )(dy, w_out, qkv, lse, tables, *held)


def write_chunk(outs, more, total):
    for ref in more:
        total = total + ref[0].astype(f32)
    total = total.astype(bf16)
    if len(outs) == 1:
        outs[0][0] = total
    else:
        for k, out in enumerate(outs):

            @pl.when(pl.program_id(0) == k)
            def _(out=out):
                out[0] = total


def chunk_outputs(order_len, span, width, separate):
    if separate:
        specs = [pl.BlockSpec((1, span, width), lambda i, order: (0, 0, 0))] * order_len
        return specs, [jax.ShapeDtypeStruct((1, span, width), bf16)] * order_len
    specs = [pl.BlockSpec((1, span, width), lambda i, order: (i, 0, 0))]
    return specs, [jax.ShapeDtypeStruct((order_len, span, width), bf16)]


def output_kernel(count, order_ref, g_ref, wd_ref, o_ref, wo_ref, *refs):
    total = dot(g_ref[...], wd_ref[...], 1, 1) + dot(o_ref[...], wo_ref[...])
    write_chunk(refs[count:], refs[:count], total)


def output_forward(g, w_down, o, w_out, span, order, first, more=(), separate=False):
    unit, width, hd = g.shape[1], w_down.shape[0], o.shape[1]
    steps = order.shape[0]
    out_specs, out_shape = chunk_outputs(steps, span, width, separate)
    return pl.pallas_call(
        partial(output_kernel, len(more)),
        grid_spec=pltpu.PrefetchScalarGridSpec(
            num_scalar_prefetch=1,
            grid=(steps,),
            in_specs=[
                pl.BlockSpec((span, unit), lambda i, order: (first + order[i], 0)),
                pl.BlockSpec(w_down.shape, lambda i, order: (0, 0)),
                pl.BlockSpec((span, hd), lambda i, order: (first + order[i], 0)),
                pl.BlockSpec(w_out.shape, lambda i, order: (0, 0)),
            ]
            + [pl.BlockSpec((1, span, width), lambda i, order: (i, 0, 0))] * len(more),
            out_specs=out_specs,
        ),
        out_shape=out_shape,
        name="output_forward",
        **params((2 * steps * span * width * (unit + hd), 8 * steps * span * width)),
    )(order, g, w_down, o, w_out, *more)


def hidden_kernel(dy_ref, wd_ref, slope_ref, du_ref, sum_ref):
    dg = dot(dy_ref[...], wd_ref[...])
    du_ref[...] = (dg * slope_ref[...].astype(f32)).astype(bf16)
    total = jnp.sum(du_ref[...].astype(f32), axis=0, keepdims=True)
    total = jnp.broadcast_to(total, sum_ref.shape)

    @pl.when(pl.program_id(0) == 0)
    def _():
        sum_ref[...] = total

    @pl.when(pl.program_id(0) > 0)
    def _():
        sum_ref[...] += total


def hidden_backward(dy, w_down, slope, tile):
    tokens, width = dy.shape
    unit = w_down.shape[1]
    return pl.pallas_call(
        hidden_kernel,
        grid=(tokens // tile,),
        in_specs=[
            pl.BlockSpec((tile, width), lambda i: (i, 0)),
            pl.BlockSpec(w_down.shape, lambda i: (0, 0)),
            pl.BlockSpec((tile, unit), lambda i: (i, 0)),
        ],
        out_specs=[
            pl.BlockSpec((tile, unit), lambda i: (i, 0)),
            pl.BlockSpec((8, unit), lambda i: (0, 0)),
        ],
        out_shape=[
            jax.ShapeDtypeStruct((tokens, unit), bf16),
            jax.ShapeDtypeStruct((8, unit), f32),
        ],
        name="hidden_backward",
        **params((2 * tokens * width * unit, 6 * tokens * width)),
    )(dy, w_down, slope)


def input_kernel(count, hd, order_ref, du_ref, dp_ref, wu_ref, wq_ref, wk_ref, wv_ref, vec_ref, *refs):
    da = (
        dot(dp_ref[:, :hd], wq_ref[...], 1, 1)
        + dot(dp_ref[:, hd : 2 * hd], wk_ref[...], 1, 1)
        + dot(dp_ref[:, 2 * hd :], wv_ref[...], 1, 1)
    )
    dm = dot(du_ref[...], wu_ref[...], 1, 1)
    write_chunk(refs[count:], refs[:count], da * vec_ref[0:1] + dm * vec_ref[2:3])


def input_backward(du, dp, w_qu, vec, span, order, first, more=(), separate=False):
    unit, width, hd = du.shape[1], w_qu.shape[0], dp.shape[1] // 3
    columns = unit // hd
    steps = order.shape[0]
    out_specs, out_shape = chunk_outputs(steps, span, width, separate)
    return pl.pallas_call(
        partial(input_kernel, len(more), hd),
        grid_spec=pltpu.PrefetchScalarGridSpec(
            num_scalar_prefetch=1,
            grid=(steps,),
            in_specs=[
                pl.BlockSpec((span, unit), lambda i, order: (first + order[i], 0)),
                pl.BlockSpec((span, 3 * hd), lambda i, order: (first + order[i], 0)),
                pl.BlockSpec((width, unit), lambda i, order: (0, 0)),
            ]
            + [pl.BlockSpec((width, hd), lambda i, order, j=j: (0, columns + j)) for j in range(3)]
            + [pl.BlockSpec((8, width), lambda i, order: (0, 0))]
            + [pl.BlockSpec((1, span, width), lambda i, order: (i, 0, 0))] * len(more),
            out_specs=out_specs,
        ),
        out_shape=out_shape,
        name="input_backward",
        **params((2 * steps * span * width * (unit + 3 * hd), 12 * steps * span * width)),
    )(order, du, dp, w_qu, w_qu, w_qu, w_qu, vec, *more)


def adam_kernel(pair, places, rate, c_ref, *refs):
    g_refs, (w_ref, m_ref, v_ref), outs = refs[:pair], refs[pair : pair + 3], refs[-4:]
    pieces = []
    for z in range(places):
        parts = [ref[z].astype(f32) for ref in g_refs]
        if pair == 2:
            swapped = c_ref[0] == 1
            parts = [jnp.where(swapped, parts[1], parts[0]), jnp.where(swapped, parts[0], parts[1])]
        pieces += parts
    grad = pieces[0] if len(pieces) == 1 else jnp.concatenate(pieces, axis=1)
    result = adamw(w_ref[...], grad, m_ref[...], v_ref[...], rate)
    for ref, value in zip(outs, result, strict=True):
        ref[...] = value


def adam_columns(lay, rate, parts, at, piece, state, start, kinds, held):
    nz, rows, _ = parts[0].shape
    pair = len(parts)
    total = state[0].shape[1]
    places = max(1, min(nz, 1024 // (pair * piece)))
    wide = places * pair * piece
    steps = nz // places
    first = start // wide

    w_spec = pl.BlockSpec((rows, wide), lambda j, z, c: (0, first + j * steps + z))
    g_spec = pl.BlockSpec((places, rows, piece), lambda j, z, c: (z, 0, at // piece + j))
    operands = list(parts) + list(state) + list(held)
    return pl.pallas_call(
        partial(adam_kernel, pair, places, rate),
        grid_spec=pltpu.PrefetchScalarGridSpec(
            num_scalar_prefetch=1,
            grid=(kinds, steps),
            in_specs=[g_spec] * pair
            + [w_spec] * 3
            + [pl.BlockSpec(memory_space=pl.ANY)] * len(held),
            out_specs=[w_spec] * 4,
        ),
        out_shape=[jax.ShapeDtypeStruct((rows, total), f32)] * 4,
        input_output_aliases={1 + pair + 3 + k: k for k in range(len(held))},
        name="adam_columns",
        **params((30 * rows * kinds * piece * HEADS, 30 * rows * kinds * piece * HEADS)),
    )(jnp.reshape(lay.c, (1,)).astype(jnp.int32), *operands)


class SeqGather:
    def __init__(self, lay, own):
        self.lay = lay
        self.rounds, self.at = lay.nz - 1, 0
        self.newest = own
        self.places, self.fresh = [lay.z], [own]

    def step(self):
        self.at += 1
        self.newest = self.lay.ring(self.newest)
        self.fresh.append(self.newest)
        self.places.append((self.lay.z - self.at) % self.lay.nz)

    def take(self):
        items = list(zip(self.fresh, self.places))
        self.fresh, self.places = [], []
        return items

    @property
    def state(self):
        return (self.newest, self.fresh)

    @state.setter
    def state(self, state):
        self.newest, self.fresh = state


class TokenBuffer:
    def __init__(self, lay):
        self.lay, self.todo, self.out = lay, [], None

    def add(self, items):
        for pieces, where in items:
            for r, piece in enumerate(pieces):
                for s in range(piece.shape[0]):
                    self.todo.append((piece[s], (r * piece.shape[0] + s) * self.lay.nz + where))

    def flush(self, count):
        blocks, slots = [(v, 0) for v, _ in self.todo], [w for _, w in self.todo]
        total = self.lay.pair * self.lay.nz * count
        self.out = place(blocks, slots, blocks[0][0].shape[0], total, self.out)
        self.todo = []
        return self.out

    @property
    def state(self):
        return ([v for v, _ in self.todo], self.out)

    @state.setter
    def state(self, state):
        blocks, self.out = state
        self.todo = [(v, w) for v, (_, w) in zip(blocks, self.todo)]


class SeqScatter:
    def __init__(self, lay):
        self.lay = lay
        self.four = lay.nz == 4
        if self.four:
            roles = [[3, 2, 1, 0], [0, 2, 3, 1], [3, 1, 0, 2], [0, 1, 2, 3]]
        else:
            roles = [list(range(lay.nz))] * lay.nz
        self.order = jnp.array(roles, jnp.int32)[lay.z]

    def load(self, chunks):
        self.state = list(chunks)

    def move(self, value, targets):
        return self.lay.hop(value, lambda g, c, z: (g, c, targets[z]) if z in targets else None)

    def send(self):
        if not self.four:
            self.state = [lax.all_to_all(self.state[0], "seq", 0, 0, tiled=True)]
            return
        near, far, last, own = self.state
        near = self.move(near, {0: 1, 3: 2, 2: 3, 1: 0})
        across = self.move(far, {0: 2, 3: 1})
        beside = self.move(far, {1: 2, 2: 1})
        self.state = [near, across, beside, last, own]

    def finish(self):
        if not self.four:
            return
        near, across, beside, last, own = self.state
        inner = jnp.logical_and(self.lay.z > 0, self.lay.z < 3)
        passed = jnp.where(inner, last.astype(f32) + near.astype(f32), last.astype(f32)).astype(bf16)
        came = self.move(passed, {1: 3, 2: 0, 0: 1, 3: 2})
        self.state = [near, across, beside, came, own]

    def result(self):
        if not self.four:
            return jnp.sum(self.state[0].astype(f32), axis=0)
        near, across, beside, came, own = (v[0].astype(f32) for v in self.state)
        inner = jnp.logical_and(self.lay.z > 0, self.lay.z < 3)
        return own + came + jnp.where(inner, across + beside, near)


def body(
    inputs,
    cotangent,
    attn_params,
    attn_first,
    attn_second,
    mlp_params,
    mlp_first,
    mlp_second,
    small,
    small_first,
    small_second,
):
    lay = Layout(lax.axis_size("dp"), lax.axis_size("seq"))
    groups, nz, pair = lay.groups, lay.nz, lay.pair
    count, span, width = inputs.shape
    rows = attn_params.shape[0]
    ff = mlp_params.shape[1] // 2
    hd = width // HEADS
    unit = ff // HEADS
    rot_dims = hd // 4
    score_scale = hd ** (-0.5)
    first_row = (lay.dp * nz + lay.z) * rows
    seqs, length = count * pair, span * nz
    tokens_here = seqs * length

    qu_sources = [(mlp_params, 0, unit)]
    qu_sources += [(attn_params, j * HEADS, hd) for j in range(3)]
    qu_sources += [(small, None, small.shape[1])]
    dn_sources = [(mlp_params, HEADS, unit)]

    def swap(sources, r):
        blocks = prepare(lay, r, sources)
        return lay.core_hop(blocks, r) if r else blocks

    def exchange(half):
        return lax.all_to_all(half, "seq", 0, 0, tiled=True).reshape(nz * rows, -1)

    class Whole:
        def __init__(self, halves, size=None, first=0, turn=0):
            self.halves, self.seen, self.state = halves, set(), None
            self.size, self.first, self.turn = size or halves[0].rows, first, turn

        def flush(self):
            items = [
                (r, m, (v[0], v[1] + self.first))
                for r, half in enumerate(self.halves)
                for m, v in half.held.items()
                if (r, m) not in self.seen
            ]
            self.seen |= {(r, m) for r, m, _ in items}
            if items:
                count = len(self.halves)
                slots = [
                    (lay.g ^ m ^ self.turn) * count + (lay.c ^ r if count > 1 else 0)
                    for r, m, _ in items
                ]
                blocks = [v for _, _, v in items]
                self.state = place(blocks, slots, self.size, groups * count, self.state)

        def result(self):
            self.flush()
            return self.state.reshape(-1, self.state.shape[-1])

    def joined(parts, *values):
        *values, states = join(*values, [p.state for p in parts])
        for p, v in zip(parts, states):
            p.state = v
        return values

    def crossed(piece):
        return [piece] + [lay.core_hop(piece, r) for r in range(1, pair)]

    positions = jnp.arange(length, dtype=f32)
    frequency = 10000.0 ** (-(jnp.arange(rot_dims // 2, dtype=f32) * 2.0) / rot_dims)
    angles = positions[:, None] * frequency[None, :]
    cosine, sine = jnp.cos(angles), jnp.sin(angles)
    blank = jnp.zeros_like(sine)
    rest = jnp.zeros((length, LANES - rot_dims), f32)
    tables = jnp.stack(
        [
            jnp.concatenate([cosine, cosine, rest + 1.0], axis=1),
            jnp.concatenate([-sine, blank, rest], axis=1),
            jnp.concatenate([blank, sine, rest], axis=1),
        ]
    )

    first = exchange(swap(qu_sources, 0))
    rest = [swap(qu_sources, r) for r in range(1, pair)]
    w_out = attn_params[:, 3 * width :].astype(bf16)
    dn = jnp.stack([prepare(lay, r, dn_sources) for r in range(pair)], axis=1)
    w_out = lax.ppermute(w_out, AXES, lay.head_owner_perm())
    first, rest, w_out, dn, tables = join(first, rest, w_out, dn, tables)

    qu = [GroupGather(lay, first, False)]
    for r in range(1, pair):
        one = exchange(rest[r - 1])
        qu[-1].send(0)
        one, w_out, dn = joined(qu, one, w_out, dn)
        qu.append(GroupGather(lay, one, bool(r % 2)))
    dn = lax.all_to_all(dn, "seq", 0, 0, tiled=True)
    qu[-1].send(0)
    xs, dy, dy_buffer = SeqGather(lay, inputs), SeqGather(lay, cotangent), TokenBuffer(lay)

    def crossing(items):
        return [(crossed(v), place) for v, place in items]

    (own,) = crossing(xs.take())
    own_pieces, dn, w_out = joined(qu + [xs], own[0], dn, w_out)
    ready = [(own_pieces, own[1])]

    w_qu = Whole(qu)
    xs.step()
    dn = [lay.core_hop(dn[:, r], r) if r else dn[:, r] for r in range(pair)]
    dn = [v.reshape(nz * rows, unit) for v in dn]
    dn[-1] = jnp.concatenate([dn[-1], w_out.reshape(-1, unit)])
    dn = [GroupGather(lay, v, bool(r)) for r, v in enumerate(dn)]
    w_qu.flush()
    for v in qu:
        v.send(1)
    (dn_stack,) = joined(qu + dn + [w_qu, xs], GroupGather.stack(dn))
    for v in qu:
        v.rest(2)

    w_qkvu = w_qu.result()
    vectors = last_columns(w_qkvu)
    norm_vec = vectors
    qkv_bias = vectors[6:9].reshape(3, HEADS, hd)
    qkv_bias = lax.dynamic_index_in_dim(qkv_bias, lay.t, 1, keepdims=False).reshape(1, 3 * hd)
    up_bias = lax.dynamic_slice(vectors[9:13].reshape(-1), (lay.t * unit,), (unit,))[None]
    out_bias = vectors[4] + vectors[5]
    held = ()

    def forward_pieces(items, held):
        where = [place for _, place in items]
        pieces = [v for pieces, _ in items for v in pieces]
        return piece_forward(
            lay, pieces, where, norm_vec, w_qkvu, qkv_bias, up_bias, tables, held
        )

    w_dn, w_wo = Whole(dn, nz * rows), Whole(dn[-1:], rows * width // unit, nz * rows, lay.z)
    tick = 0
    while xs.at < xs.rounds:
        taken = xs.take()
        xs.step()
        if tick == 0:
            GroupGather.send_first(dn, dn_stack)
        elif tick == 1:
            w_dn.flush()
            w_wo.flush()
            for v in dn:
                v.send(1)
        held = forward_pieces(ready, held)
        ready = crossing(taken)
        ready_pieces, held = joined(dn + [w_dn, w_wo, xs], [v for v, _ in ready], held)
        ready = list(zip(ready_pieces, [place for _, place in ready]))
        tick += 1
    for v in dn:
        v.rest(2)

    taken = xs.take()
    own_dy = dy.take()
    dy.step()
    held = forward_pieces(ready + crossing(taken), held)
    dy_buffer.add(crossing(own_dy))
    (held,) = joined([dy, dy_buffer, w_dn, w_wo] + dn, held)
    w_down = w_dn.result()
    w_out = w_wo.result().reshape(hd, width)
    tile = min(512, length)
    flat = (tokens_here, width)
    x_flat, qkv, g, slope = (v.reshape(seqs, length, -1) for v in held)
    x_flat, g, slope = (v.reshape(tokens_here, -1) for v in (x_flat, g, slope))

    taken = dy.take()
    dy.step()
    dy_buffer.add(crossing(taken))
    o, lse = attn_forward(qkv, score_scale)
    o = o.reshape(tokens_here, hd)
    out_sum = SeqScatter(lay)
    parts = {}
    for r in range(1, pair):
        (parts[r],) = output_forward(g, w_down, o, w_out, span, out_sum.order, r * count * nz)
    o, lse, g, parts, w_down, w_out = joined([dy, dy_buffer], o, lse, g, parts, w_down, w_out)

    taken = dy.take()
    while dy.at < dy.rounds:
        dy.step()
    dy_buffer.flush(count)
    more = [lay.core_hop(parts[r], r) for r in range(1, pair)]
    dy_buffer.add(crossing(taken))
    out_sum.load(
        output_forward(g, w_down, o, w_out, span, out_sum.order, 0, more, separate=out_sum.four)
    )
    o, lse, g = joined([dy, dy_buffer, out_sum], o, lse, g)

    def steps(*parts):
        for p in parts:
            p.step()

    def to_owners(blocks):
        return lax.all_to_all(blocks, "seq", 0, 0, tiled=True)

    def at_owner(blocks):
        parts = [blocks[:, r] for r in range(pair)]
        return [lay.core_hop(v, r) if r else v for r, v in enumerate(parts)]

    def more_rounds(parts):
        while parts[0].at < len(parts[0].bits):
            if len(parts) == pair and parts[0].keep.shape[2] < width:
                fold(parts)
            else:
                for p in parts:
                    p.fold()
            steps(*parts)

    out_sum.send()
    dy_buffer.add(crossing(dy.take()))
    dy_all = dy_buffer.flush(count).reshape(seqs, length, width)
    down = gradient(lay, dy_all.reshape(flat), g)
    (dy_all,) = joined(down, dy_all)

    z_sum = SeqScatter(lay)
    dp, dp_sums, z_parts = (), {}, {}

    def attention_part(r, held):
        *held, dp_sums[r] = attn_backward(
            dy_all, w_out, qkv, lse, tables, score_scale, r, pair, held
        )
        return held

    def input_part(r, more=(), separate=False):
        return input_backward(
            du,
            dp[0].reshape(tokens_here, 3 * hd),
            w_qkvu,
            norm_vec,
            span,
            z_sum.order,
            r * count * nz,
            more,
            separate,
        )

    steps(*down)
    du, du_sums = hidden_backward(dy_all.reshape(flat), w_down, slope, tile)
    dy_all = after(dy_all, du)
    for r in range(1, pair):
        dp = attention_part(r, dp)
    dy_all, du, du_sums, dp, dp_sums = joined([out_sum] + down, dy_all, du, du_sums, dp, dp_sums)

    out_sum.finish()
    more_rounds(down)
    for r in range(1, pair):
        (z_parts[r],) = input_part(r)
    down_blocks = final_blocks(down, nz)
    dy_all, dp, z_parts, down_blocks = joined([out_sum], dy_all, dp, z_parts, down_blocks)

    for r in range(1, pair):
        z_parts[r] = lay.core_hop(z_parts[r], r)
    down_blocks = to_owners(down_blocks)
    dp = attention_part(0, dp)
    z_sum.load(input_part(0, [z_parts[r] for r in range(1, pair)], z_sum.four))
    dp = dp[0].reshape(tokens_here, 3 * hd)
    dy_flat, du, dp, dp_sums, down_blocks = joined(
        [z_sum], dy_all.reshape(flat), du, dp, dp_sums, down_blocks
    )

    z_sum.send()
    up, lanes = folded_gradient(lay, x_flat, du, du_sums, w_qkvu, 0, 2)
    dp, lanes = joined(up, dp, lanes)

    steps(*up)
    upstream = cotangent.astype(f32)
    flat_cotangent = cotangent.reshape(count * span, width)
    others = plain_columns(lay, flat_cotangent, du_sums, list(dp_sums.values()), unit, hd)
    dp_sums = sum(jnp.sum(v[:, 0], axis=0) for v in dp_sums.values())
    dp_sums = jnp.broadcast_to(dp_sums[None], (8, 3 * hd))
    (dqkv,) = folded_gradient(lay, x_flat, dp, dp_sums, w_qkvu, unit, 0, (lanes, others))
    dy_flat, upstream = joined(up + dqkv + [z_sum], dy_flat, upstream)

    z_sum.finish()
    more_rounds(up)
    steps(*dqkv)
    out_whole = dot(o, dy_flat, 0, 0)
    out_whole = out_whole.astype(bf16).reshape(groups, rows, width)
    out_whole = jnp.stack(
        [
            lax.dynamic_index_in_dim(
                out_whole, lay.g ^ lay.z ^ GroupScatter.member(lay, i, True), 0, keepdims=False
            )
            for i in range(groups)
        ]
    )
    wo = GroupScatter(lay, out_whole[: groups // 2], out_whole[groups // 2 :], True)
    up_blocks = final_blocks(up, nz)
    (up_blocks,) = joined([wo, z_sum, out_sum], up_blocks)

    mlp_state = (mlp_params, mlp_first, mlp_second)
    attn_state = (attn_params, attn_first, attn_second)
    up_blocks = to_owners(up_blocks)
    more_rounds(dqkv)
    steps(wo)
    dqkv_blocks = final_blocks(dqkv, nz)
    outputs = (inputs.astype(f32) + out_sum.result().reshape(inputs.shape) + out_bias).astype(bf16)
    up_blocks, dqkv_blocks, down_blocks, outputs = joined(
        [wo], up_blocks, dqkv_blocks, down_blocks, outputs
    )

    dqkv_blocks = to_owners(dqkv_blocks)
    more_rounds([wo])
    mlp_result = adam_columns(
        lay, rate_mlp, at_owner(down_blocks), 0, unit, mlp_state, ff, 1, ()
    )
    normed_grad = z_sum.result().reshape(inputs.shape)
    normed, scaling = normalize(inputs.astype(f32))
    grad_mean = jnp.mean(normed_grad, axis=-1, keepdims=True)
    grad_proj = jnp.mean(normed_grad * normed, axis=-1, keepdims=True)
    input_grad = upstream + scaling * (normed_grad - grad_mean - normed * grad_proj)
    up_parts = at_owner(up_blocks)
    mlp_result = adam_columns(lay, rate_mlp, up_parts, 0, unit, mlp_state, 0, 1, mlp_result)
    dqkv_blocks, mlp_result, input_grad = joined([wo], dqkv_blocks, mlp_result, input_grad)

    out_grad = wo.result().astype(bf16)
    out_grad = lax.ppermute(out_grad, AXES, [(b, a) for a, b in lay.head_owner_perm()])
    dqkv_parts = at_owner(dqkv_blocks)
    attn_result = adam_columns(lay, rate_attention, dqkv_parts, 0, hd, attn_state, 0, 3, ())
    at = 3 * hd
    small_grad = sum(
        jnp.sum(v[:, :, at : at + small.shape[1]].astype(f32), axis=0) for v in dqkv_parts
    )
    small_result = adamw(small, small_grad, small_first, small_second, rate_vector)
    out_grad = [out_grad[None]]
    attn_result = adam_columns(
        lay, rate_attention, out_grad, 0, width, attn_state, 3 * width, 1, attn_result
    )
    return (outputs, input_grad, *attn_result, *mlp_result, *small_result)


def solution(mesh):
    tokens, weights = P("dp", "seq", None), P(("dp", "seq"), None)
    return jax.shard_map(
        body,
        mesh=mesh,
        in_specs=(tokens,) * 2 + (weights,) * 9,
        out_specs=(tokens,) * 2 + (weights,) * 12,
        check_vma=False,
    )
```
